256 devices in a mesh: lon: 64 (over z, y, x_hi), lat: 4 (over x_lo, core).
Axes of the slice: x: 4 (x_hi: 2, x_lo: 2; x = x_hi * 2 + x_lo), y: 4, z: 8, core: 2. Of those that a mesh axis runs over, the one named last changes fastest.
Arguments:
- block_input: bfloat16 [4, 24, 2304, 192], P(None, 'lat', 'lon'), may hold values from -200 to 200
- grad_out: bfloat16 [4, 24, 2304, 192], P(None, 'lat', 'lon'), may hold values from -30 to 30
- ln_gain: float32 [192], replicated, may hold values from 0.1 to 1.9
- w_qkv: bfloat16 [192, 576], replicated, may hold values from -0.4375 to 0.4375
- w_proj: bfloat16 [192, 192], replicated, may hold values from -0.4375 to 0.4375
- bias_table: float32 [4, 2, 6, 3312], P('lat'), may hold values from -305 to 305
Outputs:
- grad_x: bfloat16 [4, 24, 2304, 192], P(None, 'lat', 'lon')
- grad_gain: float32 [192], replicated
- grad_wqkv: float32 [192, 576], replicated
- grad_wproj: float32 [192, 192], replicated
- grad_bias: float32 [4, 2, 6, 3312], P('lat')
The draws below stay inside these ranges and needn't reach their ends.
All inputs are finite; a program needn't handle non-finite values.
Results may differ from the reference program's by a relative error of at most 0.009.
Values may be sent and summed in bfloat16 or wider, within the bound.
No kernel may reach another device: no remote copies, remote signals or barrier semaphores. Data moves between devices by JAX's collectives and lax.ppermute only.
A program may use at most 64 MiB of HBM per device.

```python
import math
import jax
import jax.numpy as jnp
from jax import lax

C = 192
HEADS = 6
HEAD_DIM = 32
WZ = 2
WLAT = 6
WLON = 12
NZ = 4
NLON = 72
MEMBERS = 32
NLAT = 24
NZW = 2
NWLAT = 4
WIN = 144
TABLE = 3312


def draw_block_input(key, part):
    key = jax.random.fold_in(key, 11)
    keys = jax.random.split(key, 3)
    shape = (NZ, NLAT, MEMBERS * NLON, C)
    base = jax.random.normal(keys[0], shape, jnp.float32)
    token_scale = jnp.exp(jax.random.uniform(keys[1], (NZ, NLAT, MEMBERS * NLON, 1), jnp.float32, 0.0, math.log(10.0)))
    channel_scale = jnp.exp(jax.random.uniform(keys[2], (1, 1, 1, C), jnp.float32, -0.7, 0.7))
    return (base * token_scale * channel_scale).astype(jnp.bfloat16)


def draw_grad_out(key, part):
    key = jax.random.fold_in(key, 23)
    keys = jax.random.split(key, 1)
    shape = (NZ, NLAT, MEMBERS * NLON, C)
    band_ramp = 0.5 + jnp.arange(NLAT, dtype=jnp.float32) / NLAT
    lon_ramp = 0.5 + jnp.arange(MEMBERS * NLON, dtype=jnp.float32) / (MEMBERS * NLON)
    ramp = band_ramp[None, :, None, None] * lon_ramp[None, None, :, None]
    base = jax.random.normal(keys[0], shape, jnp.float32)
    return jnp.clip(base * ramp, -30.0, 30.0).astype(jnp.bfloat16)


def draw_bias_table(key, part):
    key = jax.random.fold_in(key, 37)
    keys = jax.random.split(key, 1)
    shape = (NWLAT, NZW, HEADS, TABLE)
    return jnp.clip(jax.random.normal(keys[0], shape, jnp.float32), -6.0, 6.0)


def gaussian(rng, dims, deviation, limit, kind=jnp.bfloat16):
    result = deviation * jax.random.normal(rng, dims, jnp.float32)
    return jnp.clip(result, min=-limit, max=limit).astype(kind)


def setup_inputs(seed: int = 0) -> dict:
    streams_of = jax.random.split(jax.random.key(seed), 7)
    block_input = draw_block_input(jax.random.fold_in(streams_of[6], 71), 0)
    grad_out = draw_grad_out(jax.random.fold_in(streams_of[6], 71), 0)
    ln_gain = jnp.clip(1.0 + 0.18 * jax.random.normal(streams_of[2], (C,), jnp.float32), 0.1, 1.9)
    w_qkv = gaussian(streams_of[3], (C, 3 * C), C ** -0.5, 0.4375)
    w_proj = gaussian(streams_of[4], (C, C), C ** -0.5, 0.4375)
    bias_table = draw_bias_table(jax.random.fold_in(streams_of[6], 71), 0)
    return dict(block_input=block_input, grad_out=grad_out, ln_gain=ln_gain, w_qkv=w_qkv, w_proj=w_proj, bias_table=bias_table)


def relation_table():
    positions = jnp.arange(WLON * WLON)
    first = positions // WLON
    second = positions % WLON
    offsets = second - first + WLON - 1
    return (offsets[:, None] == jnp.arange(2 * WLON - 1)[None, :]).astype(jnp.float32)

def expand_bias(table):
    leading = table.shape[:-1]
    count = len(leading)
    pairs = table.reshape(leading + (WZ * WZ * WLAT * WLAT, 2 * WLON - 1))
    dense = jnp.einsum('...pr,qr->...pq', pairs, relation_table(), precision=lax.Precision.HIGHEST)
    dense = dense.reshape(leading + (WZ, WZ, WLAT, WLAT, WLON, WLON))
    order = tuple(range(count)) + (count, count + 2, count + 4, count + 1, count + 3, count + 5)
    return dense.transpose(order).reshape(leading + (WIN, WIN))

def reduce_bias(dense):
    leading = dense.shape[:-2]
    count = len(leading)
    split = dense.reshape(leading + (WZ, WLAT, WLON, WZ, WLAT, WLON))
    order = tuple(range(count)) + (count, count + 3, count + 1, count + 4, count + 2, count + 5)
    grouped = split.transpose(order).reshape(leading + (WZ * WZ * WLAT * WLAT, WLON * WLON))
    summed = jnp.einsum('...pq,qr->...pr', grouped, relation_table(), precision=lax.Precision.HIGHEST)
    return summed.reshape(leading + (TABLE,))

def to_windows(grid):
    depth, height, breadth, features = grid.shape
    split = grid.reshape(depth // WZ, WZ, height // WLAT, WLAT, breadth // WLON, WLON, features)
    return split.transpose(0, 2, 4, 1, 3, 5, 6).reshape(depth // WZ, height // WLAT, breadth // WLON, WIN, features)

def from_windows(blocks):
    levels, bands, strips, window, features = blocks.shape
    split = blocks.reshape(levels, bands, strips, WZ, WLAT, WLON, features)
    return split.transpose(0, 3, 1, 4, 2, 5, 6).reshape(levels * WZ, bands * WLAT, strips * WLON, features)

def allowed_pairs(last_level, last_band):
    positions = jnp.arange(WIN)
    level = positions // (WLAT * WLON)
    band = positions // WLON % WLAT
    upper = (level >= WZ - WZ // 2).astype(jnp.int32)
    edge = (band >= WLAT - WLAT // 2).astype(jnp.int32)
    region = 2 * upper[None, :] * last_level[:, None] + edge[None, :] * last_band[:, None]
    return region[:, :, None] == region[:, None, :]

def window_grads(projected, grad_mixed, bias, allowed):
    bands, strips, window, triple = projected.shape
    width = triple // 3
    heads = bias.shape[1]
    size = width // heads
    scale = HEAD_DIM ** (-0.5)
    split = (bands, strips, window, heads, size)
    query = projected[..., :width].reshape(split).astype(jnp.float32)
    key_rows = projected[..., width:2 * width].reshape(split).astype(jnp.float32)
    value_rows = projected[..., 2 * width:].reshape(split).astype(jnp.float32)
    grad_heads = grad_mixed.reshape(split).astype(jnp.float32)
    scores = jnp.einsum('abihd,abjhd->abhij', query, key_rows) * scale + bias[:, None]
    scores = jnp.where(allowed[:, None, None], scores, -1e+30)
    top = lax.optimization_barrier(jnp.max(scores, axis=-1, keepdims=True))
    powers = jnp.exp(scores - top)
    attend = powers / lax.optimization_barrier(jnp.sum(powers, axis=-1, keepdims=True))
    attend_half = attend.astype(jnp.bfloat16).astype(jnp.float32)
    outputs = jnp.einsum('abhij,abjhd->abihd', attend_half, value_rows).astype(jnp.bfloat16)
    grad_value = jnp.einsum('abhij,abihd->abjhd', attend_half, grad_heads).astype(jnp.bfloat16)
    grad_attend = jnp.einsum('abihd,abjhd->abhij', grad_heads, value_rows)
    total = lax.optimization_barrier(jnp.sum(attend * grad_attend, axis=-1, keepdims=True))
    grad_scores = attend * (grad_attend - total)
    grad_half = grad_scores.astype(jnp.bfloat16).astype(jnp.float32)
    grad_query = (jnp.einsum('abhij,abjhd->abihd', grad_half, key_rows) * scale).astype(jnp.bfloat16)
    grad_key = (jnp.einsum('abhij,abihd->abjhd', grad_half, query) * scale).astype(jnp.bfloat16)
    shape = (bands, strips, window, width)
    grad_projected = jnp.concatenate([grad_query.reshape(shape), grad_key.reshape(shape), grad_value.reshape(shape)], axis=-1)
    return (outputs.reshape(shape), grad_projected, lax.optimization_barrier(jnp.sum(grad_scores, axis=1)))

def member_grads(block_input, grad_out, ln_gain, w_qkv, w_proj, bias_table):
    width = block_input.shape[-1]
    values = block_input.astype(jnp.float32)
    mean = lax.optimization_barrier(jnp.mean(values, axis=-1, keepdims=True))
    centred = values - mean
    inverse = lax.rsqrt(lax.optimization_barrier(jnp.mean(centred * centred, axis=-1, keepdims=True)) + 1e-05)
    standard = centred * inverse
    normed = (standard * ln_gain).astype(jnp.bfloat16)
    ahead = (-(WZ // 2), -(WLAT // 2), -(WLON // 2))
    behind = (WZ // 2, WLAT // 2, WLON // 2)
    shifted = jnp.roll(normed, ahead, (0, 1, 2))
    grad_shifted = jnp.roll(grad_out, ahead, (0, 1, 2))
    grid = shifted.shape[:3]
    token_rows = shifted.reshape(-1, width)
    grad_rows = grad_shifted.reshape(-1, width)
    projected = jnp.dot(token_rows, w_qkv, preferred_element_type=jnp.float32).astype(jnp.bfloat16)
    grad_mixed = jnp.dot(grad_rows, w_proj.T, preferred_element_type=jnp.float32).astype(jnp.bfloat16)
    proj_windows = to_windows(projected.reshape(grid + (3 * width,)))
    mixed_windows = to_windows(grad_mixed.reshape(grid + (width,)))
    levels, bands, strips = proj_windows.shape[:3]
    blocks = levels * bands
    tables = jnp.transpose(bias_table, (1, 0, 2, 3)).reshape((blocks,) + bias_table.shape[2:])
    index = jnp.arange(blocks)
    last_level = (index // bands == levels - 1).astype(jnp.int32)
    last_band = (index % bands == bands - 1).astype(jnp.int32)

    def one_block(items):
        proj_block, mixed_block, table, level_flag, band_flag = items
        allowed = allowed_pairs(level_flag[None], band_flag[None])
        outputs, grad_projected, grad_scores = window_grads(proj_block[None], mixed_block[None], expand_bias(table)[None], allowed)
        return (outputs[0], grad_projected[0], reduce_bias(grad_scores[0]))
    outputs, grad_projected, table_grads = lax.map(one_block, (proj_windows.reshape((blocks,) + proj_windows.shape[2:]), mixed_windows.reshape((blocks,) + mixed_windows.shape[2:]), tables, last_level, last_band))
    out_rows = from_windows(outputs.reshape((levels, bands) + outputs.shape[1:])).reshape(-1, width)
    grad_proj_rows = from_windows(grad_projected.reshape((levels, bands) + grad_projected.shape[1:])).reshape(-1, 3 * width)
    grad_wproj = jnp.dot(out_rows.T, grad_rows, preferred_element_type=jnp.float32)
    grad_wqkv = jnp.dot(token_rows.T, grad_proj_rows, preferred_element_type=jnp.float32)
    grad_shift_rows = jnp.dot(grad_proj_rows, w_qkv.T, preferred_element_type=jnp.float32).astype(jnp.bfloat16)
    grad_normed = jnp.roll(grad_shift_rows.reshape(grid + (width,)), behind, (0, 1, 2)).astype(jnp.float32)
    grad_gain = lax.optimization_barrier(jnp.sum(grad_normed * standard, axis=(0, 1, 2)))
    scaled = grad_normed * ln_gain
    grad_local = inverse * (scaled - lax.optimization_barrier(jnp.mean(scaled, axis=-1, keepdims=True)) - standard * lax.optimization_barrier(jnp.mean(scaled * standard, axis=-1, keepdims=True)))
    grad_x = (grad_out.astype(jnp.float32) + grad_local).astype(jnp.bfloat16)
    grad_bias = jnp.transpose(table_grads.reshape((levels, bands) + table_grads.shape[1:]), (1, 0, 2, 3))
    return (grad_x, grad_gain, grad_wqkv, grad_wproj, grad_bias)

def reference(block_input, grad_out, ln_gain, w_qkv, w_proj, bias_table):
    depth, height, breadth, width = block_input.shape

    def split_members(array):
        return array.reshape(depth, height, MEMBERS, NLON, width).transpose(2, 0, 1, 3, 4)

    def one_member(items):
        return member_grads(items[0], items[1], ln_gain, w_qkv, w_proj, bias_table)
    grad_x, grad_gain, grad_wqkv, grad_wproj, grad_bias = lax.map(one_member, (split_members(block_input), split_members(grad_out)))
    grad_x = grad_x.transpose(1, 2, 0, 3, 4).reshape(block_input.shape)
    return (grad_x, lax.optimization_barrier(jnp.sum(grad_gain, axis=0)), lax.optimization_barrier(jnp.sum(grad_wqkv, axis=0)), lax.optimization_barrier(jnp.sum(grad_wproj, axis=0)), lax.optimization_barrier(jnp.sum(grad_bias, axis=0)))
```

```python
import functools

import jax
import jax.numpy as jnp
from jax import lax
from jax.experimental import pallas as pl
from jax.experimental.pallas import tpu as pltpu
from jax.sharding import Mesh, PartitionSpec as P

C = 192
HEADS = 6
HEAD_DIM = 32
WLON = 12
WIN = 144
TABLE = 3312
PAIRS = 12
OFFSETS = 23
SCALE = HEAD_DIM**-0.5
STRIPS = 3
WINDOWS = 6
TYPES = 12
GROUP = ("y", "xl", "c")
REST = ("z", "xh")
PARTS = 16
PART_ROWS = C // PARTS
QKV_LANES = 640
PROJ_LANES = 256
W_LANES = QKV_LANES + PROJ_LANES
B_LANES = 256
B_PARTS = 13
SEND_LANES = W_LANES + B_LANES
LATS = 4
MIX_LANES = W_LANES + LATS * B_LANES
WIDE = 3584
f32 = jnp.float32
bf16 = jnp.bfloat16
VMEM_LIMIT = 56 * 1024 * 1024

NN = (((1,), (0,)), ((), ()))
NT = (((1,), (1,)), ((), ()))


def dot(a, b, dims=NN):
    return lax.dot_general(a, b, dims, preferred_element_type=f32)


def table_offset(zl_i, zl_j):
    zi, li = divmod(zl_i, 6)
    zj, lj = divmod(zl_j, 6)
    return (((zi * 2 + zj) * 6 + li) * 6 + lj) * OFFSETS


def offset_match(oj):
    row = lax.broadcasted_iota(jnp.int32, (PAIRS * 32, 256), 0)
    col = lax.broadcasted_iota(jnp.int32, (PAIRS * 32, 256), 1)
    zl = col // WLON
    target = zl * 32 + (oj + 11) - (col - zl * WLON)
    return jnp.where(row == target, 1.0, 0.0).astype(bf16)


def bias_kernel(table_ref, out_ref, wide, pairs):
    wide[...] = jnp.zeros_like(wide)
    for lz in range(2):
        wide[lz * HEADS : (lz + 1) * HEADS, :TABLE] = table_ref[0, lz]
    pairs[...] = jnp.zeros_like(pairs)
    lane = lax.broadcasted_iota(jnp.int32, (16, 128), 1)
    for zl_j in range(PAIRS):
        for v in range(3):
            total = jnp.zeros((16, 128), f32)
            for q in range(4):
                off = table_offset(4 * v + q, zl_j)
                base, rest = off // 128 * 128, off % 128
                width = 128 if rest + OFFSETS <= 128 else 256
                piece = wide[:, base : base + width]
                shift = (32 * q - rest) % width
                if shift:
                    piece = pltpu.roll(piece, shift, 1)
                inside = (lane >= 32 * q) & (lane < 32 * q + OFFSETS)
                total = jnp.where(inside, piece[:, :128], total)
            pairs[v, pl.ds(zl_j, TYPES, stride=16), :] = total[:TYPES]
    full = jnp.concatenate([pairs[v] for v in range(3)], axis=1)
    high = full.astype(bf16)
    left = full - high.astype(f32)
    middle = left.astype(bf16)
    low = (left - middle.astype(f32)).astype(bf16)
    for oj in range(WLON):
        match = offset_match(oj)
        dense = dot(high, match) + (dot(middle, match) + dot(low, match))
        for t in range(TYPES):
            block = dense[t * 16 : t * 16 + PAIRS]
            out_ref[t, 0, pl.ds(oj, PAIRS, stride=WLON), :] = block[:, :128]
            out_ref[t, 1, pl.ds(oj, PAIRS, stride=WLON), :] = block[:, 128:]
    lat = lax.axis_index("xl") * 2 + lax.axis_index("c")
    last_band = (lat == LATS - 1).astype(jnp.int32)
    j = lax.broadcasted_iota(jnp.int32, (WIN, 256), 0)
    i = lax.broadcasted_iota(jnp.int32, (WIN, 256), 1)

    def region(token, last_level):
        upper = jnp.where(token >= 72, 2 * last_level, 0)
        inner = jnp.where(token >= 72, token - 72, token)
        return upper + jnp.where(inner >= 36, last_band, 0)

    for lz in range(2):
        allowed = region(i, lz) == region(j, lz)
        for h in range(HEADS):
            t = lz * HEADS + h
            for n in range(2):
                kept = allowed[:, 128 * n : 128 * (n + 1)]
                out_ref[t, n] = jnp.where(kept, out_ref[t, n], -1e30)


def bias_dense(table):
    return pl.pallas_call(
        bias_kernel,
        out_shape=jax.ShapeDtypeStruct((TYPES, 2, WIN, 128), f32),
        in_specs=[pl.BlockSpec(memory_space=pltpu.VMEM)],
        out_specs=pl.BlockSpec(memory_space=pltpu.VMEM),
        scratch_shapes=[pltpu.VMEM((16, WIDE), f32), pltpu.VMEM((3, TYPES * 16, 128), f32)],
        compiler_params=pltpu.CompilerParams(vmem_limit_bytes=VMEM_LIMIT),
        cost_estimate=pl.CostEstimate(
            flops=20_000_000_000, bytes_accessed=1_200_000, transcendentals=0
        ),
        name="bias_dense",
    )(table)


def normalised(values):
    mean = jnp.mean(values, axis=-1, keepdims=True)
    centred = values - mean
    inverse = lax.rsqrt(jnp.mean(centred * centred, axis=-1, keepdims=True) + 1e-05)
    return centred * inverse, inverse


def main_kernel(
    x_ref, g_ref, lat_ref, lon_ref, corner_ref, gain_ref, w3_ref, w3t_ref, wqkv_ref, wproj_ref,
    bias_ref, own_out, lat_out, lon_out, corner_out, send_out,
    xw, gw, rows, dense, wsum, psum, gsum, spread, wide, grads,
):
    for level in range(4):
        source = (level + 1) % 4
        lz, zi = divmod(level, 2)
        for a in range(6):
            for k, (own, to) in enumerate(((x_ref, xw), (g_ref, gw))):
                if a < 3:
                    body = own[source, a + 3].astype(f32)[6:36]
                    tail = lon_ref[k, source, a].astype(f32)
                else:
                    body = lat_ref[k, source, a - 3].astype(f32)
                    tail = corner_ref[k, source, a - 3].astype(f32)
                line = jnp.concatenate([body, tail], axis=0)
                start = zi * 72 + a * WLON
                for s in range(STRIPS):
                    to[lz * STRIPS + s, start : start + WLON, :] = line[s * WLON : (s + 1) * WLON]
    dense[...] = jnp.zeros_like(dense)
    wsum[...] = jnp.zeros_like(wsum)
    psum[...] = jnp.zeros_like(psum)
    gsum[...] = jnp.zeros_like(gsum)
    gain = gain_ref[...]
    lane_head = lax.broadcasted_iota(jnp.int32, (WIN, C), 1) // HEAD_DIM

    def of_head(value, h):
        return jnp.where(lane_head == h, value, jnp.zeros_like(value))

    def window(w, carry):
        lz = w // STRIPS
        standard, _ = normalised(xw[w])
        tokens = (standard * gain).astype(bf16)
        cot = gw[w].astype(bf16)
        query = dot(tokens, w3_ref[0]).astype(bf16)
        key = dot(tokens, w3_ref[1]).astype(bf16)
        value = dot(tokens, w3_ref[2]).astype(bf16)
        key_t = dot(w3t_ref[1], tokens, NT).astype(bf16)
        value_t = dot(w3t_ref[2], tokens, NT).astype(bf16)
        mixed = dot(cot, wproj_ref[...], NT).astype(bf16)
        out_t = []
        grad_query_t = []
        grad_key = jnp.zeros((WIN, C), f32)
        grad_value = jnp.zeros((WIN, C), f32)
        for h in range(HEADS):
            part = slice(h * HEAD_DIM, (h + 1) * HEAD_DIM)
            bias = jnp.concatenate(
                [bias_ref[lz * HEADS + h, 0], bias_ref[lz * HEADS + h, 1][:, : WIN - 128]], axis=1
            )
            scores = dot(of_head(key, h), query, NT) * SCALE + bias
            top = jnp.max(scores, axis=0, keepdims=True)
            powers = jnp.exp(scores - top)
            attend = powers * (1.0 / jnp.sum(powers, axis=0, keepdims=True))
            half = attend.astype(bf16)
            grad_attend = dot(of_head(value, h), mixed, NT)
            total = jnp.sum(attend * grad_attend, axis=0, keepdims=True)
            grad_scores = attend * (grad_attend - total)
            grad_half = grad_scores.astype(bf16)
            dense[lz * HEADS + h, 0] += grad_scores[:, :128]
            dense[lz * HEADS + h, 1, :, : WIN - 128] += grad_scores[:, 128:]
            out_t.append(dot(value_t[part], half).astype(bf16))
            grad_query_t.append(dot(key_t[part], grad_half) * SCALE)
            grad_value += dot(half, of_head(mixed, h))
            grad_key += dot(grad_half, of_head(query, h))
        out_t = jnp.concatenate(out_t, axis=0)
        grad_query = jnp.concatenate(grad_query_t, axis=0).T
        psum[...] += dot(out_t, cot)
        spread[:, 0:C] = grad_query
        spread[:, C : 2 * C] = grad_key * SCALE
        spread[:, 2 * C : 3 * C] = grad_value
        grad_projected = spread[...].astype(bf16)
        tokens_t = (standard * gain).T.astype(bf16)
        wsum[...] += dot(tokens_t, grad_projected)
        back = dot(grad_projected, wqkv_ref[...], NT).astype(bf16).astype(f32)
        rows[w] = back
        gsum[0:1, :] += jnp.sum(back * standard, axis=0, keepdims=True)
        return carry

    lax.fori_loop(0, WINDOWS, window, 0)

    for level in range(4):
        source = (level + 1) % 4
        lz, zi = divmod(level, 2)
        for a in range(6):
            start = zi * 72 + a * WLON
            line = jnp.concatenate(
                [rows[lz * STRIPS + s, start : start + WLON, :] for s in range(STRIPS)], axis=0
            )
            body, tail = line[:30].astype(bf16), line[30:].astype(bf16)
            if a < 3:
                own_out[source, a] = body
                lon_out[source, a] = tail
            else:
                lat_out[source, a - 3] = body
                corner_out[source, a - 3] = tail

    grads[...] = jnp.zeros_like(grads)
    for oj in range(WLON):
        picked = jnp.concatenate(
            [
                jnp.concatenate(
                    [
                        jnp.concatenate(
                            [dense[t, n, pl.ds(oj, PAIRS, stride=WLON), :] for n in range(2)],
                            axis=1,
                        ),
                        jnp.zeros((4, 256), f32),
                    ],
                    axis=0,
                )
                for t in range(TYPES)
            ],
            axis=0,
        )
        high = picked.astype(bf16)
        low = (picked - high.astype(f32)).astype(bf16)
        match = offset_match(oj)
        added = dot(high, match, NT) + dot(low, match, NT)
        for v in range(3):
            grads[v] += added[:, 128 * v : 128 * (v + 1)]
    wide[...] = jnp.zeros_like(wide)
    lane = lax.broadcasted_iota(jnp.int32, (TYPES, 256), 1)
    for zl_j in range(PAIRS):
        for v in range(3):
            four = grads[v, pl.ds(zl_j, TYPES, stride=16), :]
            for q in range(4):
                off = table_offset(4 * v + q, zl_j)
                base, rest = off // 128 * 128, off % 128
                width = 128 if rest + OFFSETS <= 128 else 256
                piece = four
                if width == 256:
                    piece = jnp.concatenate([four, jnp.zeros_like(four)], axis=1)
                shift = (rest - 32 * q) % width
                if shift:
                    piece = pltpu.roll(piece, shift, 1)
                position = lane[:, :width]
                inside = (position >= rest) & (position < rest + OFFSETS)
                target = (slice(0, TYPES), slice(base, base + width))
                wide[target] = jnp.where(inside, piece, wide[target])

    tail = jnp.concatenate(
        [gsum[0:1, :], jnp.zeros((16 - PART_ROWS - 1, C), f32)], axis=0
    )
    for p in range(PARTS):
        lines = slice(p * PART_ROWS, (p + 1) * PART_ROWS)
        first = jnp.concatenate([wsum[lines, :], jnp.zeros((4, 3 * C), f32)], axis=0)
        send_out[p, :, 0 : 3 * C] = first.astype(bf16)
        send_out[p, :, 3 * C : QKV_LANES] = jnp.zeros((16, QKV_LANES - 3 * C), bf16)
        second = jnp.concatenate([psum[lines, :], tail], axis=0)
        send_out[p, :, QKV_LANES : QKV_LANES + C] = second.astype(bf16)
        send_out[p, :, QKV_LANES + C : W_LANES] = jnp.zeros((16, PROJ_LANES - C), bf16)
        if p < B_PARTS:
            third = wide[:, p * B_LANES : (p + 1) * B_LANES].astype(bf16)
        else:
            third = jnp.zeros((16, B_LANES), bf16)
        send_out[p, :, W_LANES:] = third


def main(x, g, lat_in, lon_in, corner_in, gain, w3, w3t, wqkv, wproj, bias):
    vmem = pl.BlockSpec(memory_space=pltpu.VMEM)
    return pl.pallas_call(
        main_kernel,
        out_shape=(
            jax.ShapeDtypeStruct((4, 3, 30, C), bf16),
            jax.ShapeDtypeStruct((4, 3, 30, C), bf16),
            jax.ShapeDtypeStruct((4, 3, 6, C), bf16),
            jax.ShapeDtypeStruct((4, 3, 6, C), bf16),
            jax.ShapeDtypeStruct((PARTS, 16, SEND_LANES), bf16),
        ),
        in_specs=[vmem] * 11,
        out_specs=(vmem,) * 5,
        scratch_shapes=[
            pltpu.VMEM((WINDOWS, WIN, C), f32),
            pltpu.VMEM((WINDOWS, WIN, C), f32),
            pltpu.VMEM((WINDOWS, WIN, C), f32),
            pltpu.VMEM((TYPES, 2, WIN, 128), f32),
            pltpu.VMEM((C, 3 * C), f32),
            pltpu.VMEM((C, C), f32),
            pltpu.VMEM((8, C), f32),
            pltpu.VMEM((WIN, 3 * C), f32),
            pltpu.VMEM((16, WIDE), f32),
            pltpu.VMEM((3, TYPES * 16, 128), f32),
        ],
        compiler_params=pltpu.CompilerParams(vmem_limit_bytes=VMEM_LIMIT),
        cost_estimate=pl.CostEstimate(
            flops=20_000_000_000, bytes_accessed=4_000_000, transcendentals=750_000
        ),
        name="window_grads",
    )(x, g, lat_in, lon_in, corner_in, gain, w3, w3t, wqkv, wproj, bias)


def norm_kernel(x_ref, g_ref, gain_ref, own_ref, lat_ref, lon_ref, corner_ref, out_ref):
    gain = gain_ref[...]
    for level in range(4):
        for a in range(6):
            if a < 3:
                head, body = corner_ref[level, a], lat_ref[level, a]
            else:
                head, body = lon_ref[level, a - 3], own_ref[level, a - 3]
            grad = jnp.concatenate([head.astype(f32), body.astype(f32)], axis=0)
            standard, inverse = normalised(x_ref[level, a].astype(f32))
            scaled = grad * gain
            local = inverse * (
                scaled
                - jnp.mean(scaled, axis=-1, keepdims=True)
                - standard * jnp.mean(scaled * standard, axis=-1, keepdims=True)
            )
            out_ref[level, a] = (g_ref[level, a].astype(f32) + local).astype(bf16)


def norm_grads(x, g, gain, own, lat_in, lon_in, corner_in):
    vmem = pl.BlockSpec(memory_space=pltpu.VMEM)
    return pl.pallas_call(
        norm_kernel,
        out_shape=jax.ShapeDtypeStruct(x.shape, bf16),
        in_specs=[vmem] * 7,
        out_specs=vmem,
        compiler_params=pltpu.CompilerParams(vmem_limit_bytes=VMEM_LIMIT),
        cost_estimate=pl.CostEstimate(
            flops=10_000_000, bytes_accessed=1_500_000, transcendentals=1000
        ),
        name="norm_grads",
    )(x, g, gain, own, lat_in, lon_in, corner_in)


def unpack_kernel(parts_ref, gain_out, wqkv_out, wproj_out, bias_out):
    gain_out[...] = parts_ref[0, :, QKV_LANES : QKV_LANES + C].astype(f32)[12:13]
    for p in range(PARTS):
        lines = slice(p * PART_ROWS, (p + 1) * PART_ROWS)
        wqkv_out[lines, :] = parts_ref[p, :, 0 : 3 * C].astype(f32)[:PART_ROWS]
        wproj_out[lines, :] = parts_ref[p, :, QKV_LANES : QKV_LANES + C].astype(f32)[:PART_ROWS]
        if p < B_PARTS:
            width = min(B_LANES, TABLE - p * B_LANES)
            block = parts_ref[p, :, W_LANES:].astype(f32)[:, :width]
            for lz in range(2):
                bias_out[0, lz, :, p * B_LANES : p * B_LANES + width] = block[
                    lz * HEADS : (lz + 1) * HEADS
                ]


def unpack(parts):
    vmem = pl.BlockSpec(memory_space=pltpu.VMEM)
    return pl.pallas_call(
        unpack_kernel,
        out_shape=(
            jax.ShapeDtypeStruct((1, C), f32),
            jax.ShapeDtypeStruct((C, 3 * C), f32),
            jax.ShapeDtypeStruct((C, C), f32),
            jax.ShapeDtypeStruct((1, 2, HEADS, TABLE), f32),
        ),
        in_specs=[vmem],
        out_specs=(vmem,) * 4,
        compiler_params=pltpu.CompilerParams(vmem_limit_bytes=VMEM_LIMIT),
        name="unpack",
    )(parts)


def summed(send):
    lats = LATS
    got = lax.all_to_all(send, GROUP, 0, 0, tiled=True)
    got = got.reshape((PARTS // lats, lats, 16, SEND_LANES)).astype(f32)
    weights = jnp.sum(got[..., :W_LANES], axis=(0, 1))
    bias = jnp.sum(got[..., W_LANES:], axis=0).transpose(1, 0, 2).reshape(16, lats * B_LANES)
    mixed = jnp.concatenate([weights, bias], axis=1).astype(bf16)
    count = lax.axis_size(REST)
    got = lax.all_to_all(
        jnp.broadcast_to(mixed[None], (count,) + mixed.shape), REST, 0, 0, tiled=True
    )
    total = jnp.sum(got.astype(f32), axis=0).astype(bf16)
    weights = jnp.broadcast_to(total[None, None, :, :W_LANES], (PARTS // lats, lats, 16, W_LANES))
    bias = total[:, W_LANES:].reshape(16, lats, B_LANES).transpose(1, 0, 2)
    bias = jnp.broadcast_to(bias[None], (PARTS // lats, lats, 16, B_LANES))
    spread = jnp.concatenate([weights, bias], axis=-1).reshape(send.shape)
    return lax.all_to_all(spread, GROUP, 0, 0, tiled=True)


def on_device(x, g, ln_gain, w_qkv, w_proj, bias_table):
    lon_axes, lat_axes = ("z", "y", "xh"), ("xl", "c")
    both = lon_axes + lat_axes
    lons, lats = lax.axis_size(lon_axes), lax.axis_size(lat_axes)
    lon_swap = [(i, i ^ 1) for i in range(lons)]
    lat_down = [(i, (i - 1) % lats) for i in range(lats)]
    lat_up = [(i, (i + 1) % lats) for i in range(lats)]
    corner_down = [(i * lats + a, (i ^ 1) * lats + b) for i in range(lons) for a, b in lat_down]
    corner_up = [(i * lats + a, (i ^ 1) * lats + b) for i in range(lons) for a, b in lat_up]

    corner_in = lax.ppermute(jnp.stack([x[:, :3, :6], g[:, :3, :6]]), both, corner_down)
    lon_in = lax.ppermute(jnp.stack([x[:, 3:, :6], g[:, 3:, :6]]), lon_axes, lon_swap)
    lat_in = lax.ppermute(jnp.stack([x[:, :3, 6:], g[:, :3, 6:]]), lat_axes, lat_down)
    bias = bias_dense(bias_table)
    w3 = w_qkv.reshape(C, 3, C).transpose(1, 0, 2)
    w3t = w_qkv.T.reshape(3, C, C)
    gain = ln_gain.reshape(1, C)
    own, to_lat, to_lon, to_corner, send = main(
        x, g, lat_in, lon_in, corner_in, gain, w3, w3t, w_qkv, w_proj, bias
    )
    back_corner = lax.ppermute(to_corner, both, corner_up)
    back_lon = lax.ppermute(to_lon, lon_axes, lon_swap)
    back_lat = lax.ppermute(to_lat, lat_axes, lat_up)
    grad_gain, grad_wqkv, grad_wproj, grad_bias = unpack(summed(send))
    grad_x = norm_grads(x, g, gain, own, back_lat, back_lon, back_corner)
    return grad_x, grad_gain.reshape(C), grad_wqkv, grad_wproj, grad_bias


def solution(mesh):
    shape = (mesh.shape["lon"] // 8, 4, 2, 2, 2)
    split = Mesh(mesh.devices.reshape(shape), ("z", "y", "xh", "xl", "c"))
    tokens = P(None, ("xl", "c"), ("z", "y", "xh"), None)
    table = P(("xl", "c"), None, None, None)
    return jax.shard_map(
        on_device,
        mesh=split,
        in_specs=(tokens, tokens, P(), P(), P(), table),
        out_specs=(tokens, P(), P(), P(), table),
        check_vma=False,
    )
```

```python
import functools

import jax
import jax.numpy as jnp
from jax import lax
from jax.experimental import pallas as pl
from jax.experimental.pallas import tpu as pltpu
from jax.sharding import Mesh, PartitionSpec as P

C = 192
HEADS = 6
HEAD_DIM = 32
WLON = 12
WIN = 144
TABLE = 3312
PAIRS = 12
OFFSETS = 23
SCALE = HEAD_DIM**-0.5
STRIPS = 3
WINDOWS = 6
TYPES = 12
GROUP = ("y", "xh", "xl", "c")
REST = "z"
PARTS = 32
W_PARTS = 24
W_LANES = 384
B_PARTS = 26
B_LANES = 128
GAIN_PART = 24
SEND_LANES = W_LANES + B_LANES
LATS = 4
WIDE = 3584
f32 = jnp.float32
bf16 = jnp.bfloat16
VMEM_LIMIT = 24 * 1024 * 1024

NN = (((1,), (0,)), ((), ()))
NT = (((1,), (1,)), ((), ()))


def dot(a, b, dims=NN):
    return lax.dot_general(a, b, dims, preferred_element_type=f32)


def table_offset(zl_i, zl_j):
    zi, li = divmod(zl_i, 6)
    zj, lj = divmod(zl_j, 6)
    return (((zi * 2 + zj) * 6 + li) * 6 + lj) * OFFSETS


def offset_match(oj):
    row = lax.broadcasted_iota(jnp.int32, (PAIRS * 32, 256), 0)
    col = lax.broadcasted_iota(jnp.int32, (PAIRS * 32, 256), 1)
    zl = col // WLON
    target = zl * 32 + (oj + 11) - (col - zl * WLON)
    return jnp.where(row == target, 1.0, 0.0).astype(bf16)


def prepare_kernel(table_ref, wqkv_ref, out_ref, w3_ref, w3t_ref, wide, pairs):
    for k in range(3):
        part = wqkv_ref[:, k * C : (k + 1) * C]
        w3_ref[k] = part
        if k:
            w3t_ref[k - 1] = part.T
    wide[...] = jnp.zeros_like(wide)
    for h in range(HEADS):
        for lz in range(2):
            wide[lz * HEADS + h : lz * HEADS + h + 1, :TABLE] = table_ref[h, lz : lz + 1]
    pairs[...] = jnp.zeros_like(pairs)
    lane = lax.broadcasted_iota(jnp.int32, (16, 128), 1)
    for zl_j in range(PAIRS):
        for v in range(3):
            total = jnp.zeros((16, 128), f32)
            for q in range(4):
                off = table_offset(4 * v + q, zl_j)
                base, rest = off // 128 * 128, off % 128
                width = 128 if rest + OFFSETS <= 128 else 256
                piece = wide[:, base : base + width]
                shift = (32 * q - rest) % width
                if shift:
                    piece = pltpu.roll(piece, shift, 1)
                inside = (lane >= 32 * q) & (lane < 32 * q + OFFSETS)
                total = jnp.where(inside, piece[:, :128], total)
            pairs[v, pl.ds(zl_j, TYPES, stride=16), :] = total[:TYPES]
    full = jnp.concatenate([pairs[v] for v in range(3)], axis=1)
    high = full.astype(bf16)
    left = full - high.astype(f32)
    middle = left.astype(bf16)
    low = (left - middle.astype(f32)).astype(bf16)
    for oj in range(WLON):
        match = offset_match(oj)
        dense = dot(high, match) + (dot(middle, match) + dot(low, match))
        for t in range(TYPES):
            block = dense[t * 16 : t * 16 + PAIRS]
            out_ref[t, 0, pl.ds(oj, PAIRS, stride=WLON), :] = block[:, :128]
            out_ref[t, 1, pl.ds(oj, PAIRS, stride=WLON), :] = block[:, 128:]
    lat = lax.axis_index("xl") * 2 + lax.axis_index("c")
    last_band = (lat == LATS - 1).astype(jnp.int32)
    j = lax.broadcasted_iota(jnp.int32, (WIN, 256), 0)
    i = lax.broadcasted_iota(jnp.int32, (WIN, 256), 1)

    def region(token, last_level):
        upper = jnp.where(token >= 72, 2 * last_level, 0)
        inner = jnp.where(token >= 72, token - 72, token)
        return upper + jnp.where(inner >= 36, last_band, 0)

    for lz in range(2):
        allowed = region(i, lz) == region(j, lz)
        for h in range(HEADS):
            t = lz * HEADS + h
            for n in range(2):
                kept = allowed[:, 128 * n : 128 * (n + 1)]
                out_ref[t, n] = jnp.where(kept, out_ref[t, n], -1e30)


def prepare(table, wqkv):
    vmem = pl.BlockSpec(memory_space=pltpu.VMEM)
    return pl.pallas_call(
        prepare_kernel,
        out_shape=(
            jax.ShapeDtypeStruct((TYPES, 2, WIN, 128), f32),
            jax.ShapeDtypeStruct((3, C, C), bf16),
            jax.ShapeDtypeStruct((2, C, C), bf16),
        ),
        in_specs=[vmem] * 2,
        out_specs=(vmem,) * 3,
        scratch_shapes=[pltpu.VMEM((16, WIDE), f32), pltpu.VMEM((3, TYPES * 16, 128), f32)],
        compiler_params=pltpu.CompilerParams(vmem_limit_bytes=VMEM_LIMIT),
        cost_estimate=pl.CostEstimate(
            flops=4_000_000_000, bytes_accessed=4_000_000, transcendentals=0
        ),
        name="prepare",
    )(table, wqkv)


def normalised(values):
    mean = jnp.mean(values, axis=-1, keepdims=True)
    centred = values - mean
    inverse = lax.rsqrt(jnp.mean(centred * centred, axis=-1, keepdims=True) + 1e-05)
    return centred * inverse, inverse


def main_kernel(
    x_ref, g_ref, lat_ref, lon_ref, corner_ref, gain_ref, w3_ref, w3t_ref, wqkv_ref, wproj_ref,
    bias_ref, own_out, lat_out, lon_out, corner_out, send_out,
    xw, gw, rows, dense, wsum, psum, gsum, spread, wide, grads,
):
    for level in range(4):
        source = (level + 1) % 4
        lz, zi = divmod(level, 2)
        for a in range(6):
            for k, (own, to) in enumerate(((x_ref, xw), (g_ref, gw))):
                if a < 3:
                    body = own[source, a + 3].astype(f32)[6:36]
                    tail = lon_ref[k, source, a].astype(f32)
                else:
                    body = lat_ref[k, source, a - 3].astype(f32)
                    tail = corner_ref[k, source, a - 3].astype(f32)
                line = jnp.concatenate([body, tail], axis=0)
                start = zi * 72 + a * WLON
                for s in range(STRIPS):
                    to[lz * STRIPS + s, start : start + WLON, :] = line[s * WLON : (s + 1) * WLON]
    dense[...] = jnp.zeros_like(dense)
    wsum[...] = jnp.zeros_like(wsum)
    psum[...] = jnp.zeros_like(psum)
    gsum[...] = jnp.zeros_like(gsum)
    gain = gain_ref[...]
    lane_head = lax.broadcasted_iota(jnp.int32, (WIN, C), 1) // HEAD_DIM

    def of_head(value, h):
        return jnp.where(lane_head == h, value, jnp.zeros_like(value))

    def window(w, carry):
        lz = w // STRIPS
        standard, _ = normalised(xw[w])
        tokens = (standard * gain).astype(bf16)
        cot = gw[w].astype(bf16)
        query = dot(tokens, w3_ref[0]).astype(bf16)
        key = dot(tokens, w3_ref[1]).astype(bf16)
        value = dot(tokens, w3_ref[2]).astype(bf16)
        key_t = dot(w3t_ref[0], tokens, NT).astype(bf16)
        value_t = dot(w3t_ref[1], tokens, NT).astype(bf16)
        mixed = dot(cot, wproj_ref[...], NT).astype(bf16)
        out_t = []
        grad_query_t = []
        grad_key = jnp.zeros((WIN, C), f32)
        grad_value = jnp.zeros((WIN, C), f32)
        for h in range(HEADS):
            part = slice(h * HEAD_DIM, (h + 1) * HEAD_DIM)
            bias = jnp.concatenate(
                [bias_ref[lz * HEADS + h, 0], bias_ref[lz * HEADS + h, 1][:, : WIN - 128]], axis=1
            )
            scores = dot(of_head(key, h), query, NT) * SCALE + bias
            top = jnp.max(scores, axis=0, keepdims=True)
            powers = jnp.exp(scores - top)
            attend = powers * (1.0 / jnp.sum(powers, axis=0, keepdims=True))
            half = attend.astype(bf16)
            grad_attend = dot(of_head(value, h), mixed, NT)
            total = jnp.sum(attend * grad_attend, axis=0, keepdims=True)
            grad_scores = attend * (grad_attend - total)
            grad_half = grad_scores.astype(bf16)
            dense[lz * HEADS + h, 0] += grad_scores[:, :128]
            dense[lz * HEADS + h, 1, :, : WIN - 128] += grad_scores[:, 128:]
            out_t.append(dot(value_t[part], half).astype(bf16))
            grad_query_t.append(dot(key_t[part], grad_half) * SCALE)
            grad_value += dot(half, of_head(mixed, h))
            grad_key += dot(grad_half, of_head(query, h))
        out_t = jnp.concatenate(out_t, axis=0)
        grad_query = jnp.concatenate(grad_query_t, axis=0).T
        psum[...] += dot(out_t, cot)
        spread[:, 0:C] = grad_query
        spread[:, C : 2 * C] = grad_key * SCALE
        spread[:, 2 * C : 3 * C] = grad_value
        grad_projected = spread[...].astype(bf16)
        tokens_t = (standard * gain).T.astype(bf16)
        wsum[...] += dot(tokens_t, grad_projected)
        back = dot(grad_projected, wqkv_ref[...], NT).astype(bf16).astype(f32)
        rows[w] = back
        gsum[0:1, :] += jnp.sum(back * standard, axis=0, keepdims=True)
        return carry

    lax.fori_loop(0, WINDOWS, window, 0)

    for level in range(4):
        source = (level + 1) % 4
        lz, zi = divmod(level, 2)
        for a in range(6):
            start = zi * 72 + a * WLON
            line = jnp.concatenate(
                [rows[lz * STRIPS + s, start : start + WLON, :] for s in range(STRIPS)], axis=0
            )
            body, tail = line[:30].astype(bf16), line[30:].astype(bf16)
            if a < 3:
                own_out[source, a] = body
                lon_out[source, a] = tail
            else:
                lat_out[source, a - 3] = body
                corner_out[source, a - 3] = tail

    grads[...] = jnp.zeros_like(grads)
    for oj in range(WLON):
        picked = jnp.concatenate(
            [
                jnp.concatenate(
                    [
                        jnp.concatenate(
                            [dense[t, n, pl.ds(oj, PAIRS, stride=WLON), :] for n in range(2)],
                            axis=1,
                        ),
                        jnp.zeros((4, 256), f32),
                    ],
                    axis=0,
                )
                for t in range(TYPES)
            ],
            axis=0,
        )
        high = picked.astype(bf16)
        low = (picked - high.astype(f32)).astype(bf16)
        match = offset_match(oj)
        added = dot(high, match, NT) + dot(low, match, NT)
        for v in range(3):
            grads[v] += added[:, 128 * v : 128 * (v + 1)]
    wide[...] = jnp.zeros_like(wide)
    lane = lax.broadcasted_iota(jnp.int32, (TYPES, 256), 1)
    for zl_j in range(PAIRS):
        for v in range(3):
            four = grads[v, pl.ds(zl_j, TYPES, stride=16), :]
            for q in range(4):
                off = table_offset(4 * v + q, zl_j)
                base, rest = off // 128 * 128, off % 128
                width = 128 if rest + OFFSETS <= 128 else 256
                piece = four
                if width == 256:
                    piece = jnp.concatenate([four, jnp.zeros_like(four)], axis=1)
                shift = (rest - 32 * q) % width
                if shift:
                    piece = pltpu.roll(piece, shift, 1)
                position = lane[:, :width]
                inside = (position >= rest) & (position < rest + OFFSETS)
                target = (slice(0, TYPES), slice(base, base + width))
                wide[target] = jnp.where(inside, piece, wide[target])

    halves = []
    for n in range(2):
        if n == 0:
            halves.append(wsum[:, :W_LANES])
        else:
            halves.append(jnp.concatenate([wsum[:, W_LANES:], psum[...]], axis=1))
    for p in range(PARTS):
        if p < W_PARTS:
            lines = slice(p // 2 * 16, p // 2 * 16 + 16)
            send_out[p, :, :W_LANES] = halves[p % 2][lines].astype(bf16)
        elif p == GAIN_PART:
            gains = jnp.concatenate([gsum[...], jnp.zeros((8, C), f32)], axis=0)
            gains = jnp.concatenate([gains, jnp.zeros((16, W_LANES - C), f32)], axis=1)
            send_out[p, :, :W_LANES] = gains.astype(bf16)
        else:
            send_out[p, :, :W_LANES] = jnp.zeros((16, W_LANES), bf16)
        if p < B_PARTS:
            send_out[p, :, W_LANES:] = wide[:, p * B_LANES : (p + 1) * B_LANES].astype(bf16)
        else:
            send_out[p, :, W_LANES:] = jnp.zeros((16, B_LANES), bf16)


def main(x, g, lat_in, lon_in, corner_in, gain, w3, w3t, wqkv, wproj, bias):
    vmem = pl.BlockSpec(memory_space=pltpu.VMEM)
    return pl.pallas_call(
        main_kernel,
        out_shape=(
            jax.ShapeDtypeStruct((4, 3, 30, C), bf16),
            jax.ShapeDtypeStruct((4, 3, 30, C), bf16),
            jax.ShapeDtypeStruct((4, 3, 6, C), bf16),
            jax.ShapeDtypeStruct((4, 3, 6, C), bf16),
            jax.ShapeDtypeStruct((PARTS, 16, SEND_LANES), bf16),
        ),
        in_specs=[vmem] * 11,
        out_specs=(vmem,) * 5,
        scratch_shapes=[
            pltpu.VMEM((WINDOWS, WIN, C), f32),
            pltpu.VMEM((WINDOWS, WIN, C), f32),
            pltpu.VMEM((WINDOWS, WIN, C), f32),
            pltpu.VMEM((TYPES, 2, WIN, 128), f32),
            pltpu.VMEM((C, 3 * C), f32),
            pltpu.VMEM((C, C), f32),
            pltpu.VMEM((8, C), f32),
            pltpu.VMEM((WIN, 3 * C), f32),
            pltpu.VMEM((16, WIDE), f32),
            pltpu.VMEM((3, TYPES * 16, 128), f32),
        ],
        compiler_params=pltpu.CompilerParams(vmem_limit_bytes=VMEM_LIMIT),
        cost_estimate=pl.CostEstimate(
            flops=20_000_000_000, bytes_accessed=4_000_000, transcendentals=750_000
        ),
        name="window_grads",
    )(x, g, lat_in, lon_in, corner_in, gain, w3, w3t, wqkv, wproj, bias)


def norm_kernel(x_ref, g_ref, gain_ref, own_ref, lat_ref, lon_ref, corner_ref, out_ref):
    gain = gain_ref[...]
    for level in range(4):
        for a in range(6):
            if a < 3:
                head, body = corner_ref[level, a], lat_ref[level, a]
            else:
                head, body = lon_ref[level, a - 3], own_ref[level, a - 3]
            grad = jnp.concatenate([head.astype(f32), body.astype(f32)], axis=0)
            standard, inverse = normalised(x_ref[level, a].astype(f32))
            scaled = grad * gain
            local = inverse * (
                scaled
                - jnp.mean(scaled, axis=-1, keepdims=True)
                - standard * jnp.mean(scaled * standard, axis=-1, keepdims=True)
            )
            out_ref[level, a] = (g_ref[level, a].astype(f32) + local).astype(bf16)


def norm_grads(x, g, gain, own, lat_in, lon_in, corner_in):
    vmem = pl.BlockSpec(memory_space=pltpu.VMEM)
    return pl.pallas_call(
        norm_kernel,
        out_shape=jax.ShapeDtypeStruct(x.shape, bf16),
        in_specs=[vmem] * 7,
        out_specs=vmem,
        compiler_params=pltpu.CompilerParams(vmem_limit_bytes=VMEM_LIMIT),
        cost_estimate=pl.CostEstimate(
            flops=10_000_000, bytes_accessed=1_500_000, transcendentals=1000
        ),
        name="norm_grads",
    )(x, g, gain, own, lat_in, lon_in, corner_in)


def unpack_kernel(parts_ref, gain_out, wqkv_out, wproj_out, bias_out):
    gain_out[...] = parts_ref[GAIN_PART, :, :C].astype(f32)[:1]
    for p in range(W_PARTS):
        lines = slice(p // 2 * 16, p // 2 * 16 + 16)
        block = parts_ref[p, :, :W_LANES].astype(f32)
        if p % 2 == 0:
            wqkv_out[lines, :W_LANES] = block
        else:
            wqkv_out[lines, W_LANES:] = block[:, :C]
            wproj_out[lines, :] = block[:, C:]
    for p in range(B_PARTS):
        width = min(B_LANES, TABLE - p * B_LANES)
        block = parts_ref[p, :, W_LANES:].astype(f32)[:, :width]
        for h in range(HEADS):
            for lz in range(2):
                t = lz * HEADS + h
                bias_out[h, lz : lz + 1, p * B_LANES : p * B_LANES + width] = block[t : t + 1]


def unpack(parts):
    vmem = pl.BlockSpec(memory_space=pltpu.VMEM)
    return pl.pallas_call(
        unpack_kernel,
        out_shape=(
            jax.ShapeDtypeStruct((1, C), f32),
            jax.ShapeDtypeStruct((C, 3 * C), f32),
            jax.ShapeDtypeStruct((C, C), f32),
            jax.ShapeDtypeStruct((HEADS, 2, TABLE), f32),
        ),
        in_specs=[vmem],
        out_specs=(vmem,) * 4,
        compiler_params=pltpu.CompilerParams(vmem_limit_bytes=VMEM_LIMIT),
        name="unpack",
    )(parts)


def summed(send, ready):
    others = PARTS // LATS
    got = lax.all_to_all(send, GROUP, 0, 0, tiled=True)
    got = got.reshape((others, LATS, 16, SEND_LANES)).astype(f32)
    weights = jnp.sum(got[..., :W_LANES], axis=(0, 1))
    bias = jnp.sum(got[..., W_LANES:], axis=0)
    mixed = jnp.concatenate([weights] + [bias[n] for n in range(LATS)], axis=1).astype(bf16)
    mixed, ready = lax.optimization_barrier((mixed, ready))
    count = lax.axis_size(REST)
    got = lax.all_to_all(
        jnp.broadcast_to(mixed[None], (count,) + mixed.shape), REST, 0, 0, tiled=True
    )
    total = jnp.sum(got.astype(f32), axis=0).astype(bf16)
    weights = total[:, :W_LANES]
    rows = [
        jnp.concatenate([weights, total[:, W_LANES + n * B_LANES : W_LANES + (n + 1) * B_LANES]], 1)
        for n in range(LATS)
    ]
    spread = jnp.broadcast_to(jnp.stack(rows)[None], (others, LATS, 16, SEND_LANES))
    return lax.all_to_all(spread.reshape(send.shape), GROUP, 0, 0, tiled=True), ready


def on_device(x, g, ln_gain, w_qkv, w_proj, bias_table):
    lon_axes, lat_axes = ("z", "y", "xh"), ("xl", "c")
    both = lon_axes + lat_axes
    lons, lats = lax.axis_size(lon_axes), lax.axis_size(lat_axes)
    lon_swap = [(i, i ^ 1) for i in range(lons)]
    lat_down = [(i, (i - 1) % lats) for i in range(lats)]
    lat_up = [(i, (i + 1) % lats) for i in range(lats)]
    corner_down = [(i * lats + a, (i ^ 1) * lats + b) for i in range(lons) for a, b in lat_down]
    corner_up = [(i * lats + a, (i ^ 1) * lats + b) for i in range(lons) for a, b in lat_up]

    corner_in = lax.ppermute(jnp.stack([x[:, :3, :6], g[:, :3, :6]]), both, corner_down)
    lon_in = lax.ppermute(jnp.stack([x[:, 3:, :6], g[:, 3:, :6]]), lon_axes, lon_swap)
    lat_in = lax.ppermute(jnp.stack([x[:, :3, 6:], g[:, :3, 6:]]), lat_axes, lat_down)
    bias, w3, w3t = prepare(bias_table[0].transpose(1, 0, 2), w_qkv)
    gain = ln_gain.reshape(1, C)
    own, to_lat, to_lon, to_corner, send = main(
        x, g, lat_in, lon_in, corner_in, gain, w3, w3t, w_qkv, w_proj, bias
    )
    back_corner = lax.ppermute(to_corner, both, corner_up)
    back_lon = lax.ppermute(to_lon, lon_axes, lon_swap)
    back_lat = lax.ppermute(to_lat, lat_axes, lat_up)
    parts, (back_lat, back_lon, back_corner) = summed(send, (back_lat, back_lon, back_corner))
    grad_gain, grad_wqkv, grad_wproj, grad_bias = unpack(parts)
    grad_x = norm_grads(x, g, gain, own, back_lat, back_lon, back_corner)
    grad_bias = grad_bias.transpose(1, 0, 2)[None]
    return grad_x, grad_gain.reshape(C), grad_wqkv, grad_wproj, grad_bias


def solution(mesh):
    shape = (mesh.shape["lon"] // 8, 4, 2, 2, 2)
    split = Mesh(mesh.devices.reshape(shape), ("z", "y", "xh", "xl", "c"))
    tokens = P(None, ("xl", "c"), ("z", "y", "xh"), None)
    table = P(("xl", "c"), None, None, None)
    return jax.shard_map(
        on_device,
        mesh=split,
        in_specs=(tokens, tokens, P(), P(), P(), table),
        out_specs=(tokens, P(), P(), P(), table),
        check_vma=False,
    )
```

```python
import functools

import jax
import jax.numpy as jnp
from jax import lax
from jax.experimental import pallas as pl
from jax.experimental.pallas import tpu as pltpu
from jax.sharding import Mesh, PartitionSpec as P

C = 192
HEADS = 6
HEAD_DIM = 32
WLON = 12
WIN = 144
TABLE = 3312
PAIRS = 12
OFFSETS = 23
LOG2E = 1.4426950408889634
SCALE = HEAD_DIM**-0.5
BODY = 120
TAIL = 24
MAIN = 128
LEFT = 16
SHARED = HEADS * LEFT
STRIPS = 3
WINDOWS = 6
TYPES = 12
GROUP = ("y", "xh", "xl", "c")
REST = "z"
PARTS = 32
W_PARTS = 24
W_LANES = 384
B_PARTS = 26
B_LANES = 128
GAIN_PART = 24
SEND_LANES = W_LANES + B_LANES
LATS = 4
WIDE = 3584
f32 = jnp.float32
bf16 = jnp.bfloat16
VMEM_LIMIT = 40 * 1024 * 1024

NN = (((1,), (0,)), ((), ()))
NT = (((1,), (1,)), ((), ()))


def dot(a, b, dims=NN):
    return lax.dot_general(a, b, dims, preferred_element_type=f32)


def table_offset(zl_i, zl_j):
    li, zi = divmod(zl_i, 2)
    lj, zj = divmod(zl_j, 2)
    return (((zi * 2 + zj) * 6 + li) * 6 + lj) * OFFSETS


def iota(shape, dim):
    return lax.broadcasted_iota(jnp.int32, shape, dim)


def ones_where(condition):
    return jnp.where(condition, 1.0, 0.0).astype(bf16)


def query_index(column):
    return jnp.where(column < MAIN, column, MAIN + column % LEFT)


def offset_match(oj, transposed):
    shape = (2 * MAIN, PAIRS * 32) if transposed else (PAIRS * 32, 2 * MAIN)
    row, col = iota(shape, 1 if transposed else 0), iota(shape, 0 if transposed else 1)
    token = query_index(col)
    zl = token // WLON
    target = zl * 32 + (oj + 11) - (token - zl * WLON)
    return ones_where((row == target) & (col < MAIN + SHARED))


def window_order(transposed):
    dest, source = iota((WIN, WIN), 1 if transposed else 0), iota((WIN, WIN), 0 if transposed else 1)
    window = dest // 24
    lz = window // STRIPS
    strip = window - lz * STRIPS
    inside = dest - window * 24
    zi = inside // WLON
    longitude = strip * WLON + inside - zi * WLON
    level = (2 * lz + zi + 1) % 4
    return ones_where(source == 4 * longitude + level)


def prepare_kernel(
    table_ref, wqkv_ref, wproj_ref, x_ref, g_ref,
    main_ref, left_ref, w3_ref, w3t_ref, wprojt_ref, own_ref, wide, pairs,
):
    for k in range(3):
        part = wqkv_ref[:, k * C : (k + 1) * C]
        w3_ref[k] = part
        w3t_ref[k * C : (k + 1) * C] = part.T
    wprojt_ref[...] = wproj_ref[...].T
    for a in range(3):
        own_ref[0, a] = x_ref[a + 3, 6:36].reshape(BODY, C)
        own_ref[1, a] = g_ref[a + 3, 6:36].reshape(BODY, C)
    wide[...] = jnp.zeros_like(wide)
    for h in range(HEADS):
        for lz in range(2):
            wide[lz * HEADS + h : lz * HEADS + h + 1, :TABLE] = table_ref[h, lz : lz + 1] * LOG2E
    pairs[...] = jnp.zeros_like(pairs)
    lane = iota((16, 128), 1)
    for zl_j in range(PAIRS):
        for v in range(3):
            total = jnp.zeros((16, 128), f32)
            for q in range(4):
                off = table_offset(4 * v + q, zl_j)
                base, rest = off // 128 * 128, off % 128
                width = 128 if rest + OFFSETS <= 128 else 256
                piece = wide[:, base : base + width]
                shift = (32 * q - rest) % width
                if shift:
                    piece = pltpu.roll(piece, shift, 1)
                inside = (lane >= 32 * q) & (lane < 32 * q + OFFSETS)
                total = jnp.where(inside, piece[:, :128], total)
            pairs[v, pl.ds(zl_j, TYPES, stride=16), :] = total[:TYPES]
    full = jnp.concatenate([pairs[v] for v in range(3)], axis=1)
    high = full.astype(bf16)
    rest = full - high.astype(f32)
    middle = rest.astype(bf16)
    low = (rest - middle.astype(f32)).astype(bf16)
    lane_head = iota((PAIRS, MAIN), 1) // LEFT
    for oj in range(WLON):
        match = offset_match(oj, False)
        dense = dot(high, match) + (dot(middle, match) + dot(low, match))
        for lz in range(2):
            left = jnp.zeros((PAIRS, MAIN), f32)
            for h in range(HEADS):
                t = lz * HEADS + h
                block = dense[t * 16 : t * 16 + PAIRS]
                main_ref[t, pl.ds(oj, PAIRS, stride=WLON), :] = block[:, :MAIN]
                left = jnp.where(lane_head == h, block[:, MAIN:], left)
            left_ref[lz, pl.ds(oj, PAIRS, stride=WLON), :] = left
    lat = lax.axis_index("xl") * 2 + lax.axis_index("c")
    last_band = (lat == LATS - 1).astype(jnp.int32)

    def region(token, last_level):
        upper = (token // WLON) % 2 * (2 * last_level)
        return upper + jnp.where(token >= 72, last_band, 0)

    j = iota((WIN, MAIN), 0)
    column = iota((WIN, MAIN), 1)
    for lz in range(2):
        allowed = region(column, lz) == region(j, lz)
        for h in range(HEADS):
            t = lz * HEADS + h
            main_ref[t] = jnp.where(allowed, main_ref[t], -1e30)
        allowed = region(query_index(column + MAIN), lz) == region(j, lz)
        left_ref[lz] = jnp.where(allowed, left_ref[lz], -1e30)


def prepare(table, wqkv, wproj, x, g):
    vmem = pl.BlockSpec(memory_space=pltpu.VMEM)
    return pl.pallas_call(
        prepare_kernel,
        out_shape=(
            jax.ShapeDtypeStruct((TYPES, WIN, MAIN), f32),
            jax.ShapeDtypeStruct((2, WIN, MAIN), f32),
            jax.ShapeDtypeStruct((3, C, C), bf16),
            jax.ShapeDtypeStruct((3 * C, C), bf16),
            jax.ShapeDtypeStruct((C, C), bf16),
            jax.ShapeDtypeStruct((2, 3, BODY, C), bf16),
        ),
        in_specs=[vmem] * 5,
        out_specs=(vmem,) * 6,
        scratch_shapes=[pltpu.VMEM((16, WIDE), f32), pltpu.VMEM((3, TYPES * 16, 128), f32)],
        compiler_params=pltpu.CompilerParams(vmem_limit_bytes=VMEM_LIMIT),
        cost_estimate=pl.CostEstimate(
            flops=4_000_000_000, bytes_accessed=4_000_000, transcendentals=0
        ),
        name="prepare",
    )(table, wqkv, wproj, x, g)


def normalised(values):
    mean = jnp.mean(values, axis=-1, keepdims=True)
    centred = values - mean
    inverse = lax.rsqrt(jnp.mean(centred * centred, axis=-1, keepdims=True) + 1e-05)
    return centred * inverse, inverse


def main_kernel(
    own_ref, lat_ref, lon_ref, corner_ref, gain_ref, w3_ref, w3t_ref, wproj_ref, wprojt_ref,
    bias_ref, left_ref, own_out, lat_out, lon_out, corner_out, send_out,
    xw, gw, rows, standard_ref, cot_ref, query_ref, key_ref, value_ref, mixed_ref, tokens_t_ref,
    qkv_t_ref, mixed_t_ref, scores_ref, grad_attend_ref, half_ref, grad_half_ref, dense, dense_left,
    wsum, psum, gsum, spread, wide, grads,
):
    order = window_order(False)
    for a in range(6):
        for k, to in enumerate((xw, gw)):
            if a < 3:
                body, tail = own_ref[k, a], lon_ref[k, a].reshape(TAIL, C)
            else:
                body = lat_ref[k, a - 3].reshape(BODY, C)
                tail = corner_ref[k, a - 3].reshape(TAIL, C)
            line = dot(order[:, :BODY], body) + dot(order[:, BODY:], tail)
            for w in range(WINDOWS):
                to[w, 24 * a : 24 * a + 24, :] = line[24 * w : 24 * w + 24]
    dense[...] = jnp.zeros_like(dense)
    dense_left[...] = jnp.zeros_like(dense_left)
    wsum[...] = jnp.zeros_like(wsum)
    psum[...] = jnp.zeros_like(psum)
    gsum[...] = jnp.zeros_like(gsum)
    gain = gain_ref[...]
    lane_head = iota((WIN, C), 1) // HEAD_DIM
    shape = (WIN, MAIN)
    repeat = ones_where((iota(shape, 0) == MAIN + iota(shape, 1) % LEFT) & (iota(shape, 1) < SHARED))
    shape = (MAIN, WIN)
    repeat_t = ones_where((iota(shape, 1) == MAIN + iota(shape, 0) % LEFT) & (iota(shape, 0) < SHARED))
    shape = (LEFT, MAIN)
    gather = ones_where((iota(shape, 0) == iota(shape, 1) % LEFT) & (iota(shape, 1) < SHARED))
    own_head_t = iota((C, MAIN), 0) // HEAD_DIM == iota((C, MAIN), 1) // LEFT
    own_head = iota((MAIN, C), 1) // HEAD_DIM == iota((MAIN, C), 0) // LEFT

    def of_head(value, h):
        return jnp.where(lane_head[: value.shape[0]] == h, value, jnp.zeros_like(value))

    def stacked(value):
        return jnp.concatenate([of_head(value, h) for h in range(HEADS)], axis=0)

    def only_head(mask, value):
        return jnp.where(mask, value, jnp.zeros_like(value)).astype(bf16)

    standard, _ = normalised(xw[...].reshape(WINDOWS * WIN, C))
    standard_ref[...] = standard
    scaled = standard * gain
    tokens = scaled.astype(bf16)
    cots = gw[...].reshape(WINDOWS * WIN, C).astype(bf16)
    cot_ref[...] = cots
    query_ref[...] = dot(tokens, w3_ref[0]).astype(bf16)
    key_ref[...] = dot(tokens, w3_ref[1]).astype(bf16)
    value_ref[...] = dot(tokens, w3_ref[2]).astype(bf16)
    mixed_ref[...] = dot(cots, wprojt_ref[...]).astype(bf16)
    for w in range(WINDOWS):
        tokens_t = scaled[w * WIN : (w + 1) * WIN].T.astype(bf16)
        tokens_t_ref[w] = tokens_t
        qkv_t_ref[w] = dot(w3t_ref[...], tokens_t).astype(bf16)
        mixed_t_ref[w] = dot(wproj_ref[...], gw[w].T.astype(bf16)).astype(bf16)

    for w in range(WINDOWS):
        lz = w // STRIPS
        span = slice(w * WIN, (w + 1) * WIN)
        query_t, mixed_t = qkv_t_ref[w, 0:C], mixed_t_ref[w]
        key, value = key_ref[span], value_ref[span]
        scores_ref[w, : HEADS * WIN] = dot(stacked(key), query_t[:, :MAIN])
        scores_ref[w, HEADS * WIN :] = dot(key, only_head(own_head_t, dot(query_t, repeat)))
        grad_attend_ref[w, : HEADS * WIN] = dot(stacked(value), mixed_t[:, :MAIN])
        grad_attend_ref[w, HEADS * WIN :] = dot(value, only_head(own_head_t, dot(mixed_t, repeat)))
        for t in range(HEADS + 1):
            lines = slice(t * WIN, (t + 1) * WIN)
            columns = slice(t * MAIN, (t + 1) * MAIN)
            bias = bias_ref[lz * HEADS + t] if t < HEADS else left_ref[lz]
            scores = scores_ref[w, lines] * (SCALE * LOG2E) + bias
            top = jnp.max(scores, axis=0, keepdims=True)
            powers = jnp.exp2(scores - top)
            attend = powers * (1.0 / jnp.sum(powers, axis=0, keepdims=True))
            half_ref[w, :, columns] = attend.astype(bf16)
            grad_attend = grad_attend_ref[w, lines]
            total = jnp.sum(attend * grad_attend, axis=0, keepdims=True)
            grad_scores = attend * (grad_attend - total)
            grad_half_ref[w, :, columns] = grad_scores.astype(bf16)
            if t < HEADS:
                dense[lz * HEADS + t] += grad_scores
            else:
                dense_left[lz] += grad_scores

    for w in range(WINDOWS):
        span = slice(w * WIN, (w + 1) * WIN)

        def per_query(left, right_ref):
            parts = [
                dot(
                    left[h * HEAD_DIM : (h + 1) * HEAD_DIM],
                    right_ref[w, :, h * MAIN : (h + 1) * MAIN],
                )
                for h in range(HEADS)
            ]
            shared = dot(left, right_ref[w, :, HEADS * MAIN :])
            return jnp.concatenate(parts, axis=0), jnp.where(own_head_t, shared, 0.0)

        def per_key(left_ref, right):
            parts = [of_head(right[:MAIN], h) for h in range(HEADS)]
            parts.append(only_head(own_head, dot(repeat_t, right)))
            return dot(left_ref[w], jnp.concatenate(parts, axis=0))

        cot = cot_ref[span]
        out_t, out_left = per_query(qkv_t_ref[w, 2 * C :], half_ref)
        psum[...] += dot(out_t.astype(bf16), cot[:MAIN]) + dot(
            out_left.astype(bf16), dot(repeat_t, cot).astype(bf16)
        )
        query_grad, query_left = per_query(qkv_t_ref[w, C : 2 * C], grad_half_ref)
        first = slice(w * WIN, w * WIN + MAIN)
        last = slice(w * WIN + MAIN, (w + 1) * WIN)
        spread[first, 0:C] = (query_grad * SCALE).T
        spread[last, 0:C] = dot(gather, (query_left * SCALE).T.astype(bf16))
        spread[span, C : 2 * C] = per_key(grad_half_ref, query_ref[span]) * SCALE
        spread[span, 2 * C :] = per_key(half_ref, mixed_ref[span])

    grad_projected = spread[...].astype(bf16)
    back = dot(grad_projected, w3t_ref[...]).astype(bf16).astype(f32)
    rows[...] = back.reshape(WINDOWS, WIN, C)
    gsum[0:1, :] = jnp.sum(back * standard_ref[...], axis=0, keepdims=True)
    for w in range(WINDOWS):
        wsum[...] += dot(tokens_t_ref[w], grad_projected[w * WIN : (w + 1) * WIN])

    order_t = window_order(True)
    for a in range(6):
        line = jnp.concatenate([rows[w, 24 * a : 24 * a + 24, :] for w in range(WINDOWS)], axis=0)
        line = dot(order_t, line.astype(bf16))
        body, tail = line[:BODY].astype(bf16), line[BODY:].astype(bf16)
        if a < 3:
            own_out[a], lon_out[a] = body, tail
        else:
            lat_out[a - 3], corner_out[a - 3] = body, tail

    total = jnp.zeros((TYPES * 16, PAIRS * 32), f32)
    lane_left = iota((PAIRS, MAIN), 1) // LEFT
    for oj in range(WLON):
        picked = []
        for lz in range(2):
            left = dense_left[lz, pl.ds(oj, PAIRS, stride=WLON), :]
            for h in range(HEADS):
                first = dense[lz * HEADS + h, pl.ds(oj, PAIRS, stride=WLON), :]
                both = jnp.concatenate([first, jnp.where(lane_left == h, left, 0.0)], axis=1)
                picked += [both, jnp.zeros((4, 2 * MAIN), f32)]
        picked = jnp.concatenate(picked, axis=0)
        high = picked.astype(bf16)
        low = (picked - high.astype(f32)).astype(bf16)
        match = offset_match(oj, True)
        total += dot(high, match) + dot(low, match)
    for v in range(3):
        grads[v] = total[:, 128 * v : 128 * (v + 1)]
    wide[...] = jnp.zeros_like(wide)
    lane = iota((TYPES, 256), 1)
    for zl_j in range(PAIRS):
        for v in range(3):
            four = grads[v, pl.ds(zl_j, TYPES, stride=16), :]
            for q in range(4):
                off = table_offset(4 * v + q, zl_j)
                base, rest = off // 128 * 128, off % 128
                width = 128 if rest + OFFSETS <= 128 else 256
                piece = four
                if width == 256:
                    piece = jnp.concatenate([four, jnp.zeros_like(four)], axis=1)
                shift = (rest - 32 * q) % width
                if shift:
                    piece = pltpu.roll(piece, shift, 1)
                position = lane[:, :width]
                inside = (position >= rest) & (position < rest + OFFSETS)
                target = (slice(0, TYPES), slice(base, base + width))
                wide[target] = jnp.where(inside, piece, wide[target])

    halves = []
    for n in range(2):
        if n == 0:
            halves.append(wsum[:, :W_LANES])
        else:
            halves.append(jnp.concatenate([wsum[:, W_LANES:], psum[...]], axis=1))
    for p in range(PARTS):
        if p < W_PARTS:
            lines = slice(p // 2 * 16, p // 2 * 16 + 16)
            send_out[p, :, :W_LANES] = halves[p % 2][lines].astype(bf16)
        elif p == GAIN_PART:
            gains = jnp.concatenate([gsum[...], jnp.zeros((8, C), f32)], axis=0)
            gains = jnp.concatenate([gains, jnp.zeros((16, W_LANES - C), f32)], axis=1)
            send_out[p, :, :W_LANES] = gains.astype(bf16)
        else:
            send_out[p, :, :W_LANES] = jnp.zeros((16, W_LANES), bf16)
        if p < B_PARTS:
            send_out[p, :, W_LANES:] = wide[:, p * B_LANES : (p + 1) * B_LANES].astype(bf16)
        else:
            send_out[p, :, W_LANES:] = jnp.zeros((16, B_LANES), bf16)


def main(own, lat_in, lon_in, corner_in, gain, w3, w3t, wproj, wproj_t, bias, bias_left):
    vmem = pl.BlockSpec(memory_space=pltpu.VMEM)
    return pl.pallas_call(
        main_kernel,
        out_shape=(
            jax.ShapeDtypeStruct((3, BODY, C), bf16),
            jax.ShapeDtypeStruct((3, BODY, C), bf16),
            jax.ShapeDtypeStruct((3, TAIL, C), bf16),
            jax.ShapeDtypeStruct((3, TAIL, C), bf16),
            jax.ShapeDtypeStruct((PARTS, 16, SEND_LANES), bf16),
        ),
        in_specs=[vmem] * 11,
        out_specs=(vmem,) * 5,
        scratch_shapes=[
            pltpu.VMEM((WINDOWS, WIN, C), f32),
            pltpu.VMEM((WINDOWS, WIN, C), f32),
            pltpu.VMEM((WINDOWS, WIN, C), f32),
            pltpu.VMEM((WINDOWS * WIN, C), f32),
            pltpu.VMEM((WINDOWS * WIN, C), bf16),
            pltpu.VMEM((WINDOWS * WIN, C), bf16),
            pltpu.VMEM((WINDOWS * WIN, C), bf16),
            pltpu.VMEM((WINDOWS * WIN, C), bf16),
            pltpu.VMEM((WINDOWS * WIN, C), bf16),
            pltpu.VMEM((WINDOWS, C, WIN), bf16),
            pltpu.VMEM((WINDOWS, 3 * C, WIN), bf16),
            pltpu.VMEM((WINDOWS, C, WIN), bf16),
            pltpu.VMEM((WINDOWS, (HEADS + 1) * WIN, MAIN), f32),
            pltpu.VMEM((WINDOWS, (HEADS + 1) * WIN, MAIN), f32),
            pltpu.VMEM((WINDOWS, WIN, (HEADS + 1) * MAIN), bf16),
            pltpu.VMEM((WINDOWS, WIN, (HEADS + 1) * MAIN), bf16),
            pltpu.VMEM((TYPES, WIN, MAIN), f32),
            pltpu.VMEM((2, WIN, MAIN), f32),
            pltpu.VMEM((C, 3 * C), f32),
            pltpu.VMEM((C, C), f32),
            pltpu.VMEM((8, C), f32),
            pltpu.VMEM((WINDOWS * WIN, 3 * C), f32),
            pltpu.VMEM((16, WIDE), f32),
            pltpu.VMEM((3, TYPES * 16, 128), f32),
        ],
        compiler_params=pltpu.CompilerParams(vmem_limit_bytes=VMEM_LIMIT),
        cost_estimate=pl.CostEstimate(
            flops=20_000_000_000, bytes_accessed=4_000_000, transcendentals=750_000
        ),
        name="window_grads",
    )(own, lat_in, lon_in, corner_in, gain, w3, w3t, wproj, wproj_t, bias, bias_left)


def norm_kernel(x_ref, g_ref, gain_ref, own_ref, lat_ref, lon_ref, corner_ref, out_ref):
    gain = gain_ref[...]
    for a in range(6):
        if a < 3:
            head, body = corner_ref[a], lat_ref[a]
        else:
            head, body = lon_ref[a - 3], own_ref[a - 3]
        grad = jnp.concatenate([head.astype(f32), body.astype(f32)], axis=0)
        standard, inverse = normalised(x_ref[a].reshape(WIN, C).astype(f32))
        scaled = grad * gain
        local = inverse * (
            scaled
            - jnp.mean(scaled, axis=-1, keepdims=True)
            - standard * jnp.mean(scaled * standard, axis=-1, keepdims=True)
        )
        total = (g_ref[a].reshape(WIN, C).astype(f32) + local).astype(bf16)
        out_ref[a] = total.reshape(36, 4, C)


def norm_grads(x, g, gain, own, lat_in, lon_in, corner_in):
    vmem = pl.BlockSpec(memory_space=pltpu.VMEM)
    return pl.pallas_call(
        norm_kernel,
        out_shape=jax.ShapeDtypeStruct(x.shape, bf16),
        in_specs=[vmem] * 7,
        out_specs=vmem,
        compiler_params=pltpu.CompilerParams(vmem_limit_bytes=VMEM_LIMIT),
        cost_estimate=pl.CostEstimate(
            flops=10_000_000, bytes_accessed=1_500_000, transcendentals=1000
        ),
        name="norm_grads",
    )(x, g, gain, own, lat_in, lon_in, corner_in)


def unpack_kernel(parts_ref, gain_out, wqkv_out, wproj_out, bias_out):
    gain_out[...] = parts_ref[GAIN_PART, :, :C].astype(f32)[:1]
    for p in range(W_PARTS):
        lines = slice(p // 2 * 16, p // 2 * 16 + 16)
        block = parts_ref[p, :, :W_LANES].astype(f32)
        if p % 2 == 0:
            wqkv_out[lines, :W_LANES] = block
        else:
            wqkv_out[lines, W_LANES:] = block[:, :C]
            wproj_out[lines, :] = block[:, C:]
    for p in range(B_PARTS):
        width = min(B_LANES, TABLE - p * B_LANES)
        block = parts_ref[p, :, W_LANES:].astype(f32)[:, :width]
        for h in range(HEADS):
            for lz in range(2):
                t = lz * HEADS + h
                bias_out[h, lz : lz + 1, p * B_LANES : p * B_LANES + width] = block[t : t + 1]


def unpack(parts):
    vmem = pl.BlockSpec(memory_space=pltpu.VMEM)
    return pl.pallas_call(
        unpack_kernel,
        out_shape=(
            jax.ShapeDtypeStruct((1, C), f32),
            jax.ShapeDtypeStruct((C, 3 * C), f32),
            jax.ShapeDtypeStruct((C, C), f32),
            jax.ShapeDtypeStruct((HEADS, 2, TABLE), f32),
        ),
        in_specs=[vmem],
        out_specs=(vmem,) * 4,
        compiler_params=pltpu.CompilerParams(vmem_limit_bytes=VMEM_LIMIT),
        name="unpack",
    )(parts)


def summed(send, ready):
    others = PARTS // LATS
    got = lax.all_to_all(send, GROUP, 0, 0, tiled=True)
    got = got.reshape((others, LATS, 16, SEND_LANES)).astype(f32)
    weights = jnp.sum(got[..., :W_LANES], axis=(0, 1))
    bias = jnp.sum(got[..., W_LANES:], axis=0)
    mixed = jnp.concatenate([weights] + [bias[n] for n in range(LATS)], axis=1).astype(bf16)
    mixed, ready = lax.optimization_barrier((mixed, ready))
    count = lax.axis_size(REST)
    got = lax.all_to_all(
        jnp.broadcast_to(mixed[None], (count,) + mixed.shape), REST, 0, 0, tiled=True
    )
    total = jnp.sum(got.astype(f32), axis=0).astype(bf16)
    weights = total[:, :W_LANES]
    rows = [
        jnp.concatenate([weights, total[:, W_LANES + n * B_LANES : W_LANES + (n + 1) * B_LANES]], 1)
        for n in range(LATS)
    ]
    spread = jnp.broadcast_to(jnp.stack(rows)[None], (others, LATS, 16, SEND_LANES))
    return lax.all_to_all(spread.reshape(send.shape), GROUP, 0, 0, tiled=True), ready


def on_device(x, g, ln_gain, w_qkv, w_proj, bias_table):
    lon_axes, lat_axes = ("z", "y", "xh"), ("xl", "c")
    both = lon_axes + lat_axes
    lons, lats = lax.axis_size(lon_axes), lax.axis_size(lat_axes)
    lon_swap = [(i, i ^ 1) for i in range(lons)]
    lat_down = [(i, (i - 1) % lats) for i in range(lats)]
    lat_up = [(i, (i + 1) % lats) for i in range(lats)]
    corner_down = [(i * lats + a, (i ^ 1) * lats + b) for i in range(lons) for a, b in lat_down]
    corner_up = [(i * lats + a, (i ^ 1) * lats + b) for i in range(lons) for a, b in lat_up]

    x, g = x.transpose(1, 2, 0, 3), g.transpose(1, 2, 0, 3)
    corner_in = lax.ppermute(jnp.stack([x[:3, :6], g[:3, :6]]), both, corner_down)
    lon_in = lax.ppermute(jnp.stack([x[3:, :6], g[3:, :6]]), lon_axes, lon_swap)
    lat_in = lax.ppermute(jnp.stack([x[:3, 6:], g[:3, 6:]]), lat_axes, lat_down)
    bias, bias_left, w3, w3t, wproj_t, own = prepare(
        bias_table[0].transpose(1, 0, 2), w_qkv, w_proj, x, g
    )
    gain = ln_gain.reshape(1, C)
    own, to_lat, to_lon, to_corner, send = main(
        own, lat_in, lon_in, corner_in, gain, w3, w3t, w_proj, wproj_t, bias, bias_left
    )
    back_corner = lax.ppermute(to_corner, both, corner_up)
    back_lon = lax.ppermute(to_lon, lon_axes, lon_swap)
    back_lat = lax.ppermute(to_lat, lat_axes, lat_up)
    parts, (back_lat, back_lon, back_corner) = summed(send, (back_lat, back_lon, back_corner))
    grad_gain, grad_wqkv, grad_wproj, grad_bias = unpack(parts)
    grad_x = norm_grads(x, g, gain, own, back_lat, back_lon, back_corner)
    grad_x = grad_x.transpose(2, 0, 1, 3)
    grad_bias = grad_bias.transpose(1, 0, 2)[None]
    return grad_x, grad_gain.reshape(C), grad_wqkv, grad_wproj, grad_bias


def solution(mesh):
    shape = (mesh.shape["lon"] // 8, 4, 2, 2, 2)
    split = Mesh(mesh.devices.reshape(shape), ("z", "y", "xh", "xl", "c"))
    tokens = P(None, ("xl", "c"), ("z", "y", "xh"), None)
    table = P(("xl", "c"), None, None, None)
    return jax.shard_map(
        on_device,
        mesh=split,
        in_specs=(tokens, tokens, P(), P(), P(), table),
        out_specs=(tokens, P(), P(), P(), table),
        check_vma=False,
    )
```

```python
import functools

import jax
import jax.numpy as jnp
from jax import lax
from jax.experimental import pallas as pl
from jax.experimental.pallas import tpu as pltpu
from jax.sharding import Mesh, PartitionSpec as P

C = 192
HEADS = 6
HEAD_DIM = 32
WLON = 12
WIN = 144
TABLE = 3312
PAIRS = 12
OFFSETS = 23
LOG2E = 1.4426950408889634
SCALE = HEAD_DIM**-0.5
BODY = 120
TAIL = 24
MAIN = 128
LEFT = 16
SHARED = HEADS * LEFT
STRIPS = 3
WINDOWS = 6
TYPES = 12
GROUP = ("y", "xh", "xl", "c")
REST = "z"
PARTS = 32
SLOTS = 3
W_TILES = 72
W_SLOTS = 2
B_COLUMNS = 26
B_TILES = 20
B_FIRST = 8
GAIN_PART = B_FIRST + B_TILES
WIDTH = 256
LATS = 4
WIDE = 3584
f32 = jnp.float32
bf16 = jnp.bfloat16
VMEM_LIMIT = 40 * 1024 * 1024

NN = (((1,), (0,)), ((), ()))
NT = (((1,), (1,)), ((), ()))


def dot(a, b, dims=NN):
    return lax.dot_general(a, b, dims, preferred_element_type=f32)


def table_offset(zl_i, zl_j):
    li, zi = divmod(zl_i, 2)
    lj, zj = divmod(zl_j, 2)
    return (((zi * 2 + zj) * 6 + li) * 6 + lj) * OFFSETS


def iota(shape, dim):
    return lax.broadcasted_iota(jnp.int32, shape, dim)


def ones_where(condition):
    return jnp.where(condition, 1.0, 0.0).astype(bf16)


def query_index(column):
    return jnp.where(column < MAIN, column, MAIN + column % LEFT)


def offset_match(oj, transposed):
    shape = (2 * MAIN, PAIRS * 32) if transposed else (PAIRS * 32, 2 * MAIN)
    row, col = iota(shape, 1 if transposed else 0), iota(shape, 0 if transposed else 1)
    token = query_index(col)
    zl = token // WLON
    target = zl * 32 + (oj + 11) - (token - zl * WLON)
    return ones_where((row == target) & (col < MAIN + SHARED))


def window_order(transposed):
    dest, source = iota((WIN, WIN), 1 if transposed else 0), iota((WIN, WIN), 0 if transposed else 1)
    window = dest // 24
    lz = window // STRIPS
    strip = window - lz * STRIPS
    inside = dest - window * 24
    zi = inside // WLON
    longitude = strip * WLON + inside - zi * WLON
    level = (2 * lz + zi + 1) % 4
    return ones_where(source == 4 * longitude + level)


def prepare_kernel(
    table_ref, wqkv_ref, wproj_ref, gain_ref, x_ref, g_ref,
    main_ref, left_ref, w3_ref, w3t_ref, wprojt_ref, own_ref, match_ref, gain_out, wide, pairs,
):
    gain_out[...] = gain_ref[...]
    for k in range(3):
        part = wqkv_ref[:, k * C : (k + 1) * C]
        w3_ref[k] = part
        w3t_ref[k * WIDTH : k * WIDTH + C] = part.T
        w3t_ref[k * WIDTH + C : (k + 1) * WIDTH] = jnp.zeros((WIDTH - C, C), bf16)
    wprojt_ref[...] = wproj_ref[...].T
    for a in range(3):
        own_ref[0, a] = x_ref[a + 3, 6:36].reshape(BODY, C)
        own_ref[1, a] = g_ref[a + 3, 6:36].reshape(BODY, C)
    wide[...] = jnp.zeros_like(wide)
    for h in range(HEADS):
        for lz in range(2):
            wide[lz * HEADS + h : lz * HEADS + h + 1, :TABLE] = table_ref[h, lz : lz + 1] * LOG2E
    pairs[...] = jnp.zeros_like(pairs)
    lane = iota((16, 128), 1)
    for zl_j in range(PAIRS):
        for v in range(3):
            total = jnp.zeros((16, 128), f32)
            for q in range(4):
                off = table_offset(4 * v + q, zl_j)
                base, rest = off // 128 * 128, off % 128
                width = 128 if rest + OFFSETS <= 128 else 256
                piece = wide[:, base : base + width]
                shift = (32 * q - rest) % width
                if shift:
                    piece = pltpu.roll(piece, shift, 1)
                inside = (lane >= 32 * q) & (lane < 32 * q + OFFSETS)
                total = jnp.where(inside, piece[:, :128], total)
            pairs[v, pl.ds(zl_j, TYPES, stride=16), :] = total[:TYPES]
    full = jnp.concatenate([pairs[v] for v in range(3)], axis=1)
    high = full.astype(bf16)
    rest = full - high.astype(f32)
    middle = rest.astype(bf16)
    low = (rest - middle.astype(f32)).astype(bf16)
    lane_head = iota((PAIRS, MAIN), 1) // LEFT
    for oj in range(WLON):
        match_ref[oj] = offset_match(oj, True)
        match = offset_match(oj, False)
        dense = dot(high, match) + (dot(middle, match) + dot(low, match))
        for lz in range(2):
            left = jnp.zeros((PAIRS, MAIN), f32)
            for h in range(HEADS):
                t = lz * HEADS + h
                block = dense[t * 16 : t * 16 + PAIRS]
                main_ref[t, pl.ds(oj, PAIRS, stride=WLON), :] = block[:, :MAIN]
                left = jnp.where(lane_head == h, block[:, MAIN:], left)
            left_ref[lz, pl.ds(oj, PAIRS, stride=WLON), :] = left
    lat = lax.axis_index("xl") * 2 + lax.axis_index("c")
    last_band = (lat == LATS - 1).astype(jnp.int32)

    def region(token, last_level):
        upper = (token // WLON) % 2 * (2 * last_level)
        return upper + jnp.where(token >= 72, last_band, 0)

    j = iota((WIN, MAIN), 0)
    column = iota((WIN, MAIN), 1)
    for lz in range(2):
        allowed = region(column, lz) == region(j, lz)
        for h in range(HEADS):
            t = lz * HEADS + h
            main_ref[t] = jnp.where(allowed, main_ref[t], -1e30)
        allowed = region(query_index(column + MAIN), lz) == region(j, lz)
        left_ref[lz] = jnp.where(allowed, left_ref[lz], -1e30)


def prepare(table, wqkv, wproj, gain, x, g):
    vmem = pl.BlockSpec(memory_space=pltpu.VMEM)
    return pl.pallas_call(
        prepare_kernel,
        out_shape=(
            jax.ShapeDtypeStruct((TYPES, WIN, MAIN), f32),
            jax.ShapeDtypeStruct((2, WIN, MAIN), f32),
            jax.ShapeDtypeStruct((3, C, C), bf16),
            jax.ShapeDtypeStruct((3 * WIDTH, C), bf16),
            jax.ShapeDtypeStruct((C, C), bf16),
            jax.ShapeDtypeStruct((2, 3, BODY, C), bf16),
            jax.ShapeDtypeStruct((WLON, 2 * MAIN, PAIRS * 32), bf16),
            jax.ShapeDtypeStruct((1, C), f32),
        ),
        in_specs=[vmem] * 6,
        out_specs=(vmem,) * 8,
        scratch_shapes=[pltpu.VMEM((16, WIDE), f32), pltpu.VMEM((3, TYPES * 16, 128), f32)],
        compiler_params=pltpu.CompilerParams(vmem_limit_bytes=VMEM_LIMIT),
        cost_estimate=pl.CostEstimate(
            flops=4_000_000_000, bytes_accessed=4_000_000, transcendentals=0
        ),
        name="prepare",
    )(table, wqkv, wproj, gain, x, g)


def normalised(values):
    mean = jnp.mean(values, axis=-1, keepdims=True)
    centred = values - mean
    inverse = lax.rsqrt(jnp.mean(centred * centred, axis=-1, keepdims=True) + 1e-05)
    return centred * inverse, inverse


def w_place(t):
    if t < W_SLOTS * PARTS:
        return t // W_SLOTS, t % W_SLOTS
    return t - W_SLOTS * PARTS, W_SLOTS


def main_kernel(
    own_ref, lat_ref, lon_ref, corner_ref, gain_ref, w3_ref, w3t_ref, wproj_ref, wprojt_ref,
    bias_ref, left_ref, match_ref, rows_out, send_out,
    xw, gw, standard_ref, cot_ref, query_ref, key_ref, value_ref, mixed_ref, tokens_t_ref,
    qkv_t_ref, mixed_t_ref, scores_ref, grad_attend_ref, half_ref, grad_half_ref, dense, dense_left,
    wsum, psum, gsum, spread, wide, grads, stack,
):
    order = window_order(False)
    for a in range(6):
        for k, to in enumerate((xw, gw)):
            if a < 3:
                body, tail = own_ref[k, a], lon_ref[k, a].reshape(TAIL, C)
            else:
                body = lat_ref[k, a - 3].reshape(BODY, C)
                tail = corner_ref[k, a - 3].reshape(TAIL, C)
            line = dot(order[:, :BODY], body) + dot(order[:, BODY:], tail)
            for w in range(WINDOWS):
                to[w, 24 * a : 24 * a + 24, :] = line[24 * w : 24 * w + 24]
    dense[...] = jnp.zeros_like(dense)
    dense_left[...] = jnp.zeros_like(dense_left)
    gsum[...] = jnp.zeros_like(gsum)
    spread[...] = jnp.zeros_like(spread)
    gain = gain_ref[...]
    lane_head = iota((WIN, C), 1) // HEAD_DIM
    shape = (WIN, MAIN)
    repeat = ones_where((iota(shape, 0) == MAIN + iota(shape, 1) % LEFT) & (iota(shape, 1) < SHARED))
    shape = (MAIN, WIN)
    repeat_t = ones_where((iota(shape, 1) == MAIN + iota(shape, 0) % LEFT) & (iota(shape, 0) < SHARED))
    shape = (LEFT, MAIN)
    gather = ones_where((iota(shape, 0) == iota(shape, 1) % LEFT) & (iota(shape, 1) < SHARED))
    own_head_t = iota((C, MAIN), 0) // HEAD_DIM == iota((C, MAIN), 1) // LEFT
    own_head = iota((MAIN, C), 1) // HEAD_DIM == iota((MAIN, C), 0) // LEFT

    def of_head(value, h):
        return jnp.where(lane_head[: value.shape[0]] == h, value, jnp.zeros_like(value))

    def stacked(value):
        return jnp.concatenate([of_head(value, h) for h in range(HEADS)], axis=0)

    def only_head(mask, value):
        return jnp.where(mask, value, jnp.zeros_like(value)).astype(bf16)

    standard, _ = normalised(xw[...].reshape(WINDOWS * WIN, C))
    standard_ref[...] = standard
    scaled = standard * gain
    tokens = scaled.astype(bf16)
    cots = gw[...].reshape(WINDOWS * WIN, C).astype(bf16)
    cot_ref[...] = cots
    query_ref[...] = dot(tokens, w3_ref[0]).astype(bf16)
    key_ref[...] = dot(tokens, w3_ref[1]).astype(bf16)
    value_ref[...] = dot(tokens, w3_ref[2]).astype(bf16)
    mixed_ref[...] = dot(cots, wprojt_ref[...]).astype(bf16)
    for w in range(WINDOWS):
        tokens_t = scaled[w * WIN : (w + 1) * WIN].T.astype(bf16)
        tokens_t_ref[w] = tokens_t
        for k in range(3):
            part = dot(w3t_ref[k * WIDTH : k * WIDTH + C], tokens_t)
            qkv_t_ref[w, k * C : (k + 1) * C] = part.astype(bf16)
        mixed_t_ref[w] = dot(wproj_ref[...], gw[w].T.astype(bf16)).astype(bf16)

    for w in range(WINDOWS):
        lz = w // STRIPS
        span = slice(w * WIN, (w + 1) * WIN)
        query_t, mixed_t = qkv_t_ref[w, 0:C], mixed_t_ref[w]
        key, value = key_ref[span], value_ref[span]
        scores_ref[w, : HEADS * WIN] = dot(stacked(key), query_t[:, :MAIN])
        scores_ref[w, HEADS * WIN :] = dot(key, only_head(own_head_t, dot(query_t, repeat)))
        grad_attend_ref[w, : HEADS * WIN] = dot(stacked(value), mixed_t[:, :MAIN])
        grad_attend_ref[w, HEADS * WIN :] = dot(value, only_head(own_head_t, dot(mixed_t, repeat)))
        for t in range(HEADS + 1):
            lines = slice(t * WIN, (t + 1) * WIN)
            columns = slice(t * MAIN, (t + 1) * MAIN)
            bias = bias_ref[lz * HEADS + t] if t < HEADS else left_ref[lz]
            scores = scores_ref[w, lines] * (SCALE * LOG2E) + bias
            top = jnp.max(scores, axis=0, keepdims=True)
            powers = jnp.exp2(scores - top)
            attend = powers * (1.0 / jnp.sum(powers, axis=0, keepdims=True))
            half_ref[w, :, columns] = attend.astype(bf16)
            grad_attend = grad_attend_ref[w, lines]
            total = jnp.sum(attend * grad_attend, axis=0, keepdims=True)
            grad_scores = attend * (grad_attend - total)
            grad_half_ref[w, :, columns] = grad_scores.astype(bf16)
            if t < HEADS:
                dense[lz * HEADS + t] += grad_scores
            else:
                dense_left[lz] += grad_scores

    for w in range(WINDOWS):
        span = slice(w * WIN, (w + 1) * WIN)

        def per_query(left, right_ref):
            parts = []
            for h in range(0, HEADS, 2):
                two = dot(
                    left[h * HEAD_DIM : (h + 2) * HEAD_DIM],
                    right_ref[w, :, h * MAIN : (h + 2) * MAIN],
                )
                parts += [two[:HEAD_DIM, :MAIN], two[HEAD_DIM:, MAIN:]]
            shared = dot(left, right_ref[w, :, HEADS * MAIN :])
            return jnp.concatenate(parts, axis=0), jnp.where(own_head_t, shared, 0.0)

        def per_key(left_ref, right):
            parts = [of_head(right[:MAIN], h) for h in range(HEADS)]
            parts.append(only_head(own_head, dot(repeat_t, right)))
            return dot(left_ref[w], jnp.concatenate(parts, axis=0))

        cot = cot_ref[span]
        out_t, out_left = per_query(qkv_t_ref[w, 2 * C :], half_ref)
        both = jnp.concatenate([out_t.astype(bf16), out_left.astype(bf16)], axis=1)
        added = dot(both, jnp.concatenate([cot[:MAIN], dot(repeat_t, cot).astype(bf16)], axis=0))
        psum[...] = added if w == 0 else psum[...] + added
        query_grad, query_left = per_query(qkv_t_ref[w, C : 2 * C], grad_half_ref)
        first = slice(w * WIN, w * WIN + MAIN)
        last = slice(w * WIN + MAIN, (w + 1) * WIN)
        spread[first, 0:C] = (query_grad * SCALE).astype(bf16).T
        spread[last, 0:C] = dot(gather, (query_left * SCALE).astype(bf16).T).astype(bf16)
        grad_key = per_key(grad_half_ref, query_ref[span]) * SCALE
        spread[span, WIDTH : WIDTH + C] = grad_key.astype(bf16)
        spread[span, 2 * WIDTH : 2 * WIDTH + C] = per_key(half_ref, mixed_ref[span]).astype(bf16)

    grad_projected = spread[...]
    back = dot(grad_projected, w3t_ref[...]).astype(bf16)
    rows_out[...] = back
    gsum[0:1, :] = jnp.sum(back.astype(f32) * standard_ref[...], axis=0, keepdims=True)
    for w in range(WINDOWS):
        added = dot(tokens_t_ref[w], spread[w * WIN : (w + 1) * WIN])
        wsum[...] = added if w == 0 else wsum[...] + added

    total = jnp.zeros((TYPES * 16, PAIRS * 32), f32)
    lane_left = iota((PAIRS, MAIN), 1) // LEFT
    for oj in range(WLON):
        picked = []
        for lz in range(2):
            left = dense_left[lz, pl.ds(oj, PAIRS, stride=WLON), :]
            for h in range(HEADS):
                first = dense[lz * HEADS + h, pl.ds(oj, PAIRS, stride=WLON), :]
                both = jnp.concatenate([first, jnp.where(lane_left == h, left, 0.0)], axis=1)
                picked += [both, jnp.zeros((4, 2 * MAIN), f32)]
        picked = jnp.concatenate(picked, axis=0)
        high = picked.astype(bf16)
        low = (picked - high.astype(f32)).astype(bf16)
        match = match_ref[oj]
        total += dot(high, match) + dot(low, match)
    for v in range(3):
        grads[v] = total[:, 128 * v : 128 * (v + 1)]
    wide[...] = jnp.zeros_like(wide)
    lane = iota((TYPES, 256), 1)
    for zl_j in range(PAIRS):
        for v in range(3):
            four = grads[v, pl.ds(zl_j, TYPES, stride=16), :]
            for q in range(4):
                off = table_offset(4 * v + q, zl_j)
                base, rest = off // 128 * 128, off % 128
                width = 128 if rest + OFFSETS <= 128 else 256
                piece = four
                if width == 256:
                    piece = jnp.concatenate([four, jnp.zeros_like(four)], axis=1)
                shift = (rest - 32 * q) % width
                if shift:
                    piece = pltpu.roll(piece, shift, 1)
                position = lane[:, :width]
                inside = (position >= rest) & (position < rest + OFFSETS)
                target = (slice(0, TYPES), slice(base, base + width))
                wide[target] = jnp.where(inside, piece, wide[target])

    weights = jnp.concatenate(
        [wsum[:, k * WIDTH : k * WIDTH + C] for k in range(3)] + [psum[...]], axis=1
    )
    for t in range(W_TILES):
        row, column = divmod(t, 6)
        tile = weights[16 * row : 16 * row + 16, 128 * column : 128 * column + 128]
        p, slot = w_place(t)
        send_out[p, :, 128 * slot : 128 * slot + 128] = tile.astype(bf16)
    stack[...] = jnp.zeros_like(stack)
    for n in range(B_COLUMNS):
        stack[TYPES * n : TYPES * (n + 1), :] = wide[:TYPES, 128 * n : 128 * (n + 1)]
    last = slice(128 * W_SLOTS, 128 * SLOTS)
    for n in range(B_TILES):
        send_out[B_FIRST + n, :, last] = stack[16 * n : 16 * n + 16, :].astype(bf16)
    for p in range(GAIN_PART, PARTS):
        if p == GAIN_PART:
            line = gsum[0:1, :]
            gains = jnp.concatenate([line[:, :128], jnp.zeros((7, 128), f32)], axis=0)
            more = jnp.concatenate([line[:, 128:], jnp.zeros((1, 256 - C), f32)], axis=1)
            more = jnp.concatenate([more, jnp.zeros((7, 128), f32)], axis=0)
            send_out[p, :, last] = jnp.concatenate([gains, more], axis=0).astype(bf16)
        else:
            send_out[p, :, last] = jnp.zeros((16, 128), bf16)


def main(own, lat_in, lon_in, corner_in, gain, w3, w3t, wproj, wproj_t, bias, bias_left, match):
    vmem = pl.BlockSpec(memory_space=pltpu.VMEM)
    return pl.pallas_call(
        main_kernel,
        out_shape=(
            jax.ShapeDtypeStruct((WINDOWS * WIN, C), bf16),
            jax.ShapeDtypeStruct((PARTS, 16, SLOTS * 128), bf16),
        ),
        in_specs=[vmem] * 12,
        out_specs=(vmem,) * 2,
        scratch_shapes=[
            pltpu.VMEM((WINDOWS, WIN, C), f32),
            pltpu.VMEM((WINDOWS, WIN, C), f32),
            pltpu.VMEM((WINDOWS * WIN, C), f32),
            pltpu.VMEM((WINDOWS * WIN, C), bf16),
            pltpu.VMEM((WINDOWS * WIN, C), bf16),
            pltpu.VMEM((WINDOWS * WIN, C), bf16),
            pltpu.VMEM((WINDOWS * WIN, C), bf16),
            pltpu.VMEM((WINDOWS * WIN, C), bf16),
            pltpu.VMEM((WINDOWS, C, WIN), bf16),
            pltpu.VMEM((WINDOWS, 3 * C, WIN), bf16),
            pltpu.VMEM((WINDOWS, C, WIN), bf16),
            pltpu.VMEM((WINDOWS, (HEADS + 1) * WIN, MAIN), f32),
            pltpu.VMEM((WINDOWS, (HEADS + 1) * WIN, MAIN), f32),
            pltpu.VMEM((WINDOWS, WIN, (HEADS + 1) * MAIN), bf16),
            pltpu.VMEM((WINDOWS, WIN, (HEADS + 1) * MAIN), bf16),
            pltpu.VMEM((TYPES, WIN, MAIN), f32),
            pltpu.VMEM((2, WIN, MAIN), f32),
            pltpu.VMEM((C, 3 * WIDTH), f32),
            pltpu.VMEM((C, C), f32),
            pltpu.VMEM((8, C), f32),
            pltpu.VMEM((WINDOWS * WIN, 3 * WIDTH), bf16),
            pltpu.VMEM((16, WIDE), f32),
            pltpu.VMEM((3, TYPES * 16, 128), f32),
            pltpu.VMEM((B_TILES * 16, 128), f32),
        ],
        compiler_params=pltpu.CompilerParams(vmem_limit_bytes=VMEM_LIMIT),
        cost_estimate=pl.CostEstimate(
            flops=20_000_000_000, bytes_accessed=4_000_000, transcendentals=750_000
        ),
        name="window_grads",
    )(own, lat_in, lon_in, corner_in, gain, w3, w3t, wproj, wproj_t, bias, bias_left, match)


def pieces_kernel(rows_ref, body_out, tail_out):
    order_t = window_order(True)
    for a in range(6):
        line = jnp.concatenate(
            [rows_ref[WIN * w + 24 * a : WIN * w + 24 * a + 24, :] for w in range(WINDOWS)], axis=0
        )
        line = dot(order_t, line)
        body_out[a] = line[:BODY].astype(bf16)
        tail_out[a] = line[BODY:].astype(bf16)


def pieces(rows):
    vmem = pl.BlockSpec(memory_space=pltpu.VMEM)
    return pl.pallas_call(
        pieces_kernel,
        out_shape=(
            jax.ShapeDtypeStruct((6, BODY, C), bf16),
            jax.ShapeDtypeStruct((6, TAIL, C), bf16),
        ),
        in_specs=[vmem],
        out_specs=(vmem,) * 2,
        compiler_params=pltpu.CompilerParams(vmem_limit_bytes=VMEM_LIMIT),
        cost_estimate=pl.CostEstimate(
            flops=500_000_000, bytes_accessed=700_000, transcendentals=0
        ),
        name="pieces",
    )(rows)


def norm_kernel(x_ref, g_ref, gain_ref, body_ref, tail_ref, lat_ref, out_ref):
    gain = gain_ref[...]
    for a in range(6):
        if a < 3:
            grad = lat_ref[a].astype(f32)
        else:
            grad = [tail_ref[a - 3].astype(f32), body_ref[a - 3].astype(f32)]
            grad = jnp.concatenate(grad, axis=0)
        standard, inverse = normalised(x_ref[a].reshape(WIN, C).astype(f32))
        scaled = grad * gain
        local = inverse * (
            scaled
            - jnp.mean(scaled, axis=-1, keepdims=True)
            - standard * jnp.mean(scaled * standard, axis=-1, keepdims=True)
        )
        total = (g_ref[a].reshape(WIN, C).astype(f32) + local).astype(bf16)
        out_ref[a] = total.reshape(36, 4, C)


def norm_grads(x, g, gain, body, tail, lat_in):
    vmem = pl.BlockSpec(memory_space=pltpu.VMEM)
    return pl.pallas_call(
        norm_kernel,
        out_shape=jax.ShapeDtypeStruct(x.shape, bf16),
        in_specs=[vmem] * 6,
        out_specs=vmem,
        compiler_params=pltpu.CompilerParams(vmem_limit_bytes=VMEM_LIMIT),
        cost_estimate=pl.CostEstimate(
            flops=10_000_000, bytes_accessed=1_500_000, transcendentals=1000
        ),
        name="norm_grads",
    )(x, g, gain, body, tail, lat_in)


def unpack_kernel(parts_ref, gain_out, wqkv_out, wproj_out, bias_out, stack):
    last = slice(128 * W_SLOTS, 128 * SLOTS)
    gains = parts_ref[GAIN_PART, :, last].astype(f32)
    gain_out[:, :128] = gains[0:1]
    gain_out[:, 128:] = gains[8:9, : C - 128]

    def tile(t):
        p, slot = w_place(t)
        return parts_ref[p, :, 128 * slot : 128 * slot + 128].astype(f32)

    for row in range(C // 16):
        lines = slice(16 * row, 16 * row + 16)
        for column in range(4):
            wqkv_out[lines, 128 * column : 128 * column + 128] = tile(6 * row + column)
        mixed = tile(6 * row + 4)
        wqkv_out[lines, 512:] = mixed[:, :64]
        wproj_out[lines, :] = jnp.concatenate([mixed[:, 64:], tile(6 * row + 5)], axis=1)
    for n in range(B_TILES):
        stack[16 * n : 16 * n + 16, :] = parts_ref[B_FIRST + n, :, last].astype(f32)
    for n in range(B_COLUMNS):
        width = min(128, TABLE - 128 * n)
        for h in range(HEADS):
            for lz in range(2):
                t = TYPES * n + lz * HEADS + h
                bias_out[h, lz : lz + 1, 128 * n : 128 * n + width] = stack[t : t + 1, :width]


def unpack(parts):
    vmem = pl.BlockSpec(memory_space=pltpu.VMEM)
    return pl.pallas_call(
        unpack_kernel,
        out_shape=(
            jax.ShapeDtypeStruct((1, C), f32),
            jax.ShapeDtypeStruct((C, 3 * C), f32),
            jax.ShapeDtypeStruct((C, C), f32),
            jax.ShapeDtypeStruct((HEADS, 2, TABLE), f32),
        ),
        in_specs=[vmem],
        out_specs=(vmem,) * 4,
        scratch_shapes=[pltpu.VMEM((B_TILES * 16, 128), f32)],
        compiler_params=pltpu.CompilerParams(vmem_limit_bytes=VMEM_LIMIT),
        name="unpack",
    )(parts)


def scattered(send):
    got = lax.all_to_all(send, GROUP, 0, 0, tiled=True)
    got = got.reshape((PARTS // LATS, LATS, 16, SLOTS * 128)).astype(f32)
    shared = jnp.sum(got[..., : 128 * W_SLOTS], axis=(0, 1))
    last = jnp.sum(got[..., 128 * W_SLOTS :], axis=0)
    return jnp.concatenate([shared] + [last[n] for n in range(LATS)], axis=1).astype(bf16)


def exchanged(mixed):
    count = lax.axis_size(REST)
    got = lax.all_to_all(
        jnp.broadcast_to(mixed[None], (count,) + mixed.shape), REST, 0, 0, tiled=True
    )
    total = jnp.sum(got.astype(f32), axis=0)
    shared = total[:, : 128 * W_SLOTS]
    last = [total[:, 128 * (W_SLOTS + n) : 128 * (W_SLOTS + n + 1)] for n in range(LATS)]
    everywhere = last[0] + last[1] + last[2] + last[3]
    part = lax.axis_index(GROUP)
    per_lat = (part >= B_FIRST) & (part < GAIN_PART)
    rows = [
        jnp.concatenate([shared, jnp.where(per_lat, last[n], everywhere)], axis=1).astype(bf16)
        for n in range(LATS)
    ]
    spread = jnp.broadcast_to(jnp.stack(rows)[None], (PARTS // LATS, LATS, 16, SLOTS * 128))
    return spread.reshape(PARTS, 16, SLOTS * 128)


def pack_kernel(x_ref, g_ref, corner_out, lon_out, lat_out, sems):
    copies = []
    for k, ref in enumerate((x_ref, g_ref)):
        for n, (source, to) in enumerate(
            (
                (ref.at[pl.ds(0, 3), pl.ds(0, 6)], corner_out),
                (ref.at[pl.ds(3, 3), pl.ds(0, 6)], lon_out),
                (ref.at[pl.ds(0, 3), pl.ds(6, 30)], lat_out),
            )
        ):
            copies.append(pltpu.make_async_copy(source, to.at[k], sems.at[3 * k + n]))
    for copy in copies:
        copy.start()
    for copy in copies:
        copy.wait()


def pack(x, g):
    vmem = pl.BlockSpec(memory_space=pltpu.VMEM)
    return pl.pallas_call(
        pack_kernel,
        out_shape=(
            jax.ShapeDtypeStruct((2, 3, 6, 4, C), bf16),
            jax.ShapeDtypeStruct((2, 3, 6, 4, C), bf16),
            jax.ShapeDtypeStruct((2, 3, 30, 4, C), bf16),
        ),
        in_specs=[pl.BlockSpec(memory_space=pltpu.HBM)] * 2,
        out_specs=(vmem,) * 3,
        scratch_shapes=[pltpu.SemaphoreType.DMA((6,))],
        compiler_params=pltpu.CompilerParams(vmem_limit_bytes=VMEM_LIMIT),
        name="pack",
    )(x, g)


def on_device(x, g, ln_gain, w_qkv, w_proj, bias_table):
    lon_axes, lat_axes = ("z", "y", "xh"), ("xl", "c")
    both = lon_axes + lat_axes
    lons, lats = lax.axis_size(lon_axes), lax.axis_size(lat_axes)
    lon_swap = [(i, i ^ 1) for i in range(lons)]
    lat_down = [(i, (i - 1) % lats) for i in range(lats)]
    lat_up = [(i, (i + 1) % lats) for i in range(lats)]
    corner_down = [(i * lats + a, (i ^ 1) * lats + b) for i in range(lons) for a, b in lat_down]

    x, g = x.transpose(1, 2, 0, 3), g.transpose(1, 2, 0, 3)
    to_corner, to_lon, to_lat = pack(x, g)
    corner_in = lax.ppermute(to_corner, both, corner_down)
    lon_in = lax.ppermute(to_lon, lon_axes, lon_swap)
    lat_in = lax.ppermute(to_lat, lat_axes, lat_down)
    bias, bias_left, w3, w3t, wproj_t, own, match, gain = prepare(
        bias_table[0].transpose(1, 0, 2), w_qkv, w_proj, ln_gain.reshape(1, C), x, g
    )
    rows, send = main(
        own, lat_in, lon_in, corner_in, gain, w3, w3t, w_proj, wproj_t, bias, bias_left, match
    )
    body, tail = pieces(rows)
    tail = lax.ppermute(tail, lon_axes, lon_swap)
    mixed, tail = lax.optimization_barrier((scattered(send), tail))
    lat_rows = lax.ppermute(jnp.concatenate([tail[3:], body[3:]], axis=1), lat_axes, lat_up)
    spread, lat_rows = lax.optimization_barrier((exchanged(mixed), lat_rows))
    parts = lax.all_to_all(spread, GROUP, 0, 0, tiled=True)
    grad_gain, grad_wqkv, grad_wproj, grad_bias = unpack(parts)
    grad_x = norm_grads(x, g, gain, body, tail, lat_rows)
    grad_x = grad_x.transpose(2, 0, 1, 3)
    grad_bias = grad_bias.transpose(1, 0, 2)[None]
    return grad_x, grad_gain.reshape(C), grad_wqkv, grad_wproj, grad_bias


def solution(mesh):
    shape = (mesh.shape["lon"] // 8, 4, 2, 2, 2)
    split = Mesh(mesh.devices.reshape(shape), ("z", "y", "xh", "xl", "c"))
    tokens = P(None, ("xl", "c"), ("z", "y", "xh"), None)
    table = P(("xl", "c"), None, None, None)
    return jax.shard_map(
        on_device,
        mesh=split,
        in_specs=(tokens, tokens, P(), P(), P(), table),
        out_specs=(tokens, P(), P(), P(), table),
        check_vma=False,
    )
```

```python
import functools

import jax
import jax.numpy as jnp
from jax import lax
from jax.experimental import pallas as pl
from jax.experimental.pallas import tpu as pltpu
from jax.sharding import Mesh, PartitionSpec as P

C = 192
HEADS = 6
HEAD_DIM = 32
WLON = 12
WIN = 144
TABLE = 3312
PAIRS = 12
OFFSETS = 23
LOG2E = 1.4426950408889634
SCALE = HEAD_DIM**-0.5
BODY = 120
TAIL = 24
MAIN = 128
LEFT = 16
SHARED = HEADS * LEFT
STRIPS = 3
WINDOWS = 6
TYPES = 12
GROUP = ("y", "xh", "xl", "c")
REST = "z"
PARTS = 32
SLOTS = 3
W_TILES = 72
W_SLOTS = 2
B_COLUMNS = 26
B_TILES = 20
B_FIRST = 8
GAIN_PART = B_FIRST + B_TILES
WIDTH = 256
LATS = 4
WIDE = 3584
f32 = jnp.float32
bf16 = jnp.bfloat16
VMEM_LIMIT = 40 * 1024 * 1024

NN = (((1,), (0,)), ((), ()))
NT = (((1,), (1,)), ((), ()))


def dot(a, b, dims=NN):
    return lax.dot_general(a, b, dims, preferred_element_type=f32)


def table_offset(zl_i, zl_j):
    li, zi = divmod(zl_i, 2)
    lj, zj = divmod(zl_j, 2)
    return (((zi * 2 + zj) * 6 + li) * 6 + lj) * OFFSETS


def iota(shape, dim):
    return lax.broadcasted_iota(jnp.int32, shape, dim)


def ones_where(condition):
    return jnp.where(condition, 1.0, 0.0).astype(bf16)


def query_index(column):
    return jnp.where(column < MAIN, column, MAIN + column % LEFT)


def offset_match(oj, transposed):
    shape = (2 * MAIN, PAIRS * 32) if transposed else (PAIRS * 32, 2 * MAIN)
    row, col = iota(shape, 1 if transposed else 0), iota(shape, 0 if transposed else 1)
    token = query_index(col)
    zl = token // WLON
    target = zl * 32 + (oj + 11) - (token - zl * WLON)
    return ones_where((row == target) & (col < MAIN + SHARED))


def window_order(transposed):
    dest, source = iota((WIN, WIN), 1 if transposed else 0), iota((WIN, WIN), 0 if transposed else 1)
    window = dest // 24
    lz = window // STRIPS
    strip = window - lz * STRIPS
    inside = dest - window * 24
    zi = inside // WLON
    longitude = strip * WLON + inside - zi * WLON
    level = (2 * lz + zi + 1) % 4
    return ones_where(source == 4 * longitude + level)


def prepare_kernel(
    table_hbm, wqkv_hbm, wproj_hbm, gain_hbm, x_hbm, g_hbm,
    main_ref, left_ref, w3_ref, w3t_ref, wproj_ref, wprojt_ref, own_ref, match_ref, gain_out,
    wide, pairs, table_ref, wqkv_ref, mine, sems,
):
    kept = pl.ds(3, 3), pl.ds(6, 30)
    moves = (
        (table_hbm, table_ref),
        (wqkv_hbm, wqkv_ref),
        (wproj_hbm, wproj_ref),
        (gain_hbm, gain_out),
        (x_hbm.at[kept], mine.at[0]),
        (g_hbm.at[kept], mine.at[1]),
    )
    copies = [pltpu.make_async_copy(a, b, sems.at[n]) for n, (a, b) in enumerate(moves)]
    for copy in copies:
        copy.start()
    for oj in range(WLON):
        match_ref[oj] = offset_match(oj, True)
    for copy in copies:
        copy.wait()
    for k in range(3):
        part = wqkv_ref[:, k * C : (k + 1) * C]
        w3_ref[k] = part
        w3t_ref[k * WIDTH : k * WIDTH + C] = part.T
        w3t_ref[k * WIDTH + C : (k + 1) * WIDTH] = jnp.zeros((WIDTH - C, C), bf16)
    wprojt_ref[...] = wproj_ref[...].T
    for a in range(3):
        for k in range(2):
            own_ref[k, a] = mine[k, a].reshape(BODY, C)
    wide[...] = jnp.zeros_like(wide)
    for h in range(HEADS):
        for lz in range(2):
            wide[lz * HEADS + h : lz * HEADS + h + 1, :TABLE] = table_ref[h, lz : lz + 1] * LOG2E
    pairs[...] = jnp.zeros_like(pairs)
    lane = iota((16, 128), 1)
    for zl_j in range(PAIRS):
        for v in range(3):
            total = jnp.zeros((16, 128), f32)
            for q in range(4):
                off = table_offset(4 * v + q, zl_j)
                base, rest = off // 128 * 128, off % 128
                width = 128 if rest + OFFSETS <= 128 else 256
                piece = wide[:, base : base + width]
                shift = (32 * q - rest) % width
                if shift:
                    piece = pltpu.roll(piece, shift, 1)
                inside = (lane >= 32 * q) & (lane < 32 * q + OFFSETS)
                total = jnp.where(inside, piece[:, :128], total)
            pairs[v, pl.ds(zl_j, TYPES, stride=16), :] = total[:TYPES]
    full = jnp.concatenate([pairs[v] for v in range(3)], axis=1)
    high = full.astype(bf16)
    rest = full - high.astype(f32)
    middle = rest.astype(bf16)
    low = (rest - middle.astype(f32)).astype(bf16)
    lane_head = iota((PAIRS, MAIN), 1) // LEFT
    for oj in range(WLON):
        match = offset_match(oj, False)
        dense = dot(high, match) + (dot(middle, match) + dot(low, match))
        for lz in range(2):
            left = jnp.zeros((PAIRS, MAIN), f32)
            for h in range(HEADS):
                t = lz * HEADS + h
                block = dense[t * 16 : t * 16 + PAIRS]
                main_ref[t, pl.ds(oj, PAIRS, stride=WLON), :] = block[:, :MAIN]
                left = jnp.where(lane_head == h, block[:, MAIN:], left)
            left_ref[lz, pl.ds(oj, PAIRS, stride=WLON), :] = left
    lat = lax.axis_index("xl") * 2 + lax.axis_index("c")
    last_band = (lat == LATS - 1).astype(jnp.int32)

    def region(token, last_level):
        upper = (token // WLON) % 2 * (2 * last_level)
        return upper + jnp.where(token >= 72, last_band, 0)

    j = iota((WIN, MAIN), 0)
    column = iota((WIN, MAIN), 1)
    for lz in range(2):
        allowed = region(column, lz) == region(j, lz)
        for h in range(HEADS):
            t = lz * HEADS + h
            main_ref[t] = jnp.where(allowed, main_ref[t], -1e30)
        allowed = region(query_index(column + MAIN), lz) == region(j, lz)
        left_ref[lz] = jnp.where(allowed, left_ref[lz], -1e30)


def in_hbm(array):
    return pltpu.with_memory_space_constraint(array, pltpu.HBM)


def prepare(table, wqkv, wproj, gain, x, g):
    vmem = pl.BlockSpec(memory_space=pltpu.VMEM)
    return pl.pallas_call(
        prepare_kernel,
        out_shape=(
            jax.ShapeDtypeStruct((TYPES, WIN, MAIN), f32),
            jax.ShapeDtypeStruct((2, WIN, MAIN), f32),
            jax.ShapeDtypeStruct((3, C, C), bf16),
            jax.ShapeDtypeStruct((3 * WIDTH, C), bf16),
            jax.ShapeDtypeStruct((C, C), bf16),
            jax.ShapeDtypeStruct((C, C), bf16),
            jax.ShapeDtypeStruct((2, 3, BODY, C), bf16),
            jax.ShapeDtypeStruct((WLON, 2 * MAIN, PAIRS * 32), bf16),
            jax.ShapeDtypeStruct((1, C), f32),
        ),
        in_specs=[pl.BlockSpec(memory_space=pltpu.HBM)] * 6,
        out_specs=(vmem,) * 9,
        scratch_shapes=[
            pltpu.VMEM((16, WIDE), f32),
            pltpu.VMEM((3, TYPES * 16, 128), f32),
            pltpu.VMEM((HEADS, 2, TABLE), f32),
            pltpu.VMEM((C, 3 * C), bf16),
            pltpu.VMEM((2, 3, 30, 4, C), bf16),
            pltpu.SemaphoreType.DMA((6,)),
        ],
        compiler_params=pltpu.CompilerParams(vmem_limit_bytes=VMEM_LIMIT),
        cost_estimate=pl.CostEstimate(
            flops=4_000_000_000, bytes_accessed=4_000_000, transcendentals=0
        ),
        name="prepare",
    )(*(in_hbm(a) for a in (table, wqkv, wproj, gain, x, g)))


def normalised(values):
    mean = jnp.mean(values, axis=-1, keepdims=True)
    centred = values - mean
    inverse = lax.rsqrt(jnp.mean(centred * centred, axis=-1, keepdims=True) + 1e-05)
    return centred * inverse, inverse


def w_place(t):
    if t < W_SLOTS * PARTS:
        return t // W_SLOTS, t % W_SLOTS
    return t - W_SLOTS * PARTS, W_SLOTS


def main_kernel(
    own_ref, lat_ref, lon_ref, corner_ref, gain_ref, w3_ref, w3t_ref, wproj_ref, wprojt_ref,
    bias_ref, left_ref, match_ref, rows_out, send_out,
    xw, gw, standard_ref, cot_ref, query_ref, key_ref, value_ref, mixed_ref, tokens_t_ref,
    qkv_t_ref, mixed_t_ref, scores_ref, grad_attend_ref, half_ref, grad_half_ref, dense, dense_left,
    wsum, psum, gsum, spread, wide, grads, stack,
):
    order = window_order(False)
    for a in range(6):
        for k, to in enumerate((xw, gw)):
            if a < 3:
                body, tail = own_ref[k, a], lon_ref[k, a].reshape(TAIL, C)
            else:
                body = lat_ref[k, a - 3].reshape(BODY, C)
                tail = corner_ref[k, a - 3].reshape(TAIL, C)
            line = dot(order[:, :BODY], body) + dot(order[:, BODY:], tail)
            for w in range(WINDOWS):
                to[w, 24 * a : 24 * a + 24, :] = line[24 * w : 24 * w + 24]
    dense[...] = jnp.zeros_like(dense)
    dense_left[...] = jnp.zeros_like(dense_left)
    gsum[...] = jnp.zeros_like(gsum)
    spread[...] = jnp.zeros_like(spread)
    gain = gain_ref[...]
    lane_head = iota((WIN, C), 1) // HEAD_DIM
    shape = (WIN, MAIN)
    repeat = ones_where((iota(shape, 0) == MAIN + iota(shape, 1) % LEFT) & (iota(shape, 1) < SHARED))
    shape = (MAIN, WIN)
    repeat_t = ones_where((iota(shape, 1) == MAIN + iota(shape, 0) % LEFT) & (iota(shape, 0) < SHARED))
    shape = (LEFT, MAIN)
    gather = ones_where((iota(shape, 0) == iota(shape, 1) % LEFT) & (iota(shape, 1) < SHARED))
    own_head_t = iota((C, MAIN), 0) // HEAD_DIM == iota((C, MAIN), 1) // LEFT
    own_head = iota((MAIN, C), 1) // HEAD_DIM == iota((MAIN, C), 0) // LEFT

    def of_head(value, h):
        return jnp.where(lane_head[: value.shape[0]] == h, value, jnp.zeros_like(value))

    def stacked(value):
        return jnp.concatenate([of_head(value, h) for h in range(HEADS)], axis=0)

    def only_head(mask, value):
        return jnp.where(mask, value, jnp.zeros_like(value)).astype(bf16)

    standard, _ = normalised(xw[...].reshape(WINDOWS * WIN, C))
    standard_ref[...] = standard
    scaled = standard * gain
    tokens = scaled.astype(bf16)
    cots = gw[...].reshape(WINDOWS * WIN, C).astype(bf16)
    cot_ref[...] = cots
    query_ref[...] = dot(tokens, w3_ref[0]).astype(bf16)
    key_ref[...] = dot(tokens, w3_ref[1]).astype(bf16)
    value_ref[...] = dot(tokens, w3_ref[2]).astype(bf16)
    mixed_ref[...] = dot(cots, wprojt_ref[...]).astype(bf16)
    for w in range(WINDOWS):
        tokens_t = scaled[w * WIN : (w + 1) * WIN].T.astype(bf16)
        tokens_t_ref[w] = tokens_t
        for k in range(3):
            part = dot(w3t_ref[k * WIDTH : k * WIDTH + C], tokens_t)
            qkv_t_ref[w, k * C : (k + 1) * C] = part.astype(bf16)
        mixed_t_ref[w] = dot(wproj_ref[...], gw[w].T.astype(bf16)).astype(bf16)

    for w in range(WINDOWS):
        lz = w // STRIPS
        span = slice(w * WIN, (w + 1) * WIN)
        query_t, mixed_t = qkv_t_ref[w, 0:C], mixed_t_ref[w]
        key, value = key_ref[span], value_ref[span]
        scores_ref[w, : HEADS * WIN] = dot(stacked(key), query_t[:, :MAIN])
        scores_ref[w, HEADS * WIN :] = dot(key, only_head(own_head_t, dot(query_t, repeat)))
        grad_attend_ref[w, : HEADS * WIN] = dot(stacked(value), mixed_t[:, :MAIN])
        grad_attend_ref[w, HEADS * WIN :] = dot(value, only_head(own_head_t, dot(mixed_t, repeat)))
        for t in range(HEADS + 1):
            lines = slice(t * WIN, (t + 1) * WIN)
            columns = slice(t * MAIN, (t + 1) * MAIN)
            bias = bias_ref[lz * HEADS + t] if t < HEADS else left_ref[lz]
            scores = scores_ref[w, lines] * (SCALE * LOG2E) + bias
            top = jnp.max(scores, axis=0, keepdims=True)
            powers = jnp.exp2(scores - top)
            attend = powers * (1.0 / jnp.sum(powers, axis=0, keepdims=True))
            half_ref[w, :, columns] = attend.astype(bf16)
            grad_attend = grad_attend_ref[w, lines]
            total = jnp.sum(attend * grad_attend, axis=0, keepdims=True)
            grad_scores = attend * (grad_attend - total)
            grad_half_ref[w, :, columns] = grad_scores.astype(bf16)
            if t < HEADS:
                dense[lz * HEADS + t] += grad_scores
            else:
                dense_left[lz] += grad_scores

    for w in range(WINDOWS):
        span = slice(w * WIN, (w + 1) * WIN)

        def per_query(left, right_ref):
            parts = []
            for h in range(0, HEADS, 2):
                two = dot(
                    left[h * HEAD_DIM : (h + 2) * HEAD_DIM],
                    right_ref[w, :, h * MAIN : (h + 2) * MAIN],
                )
                parts += [two[:HEAD_DIM, :MAIN], two[HEAD_DIM:, MAIN:]]
            shared = dot(left, right_ref[w, :, HEADS * MAIN :])
            return jnp.concatenate(parts, axis=0), jnp.where(own_head_t, shared, 0.0)

        def per_key(left_ref, right):
            parts = [of_head(right[:MAIN], h) for h in range(HEADS)]
            parts.append(only_head(own_head, dot(repeat_t, right)))
            return dot(left_ref[w], jnp.concatenate(parts, axis=0))

        cot = cot_ref[span]
        out_t, out_left = per_query(qkv_t_ref[w, 2 * C :], half_ref)
        both = jnp.concatenate([out_t.astype(bf16), out_left.astype(bf16)], axis=1)
        added = dot(both, jnp.concatenate([cot[:MAIN], dot(repeat_t, cot).astype(bf16)], axis=0))
        psum[...] = added if w == 0 else psum[...] + added
        query_grad, query_left = per_query(qkv_t_ref[w, C : 2 * C], grad_half_ref)
        first = slice(w * WIN, w * WIN + MAIN)
        last = slice(w * WIN + MAIN, (w + 1) * WIN)
        spread[first, 0:C] = (query_grad * SCALE).astype(bf16).T
        spread[last, 0:C] = dot(gather, (query_left * SCALE).astype(bf16).T).astype(bf16)
        grad_key = per_key(grad_half_ref, query_ref[span]) * SCALE
        spread[span, WIDTH : WIDTH + C] = grad_key.astype(bf16)
        spread[span, 2 * WIDTH : 2 * WIDTH + C] = per_key(half_ref, mixed_ref[span]).astype(bf16)

    grad_projected = spread[...]
    back = dot(grad_projected, w3t_ref[...]).astype(bf16)
    rows_out[...] = back
    gsum[0:1, :] = jnp.sum(back.astype(f32) * standard_ref[...], axis=0, keepdims=True)
    for w in range(WINDOWS):
        added = dot(tokens_t_ref[w], spread[w * WIN : (w + 1) * WIN])
        wsum[...] = added if w == 0 else wsum[...] + added

    total = jnp.zeros((TYPES * 16, PAIRS * 32), f32)
    lane_left = iota((PAIRS, MAIN), 1) // LEFT
    for oj in range(WLON):
        picked = []
        for lz in range(2):
            left = dense_left[lz, pl.ds(oj, PAIRS, stride=WLON), :]
            for h in range(HEADS):
                first = dense[lz * HEADS + h, pl.ds(oj, PAIRS, stride=WLON), :]
                both = jnp.concatenate([first, jnp.where(lane_left == h, left, 0.0)], axis=1)
                picked += [both, jnp.zeros((4, 2 * MAIN), f32)]
        picked = jnp.concatenate(picked, axis=0)
        high = picked.astype(bf16)
        low = (picked - high.astype(f32)).astype(bf16)
        match = match_ref[oj]
        total += dot(high, match) + dot(low, match)
    for v in range(3):
        grads[v] = total[:, 128 * v : 128 * (v + 1)]
    wide[...] = jnp.zeros_like(wide)
    lane = iota((TYPES, 256), 1)
    for zl_j in range(PAIRS):
        for v in range(3):
            four = grads[v, pl.ds(zl_j, TYPES, stride=16), :]
            for q in range(4):
                off = table_offset(4 * v + q, zl_j)
                base, rest = off // 128 * 128, off % 128
                width = 128 if rest + OFFSETS <= 128 else 256
                piece = four
                if width == 256:
                    piece = jnp.concatenate([four, jnp.zeros_like(four)], axis=1)
                shift = (rest - 32 * q) % width
                if shift:
                    piece = pltpu.roll(piece, shift, 1)
                position = lane[:, :width]
                inside = (position >= rest) & (position < rest + OFFSETS)
                target = (slice(0, TYPES), slice(base, base + width))
                wide[target] = jnp.where(inside, piece, wide[target])

    weights = jnp.concatenate(
        [wsum[:, k * WIDTH : k * WIDTH + C] for k in range(3)] + [psum[...]], axis=1
    )
    for t in range(W_TILES):
        row, column = divmod(t, 6)
        tile = weights[16 * row : 16 * row + 16, 128 * column : 128 * column + 128]
        p, slot = w_place(t)
        send_out[p, :, 128 * slot : 128 * slot + 128] = tile.astype(bf16)
    stack[...] = jnp.zeros_like(stack)
    for n in range(B_COLUMNS):
        stack[TYPES * n : TYPES * (n + 1), :] = wide[:TYPES, 128 * n : 128 * (n + 1)]
    last = slice(128 * W_SLOTS, 128 * SLOTS)
    for n in range(B_TILES):
        send_out[B_FIRST + n, :, last] = stack[16 * n : 16 * n + 16, :].astype(bf16)
    for p in range(GAIN_PART, PARTS):
        if p == GAIN_PART:
            line = gsum[0:1, :]
            gains = jnp.concatenate([line[:, :128], jnp.zeros((7, 128), f32)], axis=0)
            more = jnp.concatenate([line[:, 128:], jnp.zeros((1, 256 - C), f32)], axis=1)
            more = jnp.concatenate([more, jnp.zeros((7, 128), f32)], axis=0)
            send_out[p, :, last] = jnp.concatenate([gains, more], axis=0).astype(bf16)
        else:
            send_out[p, :, last] = jnp.zeros((16, 128), bf16)


def main(own, lat_in, lon_in, corner_in, gain, w3, w3t, wproj, wproj_t, bias, bias_left, match):
    vmem = pl.BlockSpec(memory_space=pltpu.VMEM)
    return pl.pallas_call(
        main_kernel,
        out_shape=(
            jax.ShapeDtypeStruct((WINDOWS * WIN, C), bf16),
            jax.ShapeDtypeStruct((PARTS, 16, SLOTS * 128), bf16),
        ),
        in_specs=[vmem] * 12,
        out_specs=(vmem,) * 2,
        scratch_shapes=[
            pltpu.VMEM((WINDOWS, WIN, C), f32),
            pltpu.VMEM((WINDOWS, WIN, C), f32),
            pltpu.VMEM((WINDOWS * WIN, C), f32),
            pltpu.VMEM((WINDOWS * WIN, C), bf16),
            pltpu.VMEM((WINDOWS * WIN, C), bf16),
            pltpu.VMEM((WINDOWS * WIN, C), bf16),
            pltpu.VMEM((WINDOWS * WIN, C), bf16),
            pltpu.VMEM((WINDOWS * WIN, C), bf16),
            pltpu.VMEM((WINDOWS, C, WIN), bf16),
            pltpu.VMEM((WINDOWS, 3 * C, WIN), bf16),
            pltpu.VMEM((WINDOWS, C, WIN), bf16),
            pltpu.VMEM((WINDOWS, (HEADS + 1) * WIN, MAIN), f32),
            pltpu.VMEM((WINDOWS, (HEADS + 1) * WIN, MAIN), f32),
            pltpu.VMEM((WINDOWS, WIN, (HEADS + 1) * MAIN), bf16),
            pltpu.VMEM((WINDOWS, WIN, (HEADS + 1) * MAIN), bf16),
            pltpu.VMEM((TYPES, WIN, MAIN), f32),
            pltpu.VMEM((2, WIN, MAIN), f32),
            pltpu.VMEM((C, 3 * WIDTH), f32),
            pltpu.VMEM((C, C), f32),
            pltpu.VMEM((8, C), f32),
            pltpu.VMEM((WINDOWS * WIN, 3 * WIDTH), bf16),
            pltpu.VMEM((16, WIDE), f32),
            pltpu.VMEM((3, TYPES * 16, 128), f32),
            pltpu.VMEM((B_TILES * 16, 128), f32),
        ],
        compiler_params=pltpu.CompilerParams(vmem_limit_bytes=VMEM_LIMIT),
        cost_estimate=pl.CostEstimate(
            flops=20_000_000_000, bytes_accessed=4_000_000, transcendentals=750_000
        ),
        name="window_grads",
    )(own, lat_in, lon_in, corner_in, gain, w3, w3t, wproj, wproj_t, bias, bias_left, match)


def pieces_kernel(rows_ref, body_out, tail_out):
    order_t = window_order(True)
    for a in range(6):
        line = jnp.concatenate(
            [rows_ref[WIN * w + 24 * a : WIN * w + 24 * a + 24, :] for w in range(WINDOWS)], axis=0
        )
        line = dot(order_t, line)
        body_out[a] = line[:BODY].astype(bf16)
        tail_out[a] = line[BODY:].astype(bf16)


def pieces(rows):
    vmem = pl.BlockSpec(memory_space=pltpu.VMEM)
    return pl.pallas_call(
        pieces_kernel,
        out_shape=(
            jax.ShapeDtypeStruct((6, BODY, C), bf16),
            jax.ShapeDtypeStruct((6, TAIL, C), bf16),
        ),
        in_specs=[vmem],
        out_specs=(vmem,) * 2,
        compiler_params=pltpu.CompilerParams(vmem_limit_bytes=VMEM_LIMIT),
        cost_estimate=pl.CostEstimate(
            flops=500_000_000, bytes_accessed=700_000, transcendentals=0
        ),
        name="pieces",
    )(rows)


def norm_kernel(x_ref, g_ref, gain_ref, body_ref, tail_ref, lat_ref, out_ref):
    gain = gain_ref[...]
    for a in range(6):
        if a < 3:
            grad = lat_ref[a].astype(f32)
        else:
            grad = [tail_ref[a - 3].astype(f32), body_ref[a - 3].astype(f32)]
            grad = jnp.concatenate(grad, axis=0)
        standard, inverse = normalised(x_ref[a].reshape(WIN, C).astype(f32))
        scaled = grad * gain
        local = inverse * (
            scaled
            - jnp.mean(scaled, axis=-1, keepdims=True)
            - standard * jnp.mean(scaled * standard, axis=-1, keepdims=True)
        )
        total = (g_ref[a].reshape(WIN, C).astype(f32) + local).astype(bf16)
        out_ref[a] = total.reshape(36, 4, C)


def norm_grads(x, g, gain, body, tail, lat_in):
    vmem = pl.BlockSpec(memory_space=pltpu.VMEM)
    return pl.pallas_call(
        norm_kernel,
        out_shape=jax.ShapeDtypeStruct(x.shape, bf16),
        in_specs=[vmem] * 6,
        out_specs=vmem,
        compiler_params=pltpu.CompilerParams(vmem_limit_bytes=VMEM_LIMIT),
        cost_estimate=pl.CostEstimate(
            flops=10_000_000, bytes_accessed=1_500_000, transcendentals=1000
        ),
        name="norm_grads",
    )(x, g, gain, body, tail, lat_in)


def unpack_kernel(parts_ref, gain_out, wqkv_out, wproj_out, bias_out, stack):
    last = slice(128 * W_SLOTS, 128 * SLOTS)
    gains = parts_ref[GAIN_PART, :, last].astype(f32)
    gain_out[:, :128] = gains[0:1]
    gain_out[:, 128:] = gains[8:9, : C - 128]

    def tile(t):
        p, slot = w_place(t)
        return parts_ref[p, :, 128 * slot : 128 * slot + 128].astype(f32)

    for row in range(C // 16):
        lines = slice(16 * row, 16 * row + 16)
        for column in range(4):
            wqkv_out[lines, 128 * column : 128 * column + 128] = tile(6 * row + column)
        mixed = tile(6 * row + 4)
        wqkv_out[lines, 512:] = mixed[:, :64]
        wproj_out[lines, :] = jnp.concatenate([mixed[:, 64:], tile(6 * row + 5)], axis=1)
    for n in range(B_TILES):
        stack[16 * n : 16 * n + 16, :] = parts_ref[B_FIRST + n, :, last].astype(f32)
    for n in range(B_COLUMNS):
        width = min(128, TABLE - 128 * n)
        for h in range(HEADS):
            for lz in range(2):
                t = TYPES * n + lz * HEADS + h
                bias_out[h, lz : lz + 1, 128 * n : 128 * n + width] = stack[t : t + 1, :width]


def unpack(parts):
    vmem = pl.BlockSpec(memory_space=pltpu.VMEM)
    return pl.pallas_call(
        unpack_kernel,
        out_shape=(
            jax.ShapeDtypeStruct((1, C), f32),
            jax.ShapeDtypeStruct((C, 3 * C), f32),
            jax.ShapeDtypeStruct((C, C), f32),
            jax.ShapeDtypeStruct((HEADS, 2, TABLE), f32),
        ),
        in_specs=[vmem],
        out_specs=(vmem,) * 4,
        scratch_shapes=[pltpu.VMEM((B_TILES * 16, 128), f32)],
        compiler_params=pltpu.CompilerParams(vmem_limit_bytes=VMEM_LIMIT),
        name="unpack",
    )(parts)


def scattered(send):
    got = lax.all_to_all(send, GROUP, 0, 0, tiled=True)
    got = got.reshape((PARTS // LATS, LATS, 16, SLOTS * 128)).astype(f32)
    shared = jnp.sum(got[..., : 128 * W_SLOTS], axis=(0, 1))
    last = jnp.sum(got[..., 128 * W_SLOTS :], axis=0)
    return jnp.concatenate([shared] + [last[n] for n in range(LATS)], axis=1).astype(bf16)


def exchanged(mixed):
    count = lax.axis_size(REST)
    got = lax.all_to_all(
        jnp.broadcast_to(mixed[None], (count,) + mixed.shape), REST, 0, 0, tiled=True
    )
    total = jnp.sum(got.astype(f32), axis=0)
    shared = total[:, : 128 * W_SLOTS]
    last = [total[:, 128 * (W_SLOTS + n) : 128 * (W_SLOTS + n + 1)] for n in range(LATS)]
    everywhere = last[0] + last[1] + last[2] + last[3]
    part = lax.axis_index(GROUP)
    per_lat = (part >= B_FIRST) & (part < GAIN_PART)
    rows = [
        jnp.concatenate([shared, jnp.where(per_lat, last[n], everywhere)], axis=1).astype(bf16)
        for n in range(LATS)
    ]
    spread = jnp.broadcast_to(jnp.stack(rows)[None], (PARTS // LATS, LATS, 16, SLOTS * 128))
    return spread.reshape(PARTS, 16, SLOTS * 128)


def pack_kernel(x_ref, g_ref, corner_out, lon_out, lat_out, sems):
    copies = []
    for k, ref in enumerate((x_ref, g_ref)):
        for n, (source, to) in enumerate(
            (
                (ref.at[pl.ds(0, 3), pl.ds(0, 6)], corner_out),
                (ref.at[pl.ds(3, 3), pl.ds(0, 6)], lon_out),
                (ref.at[pl.ds(0, 3), pl.ds(6, 30)], lat_out),
            )
        ):
            copies.append(pltpu.make_async_copy(source, to.at[k], sems.at[3 * k + n]))
    for copy in copies:
        copy.start()
    for copy in copies:
        copy.wait()


def pack(x, g):
    vmem = pl.BlockSpec(memory_space=pltpu.VMEM)
    return pl.pallas_call(
        pack_kernel,
        out_shape=(
            jax.ShapeDtypeStruct((2, 3, 6, 4, C), bf16),
            jax.ShapeDtypeStruct((2, 3, 6, 4, C), bf16),
            jax.ShapeDtypeStruct((2, 3, 30, 4, C), bf16),
        ),
        in_specs=[pl.BlockSpec(memory_space=pltpu.HBM)] * 2,
        out_specs=(vmem,) * 3,
        scratch_shapes=[pltpu.SemaphoreType.DMA((6,))],
        compiler_params=pltpu.CompilerParams(vmem_limit_bytes=VMEM_LIMIT),
        name="pack",
    )(in_hbm(x), in_hbm(g))


def on_device(x, g, ln_gain, w_qkv, w_proj, bias_table):
    lon_axes, lat_axes = ("z", "y", "xh"), ("xl", "c")
    both = lon_axes + lat_axes
    lons, lats = lax.axis_size(lon_axes), lax.axis_size(lat_axes)
    lon_swap = [(i, i ^ 1) for i in range(lons)]
    lat_down = [(i, (i - 1) % lats) for i in range(lats)]
    lat_up = [(i, (i + 1) % lats) for i in range(lats)]
    corner_down = [(i * lats + a, (i ^ 1) * lats + b) for i in range(lons) for a, b in lat_down]

    x, g = x.transpose(1, 2, 0, 3), g.transpose(1, 2, 0, 3)
    to_corner, to_lon, to_lat = pack(x, g)
    corner_in = lax.ppermute(to_corner, both, corner_down)
    lon_in = lax.ppermute(to_lon, lon_axes, lon_swap)
    lat_in = lax.ppermute(to_lat, lat_axes, lat_down)
    bias, bias_left, w3, w3t, wproj, wproj_t, own, match, gain = prepare(
        bias_table[0].transpose(1, 0, 2), w_qkv, w_proj, ln_gain.reshape(1, C), x, g
    )
    rows, send = main(
        own, lat_in, lon_in, corner_in, gain, w3, w3t, wproj, wproj_t, bias, bias_left, match
    )
    body, tail = pieces(rows)
    tail = lax.ppermute(tail, lon_axes, lon_swap)
    mixed, tail = lax.optimization_barrier((scattered(send), tail))
    lat_rows = lax.ppermute(jnp.concatenate([tail[3:], body[3:]], axis=1), lat_axes, lat_up)
    spread, lat_rows = lax.optimization_barrier((exchanged(mixed), lat_rows))
    parts = lax.all_to_all(spread, GROUP, 0, 0, tiled=True)
    grad_gain, grad_wqkv, grad_wproj, grad_bias = unpack(parts)
    grad_x = norm_grads(x, g, gain, body, tail, lat_rows)
    grad_x = grad_x.transpose(2, 0, 1, 3)
    grad_bias = grad_bias.transpose(1, 0, 2)[None]
    return grad_x, grad_gain.reshape(C), grad_wqkv, grad_wproj, grad_bias


def solution(mesh):
    shape = (mesh.shape["lon"] // 8, 4, 2, 2, 2)
    split = Mesh(mesh.devices.reshape(shape), ("z", "y", "xh", "xl", "c"))
    tokens = P(None, ("xl", "c"), ("z", "y", "xh"), None)
    table = P(("xl", "c"), None, None, None)
    return jax.shard_map(
        on_device,
        mesh=split,
        in_specs=(tokens, tokens, P(), P(), P(), table),
        out_specs=(tokens, P(), P(), P(), table),
        check_vma=False,
    )
```

```python
import functools

import jax
import jax.numpy as jnp
from jax import lax
from jax.experimental import pallas as pl
from jax.experimental.pallas import tpu as pltpu
from jax.sharding import Mesh, PartitionSpec as P

C = 192
HEADS = 6
HEAD_DIM = 32
WLON = 12
WIN = 144
TABLE = 3312
PAIRS = 12
OFFSETS = 23
LOG2E = 1.4426950408889634
SCALE = HEAD_DIM**-0.5
BODY = 120
TAIL = 24
MAIN = 128
LEFT = 16
SHARED = HEADS * LEFT
STRIPS = 3
WINDOWS = 6
TYPES = 12
GROUP = ("y", "xh", "xl", "c")
REST = "z"
PARTS = 32
SLOTS = 3
W_TILES = 72
W_SLOTS = 2
B_COLUMNS = 26
B_TILES = 20
B_FIRST = 8
GAIN_PART = B_FIRST + B_TILES
WIDTH = 256
LATS = 4
WIDE = 3584
f32 = jnp.float32
bf16 = jnp.bfloat16
VMEM_LIMIT = 40 * 1024 * 1024

NN = (((1,), (0,)), ((), ()))
TN = (((0,), (0,)), ((), ()))


def dot(a, b, dims=NN):
    return lax.dot_general(a, b, dims, preferred_element_type=f32)


def table_offset(zl_i, zl_j):
    li, zi = divmod(zl_i, 2)
    lj, zj = divmod(zl_j, 2)
    return (((zi * 2 + zj) * 6 + li) * 6 + lj) * OFFSETS


def iota(shape, dim):
    return lax.broadcasted_iota(jnp.int32, shape, dim)


def ones_where(condition):
    return jnp.where(condition, 1.0, 0.0).astype(bf16)


def query_index(column):
    return jnp.where(column < MAIN, column, MAIN + column % LEFT)


def offset_match(oj, transposed):
    shape = (2 * MAIN, PAIRS * 32) if transposed else (PAIRS * 32, 2 * MAIN)
    row, col = iota(shape, 1 if transposed else 0), iota(shape, 0 if transposed else 1)
    token = query_index(col)
    zl = token // WLON
    target = zl * 32 + (oj + 11) - (token - zl * WLON)
    return ones_where((row == target) & (col < MAIN + SHARED))


def window_order(transposed):
    dest, source = iota((WIN, WIN), 1 if transposed else 0), iota((WIN, WIN), 0 if transposed else 1)
    window = dest // 24
    lz = window // STRIPS
    strip = window - lz * STRIPS
    inside = dest - window * 24
    zi = inside // WLON
    longitude = strip * WLON + inside - zi * WLON
    level = (2 * lz + zi + 1) % 4
    return ones_where(source == 4 * longitude + level)


def prepare_kernel(
    table_hbm, wqkv_hbm, wproj_hbm, gain_hbm, x_hbm, g_hbm,
    main_ref, left_ref, w3_ref, w3t_ref, wprojt_ref, own_ref, match_ref, gain_out,
    wide, pairs, table_ref, wqkv_ref, wproj_ref, mine, sems,
):
    kept = pl.ds(3, 3), pl.ds(6, 30)
    moves = (
        (table_hbm, table_ref),
        (wqkv_hbm, wqkv_ref),
        (wproj_hbm, wproj_ref),
        (gain_hbm, gain_out),
        (x_hbm.at[kept], mine.at[0]),
        (g_hbm.at[kept], mine.at[1]),
    )
    copies = [pltpu.make_async_copy(a, b, sems.at[n]) for n, (a, b) in enumerate(moves)]
    for copy in copies:
        copy.start()
    for oj in range(WLON):
        match_ref[oj] = offset_match(oj, True)
    for copy in copies:
        copy.wait()
    for k in range(3):
        part = wqkv_ref[:, k * C : (k + 1) * C]
        w3_ref[k] = part
        w3t_ref[k * WIDTH : k * WIDTH + C] = part.T
        w3t_ref[k * WIDTH + C : (k + 1) * WIDTH] = jnp.zeros((WIDTH - C, C), bf16)
    wprojt_ref[...] = wproj_ref[...].T
    for a in range(3):
        for k in range(2):
            own_ref[k, a] = mine[k, a].reshape(BODY, C)
    wide[...] = jnp.zeros_like(wide)
    for h in range(HEADS):
        for lz in range(2):
            wide[lz * HEADS + h : lz * HEADS + h + 1, :TABLE] = table_ref[h, lz : lz + 1] * LOG2E
    pairs[...] = jnp.zeros_like(pairs)
    lane = iota((16, 128), 1)
    for zl_j in range(PAIRS):
        for v in range(3):
            total = jnp.zeros((16, 128), f32)
            for q in range(4):
                off = table_offset(4 * v + q, zl_j)
                base, rest = off // 128 * 128, off % 128
                width = 128 if rest + OFFSETS <= 128 else 256
                piece = wide[:, base : base + width]
                shift = (32 * q - rest) % width
                if shift:
                    piece = pltpu.roll(piece, shift, 1)
                inside = (lane >= 32 * q) & (lane < 32 * q + OFFSETS)
                total = jnp.where(inside, piece[:, :128], total)
            pairs[v, pl.ds(zl_j, TYPES, stride=16), :] = total[:TYPES]
    full = jnp.concatenate([pairs[v] for v in range(3)], axis=1)
    high = full.astype(bf16)
    rest = full - high.astype(f32)
    middle = rest.astype(bf16)
    low = (rest - middle.astype(f32)).astype(bf16)
    lane_head = iota((PAIRS, MAIN), 1) // LEFT
    for oj in range(WLON):
        match = offset_match(oj, False)
        dense = dot(high, match) + (dot(middle, match) + dot(low, match))
        for lz in range(2):
            left = jnp.zeros((PAIRS, MAIN), f32)
            for h in range(HEADS):
                t = lz * HEADS + h
                block = dense[t * 16 : t * 16 + PAIRS]
                main_ref[t, pl.ds(oj, PAIRS, stride=WLON), :] = block[:, :MAIN]
                left = jnp.where(lane_head == h, block[:, MAIN:], left)
            left_ref[lz, pl.ds(oj, PAIRS, stride=WLON), :] = left
    lat = lax.axis_index("xl") * 2 + lax.axis_index("c")
    last_band = (lat == LATS - 1).astype(jnp.int32)

    def region(token, last_level):
        upper = (token // WLON) % 2 * (2 * last_level)
        return upper + jnp.where(token >= 72, last_band, 0)

    j = iota((WIN, MAIN), 0)
    column = iota((WIN, MAIN), 1)
    for lz in range(2):
        allowed = region(column, lz) == region(j, lz)
        for h in range(HEADS):
            t = lz * HEADS + h
            main_ref[t] = jnp.where(allowed, main_ref[t], -1e30)
        allowed = region(query_index(column + MAIN), lz) == region(j, lz)
        left_ref[lz] = jnp.where(allowed, left_ref[lz], -1e30)


def in_hbm(array):
    return pltpu.with_memory_space_constraint(array, pltpu.HBM)


def prepare(table, wqkv, wproj, gain, x, g):
    vmem = pl.BlockSpec(memory_space=pltpu.VMEM)
    return pl.pallas_call(
        prepare_kernel,
        out_shape=(
            jax.ShapeDtypeStruct((TYPES, WIN, MAIN), f32),
            jax.ShapeDtypeStruct((2, WIN, MAIN), f32),
            jax.ShapeDtypeStruct((3, C, C), bf16),
            jax.ShapeDtypeStruct((3 * WIDTH, C), bf16),
            jax.ShapeDtypeStruct((C, C), bf16),
            jax.ShapeDtypeStruct((2, 3, BODY, C), bf16),
            jax.ShapeDtypeStruct((WLON, 2 * MAIN, PAIRS * 32), bf16),
            jax.ShapeDtypeStruct((1, C), f32),
        ),
        in_specs=[pl.BlockSpec(memory_space=pltpu.HBM)] * 6,
        out_specs=(vmem,) * 8,
        scratch_shapes=[
            pltpu.VMEM((16, WIDE), f32),
            pltpu.VMEM((3, TYPES * 16, 128), f32),
            pltpu.VMEM((HEADS, 2, TABLE), f32),
            pltpu.VMEM((C, 3 * C), bf16),
            pltpu.VMEM((C, C), bf16),
            pltpu.VMEM((2, 3, 30, 4, C), bf16),
            pltpu.SemaphoreType.DMA((6,)),
        ],
        compiler_params=pltpu.CompilerParams(vmem_limit_bytes=VMEM_LIMIT),
        cost_estimate=pl.CostEstimate(
            flops=4_000_000_000, bytes_accessed=4_000_000, transcendentals=0
        ),
        name="prepare",
    )(*(in_hbm(a) for a in (table, wqkv, wproj, gain, x, g)))


def normalised(values):
    mean = jnp.mean(values, axis=-1, keepdims=True)
    centred = values - mean
    inverse = lax.rsqrt(jnp.mean(centred * centred, axis=-1, keepdims=True) + 1e-05)
    return centred * inverse, inverse


def w_place(t):
    if t < W_SLOTS * PARTS:
        return t // W_SLOTS, t % W_SLOTS
    return t - W_SLOTS * PARTS, W_SLOTS


def main_kernel(
    own_ref, lat_ref, lon_ref, corner_ref, gain_ref, w3_ref, w3t_ref, wprojt_ref,
    bias_ref, left_ref, match_ref, rows_out, send_out,
    xw, gw, standard_ref, cot_ref, query_ref, key_ref, value_ref, mixed_ref, tokens_ref,
    qkv_t_ref, mixed_t_ref, scores_ref, grad_attend_ref, half_ref, grad_half_ref, dense, dense_left,
    wsum, psum, gsum, spread, outputs_ref, cots_ref, wide, grads, stack,
):
    order = window_order(False)
    for a in range(6):
        for k, to in enumerate((xw, gw)):
            if a < 3:
                body, tail = own_ref[k, a], lon_ref[k, a].reshape(TAIL, C)
            else:
                body = lat_ref[k, a - 3].reshape(BODY, C)
                tail = corner_ref[k, a - 3].reshape(TAIL, C)
            line = dot(order[:, :BODY], body) + dot(order[:, BODY:], tail)
            for w in range(WINDOWS):
                to[w, 24 * a : 24 * a + 24, :] = line[24 * w : 24 * w + 24]
    dense[...] = jnp.zeros_like(dense)
    dense_left[...] = jnp.zeros_like(dense_left)
    gsum[...] = jnp.zeros_like(gsum)
    spread[...] = jnp.zeros_like(spread)
    gain = gain_ref[...]
    lane_head = iota((WIN, C), 1) // HEAD_DIM
    shape = (WIN, MAIN)
    repeat = ones_where((iota(shape, 0) == MAIN + iota(shape, 1) % LEFT) & (iota(shape, 1) < SHARED))
    shape = (LEFT, MAIN)
    gather = ones_where((iota(shape, 0) == iota(shape, 1) % LEFT) & (iota(shape, 1) < SHARED))
    own_head_t = iota((C, MAIN), 0) // HEAD_DIM == iota((C, MAIN), 1) // LEFT
    own_head = iota((MAIN, C), 1) // HEAD_DIM == iota((MAIN, C), 0) // LEFT

    def of_head(value, h):
        return jnp.where(lane_head[: value.shape[0]] == h, value, jnp.zeros_like(value))

    def per_head(columns, left):
        blocks = []
        for h in range(HEADS):
            above = jnp.zeros((h * HEAD_DIM, MAIN), bf16)
            below = jnp.zeros((C - (h + 1) * HEAD_DIM, MAIN), bf16)
            own = columns[h * HEAD_DIM : (h + 1) * HEAD_DIM, :MAIN]
            blocks.append(jnp.concatenate([x for x in (above, own, below) if x.shape[0]], axis=0))
        return jnp.concatenate(blocks + [only_head(own_head_t, left)], axis=1)

    def repeated(rows):
        zeros = jnp.zeros((MAIN - SHARED, C), bf16)
        return jnp.concatenate([rows[MAIN:]] * HEADS + [zeros], axis=0)

    def only_head(mask, value):
        return jnp.where(mask, value, jnp.zeros_like(value)).astype(bf16)

    standard, _ = normalised(xw[...].reshape(WINDOWS * WIN, C))
    standard_ref[...] = standard
    tokens = (standard * gain).astype(bf16)
    tokens_ref[...] = tokens
    cots = gw[...].reshape(WINDOWS * WIN, C).astype(bf16)
    cot_ref[...] = cots
    query_ref[...] = dot(tokens, w3_ref[0]).astype(bf16)
    key_ref[...] = dot(tokens, w3_ref[1]).astype(bf16)
    value_ref[...] = dot(tokens, w3_ref[2]).astype(bf16)
    mixed_ref[...] = dot(cots, wprojt_ref[...]).astype(bf16)
    for w in range(WINDOWS):
        span = slice(w * WIN, (w + 1) * WIN)
        for k, ref in enumerate((query_ref, key_ref, value_ref)):
            qkv_t_ref[w, k * C : (k + 1) * C] = ref[span].T
        mixed_t_ref[w] = mixed_ref[span].T

    for w in range(WINDOWS):
        lz = w // STRIPS
        span = slice(w * WIN, (w + 1) * WIN)
        query_t, mixed_t = qkv_t_ref[w, 0:C], mixed_t_ref[w]
        key, value = key_ref[span], value_ref[span]
        scores_ref[w] = dot(key, per_head(query_t, dot(query_t, repeat)))
        grad_attend_ref[w] = dot(value, per_head(mixed_t, dot(mixed_t, repeat)))
        for t in range(HEADS + 1):
            columns = slice(t * MAIN, (t + 1) * MAIN)
            bias = bias_ref[lz * HEADS + t] if t < HEADS else left_ref[lz]
            scores = scores_ref[w, :, columns] * (SCALE * LOG2E) + bias
            top = jnp.max(scores, axis=0, keepdims=True)
            powers = jnp.exp2(scores - top)
            attend = powers * (1.0 / jnp.sum(powers, axis=0, keepdims=True))
            half_ref[w, :, columns] = attend.astype(bf16)
            grad_attend = grad_attend_ref[w, :, columns]
            total = jnp.sum(attend * grad_attend, axis=0, keepdims=True)
            grad_scores = attend * (grad_attend - total)
            grad_half_ref[w, :, columns] = grad_scores.astype(bf16)
            if t < HEADS:
                dense[lz * HEADS + t] += grad_scores
            else:
                dense_left[lz] += grad_scores

    for w in range(WINDOWS):
        span = slice(w * WIN, (w + 1) * WIN)

        def per_query(left, right_ref):
            parts = []
            for h in range(0, HEADS, 2):
                two = dot(
                    left[h * HEAD_DIM : (h + 2) * HEAD_DIM],
                    right_ref[w, :, h * MAIN : (h + 2) * MAIN],
                )
                parts += [two[:HEAD_DIM, :MAIN], two[HEAD_DIM:, MAIN:]]
            shared = dot(left, right_ref[w, :, HEADS * MAIN :])
            return jnp.concatenate(parts, axis=0), jnp.where(own_head_t, shared, 0.0)

        def per_key(left_ref, right):
            parts = [of_head(right[:MAIN], h) for h in range(HEADS)]
            parts.append(only_head(own_head, repeated(right)))
            return dot(left_ref[w], jnp.concatenate(parts, axis=0))

        cot = cot_ref[span]
        out_t, out_left = per_query(qkv_t_ref[w, 2 * C :], half_ref)
        outputs_ref[:, 2 * w * MAIN : (2 * w + 1) * MAIN] = out_t.astype(bf16)
        outputs_ref[:, (2 * w + 1) * MAIN : 2 * (w + 1) * MAIN] = out_left.astype(bf16)
        cots_ref[2 * w * MAIN : (2 * w + 1) * MAIN] = cot[:MAIN]
        cots_ref[(2 * w + 1) * MAIN : 2 * (w + 1) * MAIN] = repeated(cot)
        query_grad, query_left = per_query(qkv_t_ref[w, C : 2 * C], grad_half_ref)
        first = slice(w * WIN, w * WIN + MAIN)
        last = slice(w * WIN + MAIN, (w + 1) * WIN)
        spread[first, 0:C] = (query_grad * SCALE).astype(bf16).T
        spread[last, 0:C] = dot(gather, (query_left * SCALE).astype(bf16).T).astype(bf16)
        grad_key = per_key(grad_half_ref, query_ref[span]) * SCALE
        spread[span, WIDTH : WIDTH + C] = grad_key.astype(bf16)
        spread[span, 2 * WIDTH : 2 * WIDTH + C] = per_key(half_ref, mixed_ref[span]).astype(bf16)

    grad_projected = spread[...]
    back = dot(grad_projected, w3t_ref[...]).astype(bf16)
    rows_out[...] = back
    gsum[0:1, :] = jnp.sum(back.astype(f32) * standard_ref[...], axis=0, keepdims=True)
    wsum[...] = dot(tokens_ref[...], grad_projected, TN)
    psum[...] = dot(outputs_ref[...], cots_ref[...])

    total = jnp.zeros((TYPES * 16, PAIRS * 32), f32)
    lane_left = iota((PAIRS, MAIN), 1) // LEFT
    for oj in range(WLON):
        picked = []
        for lz in range(2):
            left = dense_left[lz, pl.ds(oj, PAIRS, stride=WLON), :]
            for h in range(HEADS):
                first = dense[lz * HEADS + h, pl.ds(oj, PAIRS, stride=WLON), :]
                both = jnp.concatenate([first, jnp.where(lane_left == h, left, 0.0)], axis=1)
                picked += [both, jnp.zeros((4, 2 * MAIN), f32)]
        picked = jnp.concatenate(picked, axis=0)
        high = picked.astype(bf16)
        match = match_ref[oj]
        total += dot(high, match)
    for v in range(3):
        grads[v] = total[:, 128 * v : 128 * (v + 1)]
    wide[...] = jnp.zeros_like(wide)
    lane = iota((TYPES, 256), 1)
    for zl_j in range(PAIRS):
        for v in range(3):
            four = grads[v, pl.ds(zl_j, TYPES, stride=16), :]
            for q in range(4):
                off = table_offset(4 * v + q, zl_j)
                base, rest = off // 128 * 128, off % 128
                width = 128 if rest + OFFSETS <= 128 else 256
                piece = four
                if width == 256:
                    piece = jnp.concatenate([four, jnp.zeros_like(four)], axis=1)
                shift = (rest - 32 * q) % width
                if shift:
                    piece = pltpu.roll(piece, shift, 1)
                position = lane[:, :width]
                inside = (position >= rest) & (position < rest + OFFSETS)
                target = (slice(0, TYPES), slice(base, base + width))
                wide[target] = jnp.where(inside, piece, wide[target])

    weights = jnp.concatenate(
        [wsum[:, k * WIDTH : k * WIDTH + C] for k in range(3)] + [psum[...]], axis=1
    )
    for t in range(W_TILES):
        row, column = divmod(t, 6)
        tile = weights[16 * row : 16 * row + 16, 128 * column : 128 * column + 128]
        p, slot = w_place(t)
        send_out[p, :, 128 * slot : 128 * slot + 128] = tile.astype(bf16)
    stack[...] = jnp.zeros_like(stack)
    for n in range(B_COLUMNS):
        stack[TYPES * n : TYPES * (n + 1), :] = wide[:TYPES, 128 * n : 128 * (n + 1)]
    last = slice(128 * W_SLOTS, 128 * SLOTS)
    for n in range(B_TILES):
        send_out[B_FIRST + n, :, last] = stack[16 * n : 16 * n + 16, :].astype(bf16)
    for p in range(GAIN_PART, PARTS):
        if p == GAIN_PART:
            line = gsum[0:1, :]
            gains = jnp.concatenate([line[:, :128], jnp.zeros((7, 128), f32)], axis=0)
            more = jnp.concatenate([line[:, 128:], jnp.zeros((1, 256 - C), f32)], axis=1)
            more = jnp.concatenate([more, jnp.zeros((7, 128), f32)], axis=0)
            send_out[p, :, last] = jnp.concatenate([gains, more], axis=0).astype(bf16)
        else:
            send_out[p, :, last] = jnp.zeros((16, 128), bf16)


def main(own, lat_in, lon_in, corner_in, gain, w3, w3t, wproj_t, bias, bias_left, match):
    vmem = pl.BlockSpec(memory_space=pltpu.VMEM)
    return pl.pallas_call(
        main_kernel,
        out_shape=(
            jax.ShapeDtypeStruct((WINDOWS * WIN, C), bf16),
            jax.ShapeDtypeStruct((PARTS, 16, SLOTS * 128), bf16),
        ),
        in_specs=[vmem] * 11,
        out_specs=(vmem,) * 2,
        scratch_shapes=[
            pltpu.VMEM((WINDOWS, WIN, C), f32),
            pltpu.VMEM((WINDOWS, WIN, C), f32),
            pltpu.VMEM((WINDOWS * WIN, C), f32),
            pltpu.VMEM((WINDOWS * WIN, C), bf16),
            pltpu.VMEM((WINDOWS * WIN, C), bf16),
            pltpu.VMEM((WINDOWS * WIN, C), bf16),
            pltpu.VMEM((WINDOWS * WIN, C), bf16),
            pltpu.VMEM((WINDOWS * WIN, C), bf16),
            pltpu.VMEM((WINDOWS * WIN, C), bf16),
            pltpu.VMEM((WINDOWS, 3 * C, WIN), bf16),
            pltpu.VMEM((WINDOWS, C, WIN), bf16),
            pltpu.VMEM((WINDOWS, WIN, (HEADS + 1) * MAIN), f32),
            pltpu.VMEM((WINDOWS, WIN, (HEADS + 1) * MAIN), f32),
            pltpu.VMEM((WINDOWS, WIN, (HEADS + 1) * MAIN), bf16),
            pltpu.VMEM((WINDOWS, WIN, (HEADS + 1) * MAIN), bf16),
            pltpu.VMEM((TYPES, WIN, MAIN), f32),
            pltpu.VMEM((2, WIN, MAIN), f32),
            pltpu.VMEM((C, 3 * WIDTH), f32),
            pltpu.VMEM((C, C), f32),
            pltpu.VMEM((8, C), f32),
            pltpu.VMEM((WINDOWS * WIN, 3 * WIDTH), bf16),
            pltpu.VMEM((C, 2 * WINDOWS * MAIN), bf16),
            pltpu.VMEM((2 * WINDOWS * MAIN, C), bf16),
            pltpu.VMEM((16, WIDE), f32),
            pltpu.VMEM((3, TYPES * 16, 128), f32),
            pltpu.VMEM((B_TILES * 16, 128), f32),
        ],
        compiler_params=pltpu.CompilerParams(vmem_limit_bytes=VMEM_LIMIT),
        cost_estimate=pl.CostEstimate(
            flops=20_000_000_000, bytes_accessed=4_000_000, transcendentals=750_000
        ),
        name="window_grads",
    )(own, lat_in, lon_in, corner_in, gain, w3, w3t, wproj_t, bias, bias_left, match)


def pieces_kernel(rows_ref, body_out, tail_out):
    order_t = window_order(True)
    for a in range(6):
        line = jnp.concatenate(
            [rows_ref[WIN * w + 24 * a : WIN * w + 24 * a + 24, :] for w in range(WINDOWS)], axis=0
        )
        line = dot(order_t, line)
        body_out[a] = line[:BODY].astype(bf16)
        tail_out[a] = line[BODY:].astype(bf16)


def pieces(rows):
    vmem = pl.BlockSpec(memory_space=pltpu.VMEM)
    return pl.pallas_call(
        pieces_kernel,
        out_shape=(
            jax.ShapeDtypeStruct((6, BODY, C), bf16),
            jax.ShapeDtypeStruct((6, TAIL, C), bf16),
        ),
        in_specs=[vmem],
        out_specs=(vmem,) * 2,
        compiler_params=pltpu.CompilerParams(vmem_limit_bytes=VMEM_LIMIT),
        cost_estimate=pl.CostEstimate(
            flops=500_000_000, bytes_accessed=700_000, transcendentals=0
        ),
        name="pieces",
    )(rows)


def norm_kernel(x_ref, g_ref, gain_ref, body_ref, tail_ref, lat_ref, out_ref):
    gain = gain_ref[...]
    for a in range(6):
        if a < 3:
            grad = lat_ref[a].astype(f32)
        else:
            grad = [tail_ref[a - 3].astype(f32), body_ref[a - 3].astype(f32)]
            grad = jnp.concatenate(grad, axis=0)
        standard, inverse = normalised(x_ref[a].reshape(WIN, C).astype(f32))
        scaled = grad * gain
        local = inverse * (
            scaled
            - jnp.mean(scaled, axis=-1, keepdims=True)
            - standard * jnp.mean(scaled * standard, axis=-1, keepdims=True)
        )
        total = (g_ref[a].reshape(WIN, C).astype(f32) + local).astype(bf16)
        out_ref[a] = total.reshape(36, 4, C)


def norm_grads(x, g, gain, body, tail, lat_in):
    vmem = pl.BlockSpec(memory_space=pltpu.VMEM)
    return pl.pallas_call(
        norm_kernel,
        out_shape=jax.ShapeDtypeStruct(x.shape, bf16),
        in_specs=[vmem] * 6,
        out_specs=vmem,
        compiler_params=pltpu.CompilerParams(vmem_limit_bytes=VMEM_LIMIT),
        cost_estimate=pl.CostEstimate(
            flops=10_000_000, bytes_accessed=1_500_000, transcendentals=1000
        ),
        name="norm_grads",
    )(x, g, gain, body, tail, lat_in)


def unpack_kernel(parts_ref, gain_out, wqkv_out, wproj_out, bias_out, stack):
    last = slice(128 * W_SLOTS, 128 * SLOTS)
    gains = parts_ref[GAIN_PART, :, last].astype(f32)
    gain_out[:, :128] = gains[0:1]
    gain_out[:, 128:] = gains[8:9, : C - 128]

    def tile(t):
        p, slot = w_place(t)
        return parts_ref[p, :, 128 * slot : 128 * slot + 128].astype(f32)

    for row in range(C // 16):
        lines = slice(16 * row, 16 * row + 16)
        for column in range(4):
            wqkv_out[lines, 128 * column : 128 * column + 128] = tile(6 * row + column)
        mixed = tile(6 * row + 4)
        wqkv_out[lines, 512:] = mixed[:, :64]
        wproj_out[lines, :] = jnp.concatenate([mixed[:, 64:], tile(6 * row + 5)], axis=1)
    for n in range(B_TILES):
        stack[16 * n : 16 * n + 16, :] = parts_ref[B_FIRST + n, :, last].astype(f32)
    for n in range(B_COLUMNS):
        width = min(128, TABLE - 128 * n)
        for h in range(HEADS):
            for lz in range(2):
                t = TYPES * n + lz * HEADS + h
                bias_out[h, lz : lz + 1, 128 * n : 128 * n + width] = stack[t : t + 1, :width]


def unpack(parts):
    vmem = pl.BlockSpec(memory_space=pltpu.VMEM)
    return pl.pallas_call(
        unpack_kernel,
        out_shape=(
            jax.ShapeDtypeStruct((1, C), f32),
            jax.ShapeDtypeStruct((C, 3 * C), f32),
            jax.ShapeDtypeStruct((C, C), f32),
            jax.ShapeDtypeStruct((HEADS, 2, TABLE), f32),
        ),
        in_specs=[vmem],
        out_specs=(vmem,) * 4,
        scratch_shapes=[pltpu.VMEM((B_TILES * 16, 128), f32)],
        compiler_params=pltpu.CompilerParams(vmem_limit_bytes=VMEM_LIMIT),
        name="unpack",
    )(parts)


def fold_kernel(got_ref, out_ref):
    shared = jnp.zeros((16, 128 * W_SLOTS), f32)
    last = [jnp.zeros((16, 128), f32)] * LATS
    for p in range(PARTS):
        shared += got_ref[p, :, : 128 * W_SLOTS].astype(f32)
        last[p % LATS] += got_ref[p, :, 128 * W_SLOTS :].astype(f32)
    total = jnp.concatenate([shared] + last, axis=1).astype(bf16)
    for n in range(out_ref.shape[0]):
        out_ref[n] = total


def share_kernel(got_ref, out_ref):
    total = jnp.zeros(got_ref.shape[1:], f32)
    for n in range(got_ref.shape[0]):
        total += got_ref[n].astype(f32)
    shared = total[:, : 128 * W_SLOTS].astype(bf16)
    last = [total[:, 128 * (W_SLOTS + n) : 128 * (W_SLOTS + n + 1)] for n in range(LATS)]
    everywhere = last[0] + last[1] + last[2] + last[3]
    part = lax.axis_index(GROUP)
    per_lat = (part >= B_FIRST) & (part < GAIN_PART)
    last = [jnp.where(per_lat, one, everywhere).astype(bf16) for one in last]
    for p in range(PARTS):
        out_ref[p, :, : 128 * W_SLOTS] = shared
        out_ref[p, :, 128 * W_SLOTS :] = last[p % LATS]


def on_chip(kernel, shape, name):
    vmem = pl.BlockSpec(memory_space=pltpu.VMEM)
    return pl.pallas_call(
        kernel,
        out_shape=jax.ShapeDtypeStruct(shape, bf16),
        in_specs=[vmem],
        out_specs=vmem,
        compiler_params=pltpu.CompilerParams(vmem_limit_bytes=VMEM_LIMIT),
        cost_estimate=pl.CostEstimate(flops=1_000_000, bytes_accessed=600_000, transcendentals=0),
        name=name,
    )


def pack_kernel(x_ref, g_ref, corner_out, lon_out, lat_out, sems):
    copies = []
    for k, ref in enumerate((x_ref, g_ref)):
        for n, (source, to) in enumerate(
            (
                (ref.at[pl.ds(0, 3), pl.ds(0, 6)], corner_out),
                (ref.at[pl.ds(3, 3), pl.ds(0, 6)], lon_out),
                (ref.at[pl.ds(0, 3), pl.ds(6, 30)], lat_out),
            )
        ):
            copies.append(pltpu.make_async_copy(source, to.at[k], sems.at[3 * k + n]))
    for copy in copies:
        copy.start()
    for copy in copies:
        copy.wait()


def pack(x, g):
    vmem = pl.BlockSpec(memory_space=pltpu.VMEM)
    return pl.pallas_call(
        pack_kernel,
        out_shape=(
            jax.ShapeDtypeStruct((2, 3, 6, 4, C), bf16),
            jax.ShapeDtypeStruct((2, 3, 6, 4, C), bf16),
            jax.ShapeDtypeStruct((2, 3, 30, 4, C), bf16),
        ),
        in_specs=[pl.BlockSpec(memory_space=pltpu.HBM)] * 2,
        out_specs=(vmem,) * 3,
        scratch_shapes=[pltpu.SemaphoreType.DMA((6,))],
        compiler_params=pltpu.CompilerParams(vmem_limit_bytes=VMEM_LIMIT),
        name="pack",
    )(in_hbm(x), in_hbm(g))


def on_device(x, g, ln_gain, w_qkv, w_proj, bias_table):
    lon_axes, lat_axes = ("z", "y", "xh"), ("xl", "c")
    both = lon_axes + lat_axes
    lons, lats = lax.axis_size(lon_axes), lax.axis_size(lat_axes)
    lon_swap = [(i, i ^ 1) for i in range(lons)]
    lat_down = [(i, (i - 1) % lats) for i in range(lats)]
    lat_up = [(i, (i + 1) % lats) for i in range(lats)]
    corner_down = [(i * lats + a, (i ^ 1) * lats + b) for i in range(lons) for a, b in lat_down]

    x, g = x.transpose(1, 2, 0, 3), g.transpose(1, 2, 0, 3)
    to_corner, to_lon, to_lat = pack(x, g)
    corner_in = lax.ppermute(to_corner, both, corner_down)
    lon_in = lax.ppermute(to_lon, lon_axes, lon_swap)
    lat_in = lax.ppermute(to_lat, lat_axes, lat_down)
    bias, bias_left, w3, w3t, wproj_t, own, match, gain = prepare(
        bias_table[0].transpose(1, 0, 2), w_qkv, w_proj, ln_gain.reshape(1, C), x, g
    )
    rows, send = main(
        own, lat_in, lon_in, corner_in, gain, w3, w3t, wproj_t, bias, bias_left, match
    )
    body, tail = pieces(rows)
    tail = lax.ppermute(tail, lon_axes, lon_swap)
    got = lax.all_to_all(send, GROUP, 0, 0, tiled=True)
    mixed = on_chip(fold_kernel, (lax.axis_size(REST), 16, 128 * (W_SLOTS + LATS)), "fold")(got)
    mixed, tail = lax.optimization_barrier((mixed, tail))
    lat_rows = lax.ppermute(jnp.concatenate([tail[3:], body[3:]], axis=1), lat_axes, lat_up)
    got = lax.all_to_all(mixed, REST, 0, 0, tiled=True)
    spread = on_chip(share_kernel, send.shape, "share")(got)
    spread, lat_rows = lax.optimization_barrier((spread, lat_rows))
    parts = lax.all_to_all(spread, GROUP, 0, 0, tiled=True)
    grad_gain, grad_wqkv, grad_wproj, grad_bias = unpack(parts)
    grad_x = norm_grads(x, g, gain, body, tail, lat_rows)
    grad_x = grad_x.transpose(2, 0, 1, 3)
    grad_bias = grad_bias.transpose(1, 0, 2)[None]
    return grad_x, grad_gain.reshape(C), grad_wqkv, grad_wproj, grad_bias


def solution(mesh):
    shape = (mesh.shape["lon"] // 8, 4, 2, 2, 2)
    split = Mesh(mesh.devices.reshape(shape), ("z", "y", "xh", "xl", "c"))
    tokens = P(None, ("xl", "c"), ("z", "y", "xh"), None)
    table = P(("xl", "c"), None, None, None)
    return jax.shard_map(
        on_device,
        mesh=split,
        in_specs=(tokens, tokens, P(), P(), P(), table),
        out_specs=(tokens, P(), P(), P(), table),
        check_vma=False,
    )
```

```python
import functools

import jax
import jax.numpy as jnp
from jax import lax
from jax.experimental import pallas as pl
from jax.experimental.pallas import tpu as pltpu
from jax.sharding import Mesh, PartitionSpec as P

C = 192
HEADS = 6
HEAD_DIM = 32
WLON = 12
WIN = 144
TABLE = 3312
PAIRS = 12
OFFSETS = 23
LOG2E = 1.4426950408889634
SCALE = HEAD_DIM**-0.5
BODY = 120
TAIL = 24
MAIN = 128
LEFT = 16
SHARED = HEADS * LEFT
STRIPS = 3
WINDOWS = 6
TYPES = 12
GROUP = ("y", "xh", "xl", "c")
REST = "z"
PARTS = 32
SLOTS = 3
W_TILES = 72
W_SLOTS = 2
B_COLUMNS = 26
B_TILES = 20
B_FIRST = 8
GAIN_PART = B_FIRST + B_TILES
WIDTH = 256
LATS = 4
WIDE = 3584
f32 = jnp.float32
bf16 = jnp.bfloat16
VMEM_LIMIT = 40 * 1024 * 1024

NN = (((1,), (0,)), ((), ()))
TN = (((0,), (0,)), ((), ()))


def dot(a, b, dims=NN):
    return lax.dot_general(a, b, dims, preferred_element_type=f32)


def table_offset(zl_i, zl_j):
    li, zi = divmod(zl_i, 2)
    lj, zj = divmod(zl_j, 2)
    return (((zi * 2 + zj) * 6 + li) * 6 + lj) * OFFSETS


def iota(shape, dim):
    return lax.broadcasted_iota(jnp.int32, shape, dim)


def ones_where(condition):
    return jnp.where(condition, 1.0, 0.0).astype(bf16)


def query_index(column):
    return jnp.where(column < MAIN, column, MAIN + column % LEFT)


def offset_match(oj, transposed):
    shape = (2 * MAIN, PAIRS * 32) if transposed else (PAIRS * 32, 2 * MAIN)
    row, col = iota(shape, 1 if transposed else 0), iota(shape, 0 if transposed else 1)
    token = query_index(col)
    zl = token // WLON
    target = zl * 32 + (oj + 11) - (token - zl * WLON)
    return ones_where((row == target) & (col < MAIN + SHARED))


def window_order(transposed):
    dest, source = iota((WIN, WIN), 1 if transposed else 0), iota((WIN, WIN), 0 if transposed else 1)
    window = dest // 24
    lz = window // STRIPS
    strip = window - lz * STRIPS
    inside = dest - window * 24
    zi = inside // WLON
    longitude = strip * WLON + inside - zi * WLON
    level = (2 * lz + zi + 1) % 4
    return ones_where(source == 4 * longitude + level)


def prepare_kernel(
    table_hbm, wqkv_hbm, wproj_hbm, gain_hbm, x_hbm, g_hbm,
    main_ref, left_ref, w3_ref, w3t_ref, wprojt_ref, own_ref, match_ref, gain_out,
    wide, pairs, table_ref, wqkv_ref, wproj_ref, mine, sems,
):
    kept = pl.ds(3, 3), pl.ds(6, 30)
    moves = (
        (table_hbm, table_ref),
        (wqkv_hbm, wqkv_ref),
        (wproj_hbm, wproj_ref),
        (gain_hbm, gain_out),
        (x_hbm.at[kept], mine.at[0]),
        (g_hbm.at[kept], mine.at[1]),
    )
    copies = [pltpu.make_async_copy(a, b, sems.at[n]) for n, (a, b) in enumerate(moves)]
    for copy in copies:
        copy.start()
    for oj in range(WLON):
        match_ref[oj] = offset_match(oj, True)
    for copy in copies:
        copy.wait()
    for k in range(3):
        part = wqkv_ref[:, k * C : (k + 1) * C]
        w3_ref[k] = part
        w3t_ref[k * WIDTH : k * WIDTH + C] = part.T
        w3t_ref[k * WIDTH + C : (k + 1) * WIDTH] = jnp.zeros((WIDTH - C, C), bf16)
    wprojt_ref[...] = wproj_ref[...].T
    for a in range(3):
        own_ref[a] = side_by_side(mine, a)
    wide[...] = jnp.zeros_like(wide)
    for h in range(HEADS):
        for lz in range(2):
            wide[lz * HEADS + h : lz * HEADS + h + 1, :TABLE] = table_ref[h, lz : lz + 1] * LOG2E
    pairs[...] = jnp.zeros_like(pairs)
    lane = iota((16, 128), 1)
    for zl_j in range(PAIRS):
        for v in range(3):
            total = jnp.zeros((16, 128), f32)
            for q in range(4):
                off = table_offset(4 * v + q, zl_j)
                base, rest = off // 128 * 128, off % 128
                width = 128 if rest + OFFSETS <= 128 else 256
                piece = wide[:, base : base + width]
                shift = (32 * q - rest) % width
                if shift:
                    piece = pltpu.roll(piece, shift, 1)
                inside = (lane >= 32 * q) & (lane < 32 * q + OFFSETS)
                total = jnp.where(inside, piece[:, :128], total)
            pairs[v, pl.ds(zl_j, TYPES, stride=16), :] = total[:TYPES]
    full = jnp.concatenate([pairs[v] for v in range(3)], axis=1)
    high = full.astype(bf16)
    rest = full - high.astype(f32)
    middle = rest.astype(bf16)
    low = (rest - middle.astype(f32)).astype(bf16)
    lane_head = iota((PAIRS, MAIN), 1) // LEFT
    for oj in range(WLON):
        match = offset_match(oj, False)
        dense = dot(high, match) + (dot(middle, match) + dot(low, match))
        for lz in range(2):
            left = jnp.zeros((PAIRS, MAIN), f32)
            for h in range(HEADS):
                t = lz * HEADS + h
                block = dense[t * 16 : t * 16 + PAIRS]
                main_ref[t, pl.ds(oj, PAIRS, stride=WLON), :] = block[:, :MAIN]
                left = jnp.where(lane_head == h, block[:, MAIN:], left)
            left_ref[lz, pl.ds(oj, PAIRS, stride=WLON), :] = left
    lat = lax.axis_index("xl") * 2 + lax.axis_index("c")
    last_band = (lat == LATS - 1).astype(jnp.int32)

    def region(token, last_level):
        upper = (token // WLON) % 2 * (2 * last_level)
        return upper + jnp.where(token >= 72, last_band, 0)

    j = iota((WIN, MAIN), 0)
    column = iota((WIN, MAIN), 1)
    for lz in range(2):
        allowed = region(column, lz) == region(j, lz)
        for h in range(HEADS):
            t = lz * HEADS + h
            main_ref[t] = jnp.where(allowed, main_ref[t], -1e30)
        allowed = region(query_index(column + MAIN), lz) == region(j, lz)
        left_ref[lz] = jnp.where(allowed, left_ref[lz], -1e30)


def in_hbm(array):
    return pltpu.with_memory_space_constraint(array, pltpu.HBM)


def prepare(table, wqkv, wproj, gain, x, g):
    vmem = pl.BlockSpec(memory_space=pltpu.VMEM)
    return pl.pallas_call(
        prepare_kernel,
        out_shape=(
            jax.ShapeDtypeStruct((TYPES, WIN, MAIN), f32),
            jax.ShapeDtypeStruct((2, WIN, MAIN), f32),
            jax.ShapeDtypeStruct((3, C, C), bf16),
            jax.ShapeDtypeStruct((3 * WIDTH, C), bf16),
            jax.ShapeDtypeStruct((C, C), bf16),
            jax.ShapeDtypeStruct((3, BODY, 2 * C), bf16),
            jax.ShapeDtypeStruct((WLON, 2 * MAIN, PAIRS * 32), bf16),
            jax.ShapeDtypeStruct((1, C), f32),
        ),
        in_specs=[pl.BlockSpec(memory_space=pltpu.HBM)] * 6,
        out_specs=(vmem,) * 8,
        scratch_shapes=[
            pltpu.VMEM((16, WIDE), f32),
            pltpu.VMEM((3, TYPES * 16, 128), f32),
            pltpu.VMEM((HEADS, 2, TABLE), f32),
            pltpu.VMEM((C, 3 * C), bf16),
            pltpu.VMEM((C, C), bf16),
            pltpu.VMEM((2, 3, 30, 4, C), bf16),
            pltpu.SemaphoreType.DMA((6,)),
        ],
        compiler_params=pltpu.CompilerParams(vmem_limit_bytes=VMEM_LIMIT),
        cost_estimate=pl.CostEstimate(
            flops=4_000_000_000, bytes_accessed=4_000_000, transcendentals=0
        ),
        name="prepare",
    )(*(in_hbm(a) for a in (table, wqkv, wproj, gain, x, g)))


def normalised(values):
    mean = jnp.mean(values, axis=-1, keepdims=True)
    centred = values - mean
    inverse = lax.rsqrt(jnp.mean(centred * centred, axis=-1, keepdims=True) + 1e-05)
    return centred * inverse, inverse


def w_place(t):
    if t < W_SLOTS * PARTS:
        return t // W_SLOTS, t % W_SLOTS
    return t - W_SLOTS * PARTS, W_SLOTS


def main_kernel(
    own_ref, lat_ref, lon_ref, corner_ref, gain_ref, w3_ref, w3t_ref, wprojt_ref,
    bias_ref, left_ref, match_ref, rows_out, send_hbm,
    xw, gw, standard_ref, cot_ref, query_ref, key_ref, value_ref, mixed_ref, tokens_ref,
    qkv_t_ref, mixed_t_ref, scores_ref, grad_attend_ref, half_ref, grad_half_ref, dense, dense_left,
    wsum, psum, gsum, spread, outputs_ref, cots_ref, wide, grads, stack,
    send_shared, send_last, sems,
):
    order = window_order(False)
    for a in range(6):
        body, tail = (own_ref[a], lon_ref[a]) if a < 3 else (lat_ref[a - 3], corner_ref[a - 3])
        line = dot(order[:, :BODY], body) + dot(order[:, BODY:], tail)
        for w in range(WINDOWS):
            xw[w, 24 * a : 24 * a + 24, :] = line[24 * w : 24 * w + 24, :C]
            gw[w, 24 * a : 24 * a + 24, :] = line[24 * w : 24 * w + 24, C:]
    dense[...] = jnp.zeros_like(dense)
    dense_left[...] = jnp.zeros_like(dense_left)
    gsum[...] = jnp.zeros_like(gsum)
    spread[...] = jnp.zeros_like(spread)
    gain = gain_ref[...]
    lane_head = iota((WIN, C), 1) // HEAD_DIM
    shape = (WIN, MAIN)
    repeat = ones_where((iota(shape, 0) == MAIN + iota(shape, 1) % LEFT) & (iota(shape, 1) < SHARED))
    shape = (LEFT, MAIN)
    gather = ones_where((iota(shape, 0) == iota(shape, 1) % LEFT) & (iota(shape, 1) < SHARED))
    own_head_t = iota((C, MAIN), 0) // HEAD_DIM == iota((C, MAIN), 1) // LEFT
    own_head = iota((MAIN, C), 1) // HEAD_DIM == iota((MAIN, C), 0) // LEFT

    def of_head(value, h):
        return jnp.where(lane_head[: value.shape[0]] == h, value, jnp.zeros_like(value))

    def per_head(columns, left):
        blocks = []
        for h in range(HEADS):
            above = jnp.zeros((h * HEAD_DIM, MAIN), bf16)
            below = jnp.zeros((C - (h + 1) * HEAD_DIM, MAIN), bf16)
            own = columns[h * HEAD_DIM : (h + 1) * HEAD_DIM, :MAIN]
            blocks.append(jnp.concatenate([x for x in (above, own, below) if x.shape[0]], axis=0))
        return jnp.concatenate(blocks + [only_head(own_head_t, left)], axis=1)

    def repeated(rows):
        zeros = jnp.zeros((MAIN - SHARED, C), bf16)
        return jnp.concatenate([rows[MAIN:]] * HEADS + [zeros], axis=0)

    def only_head(mask, value):
        return jnp.where(mask, value, jnp.zeros_like(value)).astype(bf16)

    standard, _ = normalised(xw[...].reshape(WINDOWS * WIN, C))
    standard_ref[...] = standard
    tokens = (standard * gain).astype(bf16)
    tokens_ref[...] = tokens
    cots = gw[...].reshape(WINDOWS * WIN, C).astype(bf16)
    cot_ref[...] = cots
    query_ref[...] = dot(tokens, w3_ref[0]).astype(bf16)
    key_ref[...] = dot(tokens, w3_ref[1]).astype(bf16)
    value_ref[...] = dot(tokens, w3_ref[2]).astype(bf16)
    mixed_ref[...] = dot(cots, wprojt_ref[...]).astype(bf16)
    for w in range(WINDOWS):
        span = slice(w * WIN, (w + 1) * WIN)
        for k, ref in enumerate((query_ref, key_ref, value_ref)):
            qkv_t_ref[w, k * C : (k + 1) * C] = ref[span].T
        mixed_t_ref[w] = mixed_ref[span].T

    for w in range(WINDOWS):
        lz = w // STRIPS
        span = slice(w * WIN, (w + 1) * WIN)
        query_t, mixed_t = qkv_t_ref[w, 0:C], mixed_t_ref[w]
        key, value = key_ref[span], value_ref[span]
        scores_ref[w] = dot(key, per_head(query_t, dot(query_t, repeat)))
        grad_attend_ref[w] = dot(value, per_head(mixed_t, dot(mixed_t, repeat)))
        for t in range(HEADS + 1):
            columns = slice(t * MAIN, (t + 1) * MAIN)
            bias = bias_ref[lz * HEADS + t] if t < HEADS else left_ref[lz]
            scores = scores_ref[w, :, columns] * (SCALE * LOG2E) + bias
            top = jnp.max(scores, axis=0, keepdims=True)
            powers = jnp.exp2(scores - top)
            attend = powers * (1.0 / jnp.sum(powers, axis=0, keepdims=True))
            half_ref[w, :, columns] = attend.astype(bf16)
            grad_attend = grad_attend_ref[w, :, columns]
            total = jnp.sum(attend * grad_attend, axis=0, keepdims=True)
            grad_scores = attend * (grad_attend - total)
            grad_half_ref[w, :, columns] = grad_scores.astype(bf16)
            if t < HEADS:
                dense[lz * HEADS + t] += grad_scores
            else:
                dense_left[lz] += grad_scores

    for w in range(WINDOWS):
        span = slice(w * WIN, (w + 1) * WIN)

        def per_query(left, right_ref):
            parts = []
            for h in range(0, HEADS, 2):
                two = dot(
                    left[h * HEAD_DIM : (h + 2) * HEAD_DIM],
                    right_ref[w, :, h * MAIN : (h + 2) * MAIN],
                )
                parts += [two[:HEAD_DIM, :MAIN], two[HEAD_DIM:, MAIN:]]
            shared = dot(left, right_ref[w, :, HEADS * MAIN :])
            return jnp.concatenate(parts, axis=0), jnp.where(own_head_t, shared, 0.0)

        def per_key(left_ref, right):
            parts = [of_head(right[:MAIN], h) for h in range(HEADS)]
            parts.append(only_head(own_head, repeated(right)))
            return dot(left_ref[w], jnp.concatenate(parts, axis=0))

        cot = cot_ref[span]
        out_t, out_left = per_query(qkv_t_ref[w, 2 * C :], half_ref)
        outputs_ref[:, 2 * w * MAIN : (2 * w + 1) * MAIN] = out_t.astype(bf16)
        outputs_ref[:, (2 * w + 1) * MAIN : 2 * (w + 1) * MAIN] = out_left.astype(bf16)
        cots_ref[2 * w * MAIN : (2 * w + 1) * MAIN] = cot[:MAIN]
        cots_ref[(2 * w + 1) * MAIN : 2 * (w + 1) * MAIN] = repeated(cot)
        query_grad, query_left = per_query(qkv_t_ref[w, C : 2 * C], grad_half_ref)
        first = slice(w * WIN, w * WIN + MAIN)
        last = slice(w * WIN + MAIN, (w + 1) * WIN)
        spread[first, 0:C] = (query_grad * SCALE).astype(bf16).T
        spread[last, 0:C] = dot(gather, (query_left * SCALE).astype(bf16).T).astype(bf16)
        grad_key = per_key(grad_half_ref, query_ref[span]) * SCALE
        spread[span, WIDTH : WIDTH + C] = grad_key.astype(bf16)
        spread[span, 2 * WIDTH : 2 * WIDTH + C] = per_key(half_ref, mixed_ref[span]).astype(bf16)

    grad_projected = spread[...]
    back = dot(grad_projected, w3t_ref[...]).astype(bf16)
    rows_out[...] = back
    gsum[0:1, :] = jnp.sum(back.astype(f32) * standard_ref[...], axis=0, keepdims=True)
    wsum[...] = dot(tokens_ref[...], grad_projected, TN)
    psum[...] = dot(outputs_ref[...], cots_ref[...])

    weights = jnp.concatenate(
        [wsum[:, k * WIDTH : k * WIDTH + C] for k in range(3)] + [psum[...]], axis=1
    )
    for t in range(W_TILES):
        row, column = divmod(t, 6)
        tile = weights[16 * row : 16 * row + 16, 128 * column : 128 * column + 128]
        p, slot = w_place(t)
        if slot < W_SLOTS:
            send_shared[p, :, 128 * slot : 128 * slot + 128] = tile.astype(bf16)
        else:
            send_last[p] = tile.astype(bf16)
    shared_copy = pltpu.make_async_copy(
        send_shared, send_hbm.at[:, :, pl.ds(0, 128 * W_SLOTS)], sems.at[0]
    )
    shared_copy.start()

    total = jnp.zeros((TYPES * 16, PAIRS * 32), f32)
    lane_left = iota((PAIRS, MAIN), 1) // LEFT
    for oj in range(WLON):
        picked = []
        for lz in range(2):
            left = dense_left[lz, pl.ds(oj, PAIRS, stride=WLON), :]
            for h in range(HEADS):
                first = dense[lz * HEADS + h, pl.ds(oj, PAIRS, stride=WLON), :]
                both = jnp.concatenate([first, jnp.where(lane_left == h, left, 0.0)], axis=1)
                picked += [both, jnp.zeros((4, 2 * MAIN), f32)]
        picked = jnp.concatenate(picked, axis=0)
        high = picked.astype(bf16)
        match = match_ref[oj]
        total += dot(high, match)
    for v in range(3):
        grads[v] = total[:, 128 * v : 128 * (v + 1)]
    wide[...] = jnp.zeros_like(wide)
    lane = iota((TYPES, 256), 1)
    for zl_j in range(PAIRS):
        for v in range(3):
            four = grads[v, pl.ds(zl_j, TYPES, stride=16), :]
            for q in range(4):
                off = table_offset(4 * v + q, zl_j)
                base, rest = off // 128 * 128, off % 128
                width = 128 if rest + OFFSETS <= 128 else 256
                piece = four
                if width == 256:
                    piece = jnp.concatenate([four, jnp.zeros_like(four)], axis=1)
                shift = (rest - 32 * q) % width
                if shift:
                    piece = pltpu.roll(piece, shift, 1)
                position = lane[:, :width]
                inside = (position >= rest) & (position < rest + OFFSETS)
                target = (slice(0, TYPES), slice(base, base + width))
                wide[target] = jnp.where(inside, piece, wide[target])

    stack[...] = jnp.zeros_like(stack)
    for n in range(B_COLUMNS):
        stack[TYPES * n : TYPES * (n + 1), :] = wide[:TYPES, 128 * n : 128 * (n + 1)]
    for n in range(B_TILES):
        send_last[B_FIRST + n] = stack[16 * n : 16 * n + 16, :].astype(bf16)
    for p in range(GAIN_PART, PARTS):
        if p == GAIN_PART:
            line = gsum[0:1, :]
            gains = jnp.concatenate([line[:, :128], jnp.zeros((7, 128), f32)], axis=0)
            more = jnp.concatenate([line[:, 128:], jnp.zeros((1, 256 - C), f32)], axis=1)
            more = jnp.concatenate([more, jnp.zeros((7, 128), f32)], axis=0)
            send_last[p] = jnp.concatenate([gains, more], axis=0).astype(bf16)
        else:
            send_last[p] = jnp.zeros((16, 128), bf16)
    second = pltpu.make_async_copy(
        send_last, send_hbm.at[:, :, pl.ds(128 * W_SLOTS, 128)], sems.at[1]
    )
    second.start()
    shared_copy.wait()
    second.wait()


def main(own, lat_in, lon_in, corner_in, gain, w3, w3t, wproj_t, bias, bias_left, match):
    vmem = pl.BlockSpec(memory_space=pltpu.VMEM)
    return pl.pallas_call(
        main_kernel,
        out_shape=(
            jax.ShapeDtypeStruct((WINDOWS * WIN, C), bf16),
            jax.ShapeDtypeStruct((PARTS, 16, SLOTS * 128), bf16),
        ),
        in_specs=[vmem] * 11,
        out_specs=(vmem, pl.BlockSpec(memory_space=pltpu.HBM)),
        scratch_shapes=[
            pltpu.VMEM((WINDOWS, WIN, C), f32),
            pltpu.VMEM((WINDOWS, WIN, C), f32),
            pltpu.VMEM((WINDOWS * WIN, C), f32),
            pltpu.VMEM((WINDOWS * WIN, C), bf16),
            pltpu.VMEM((WINDOWS * WIN, C), bf16),
            pltpu.VMEM((WINDOWS * WIN, C), bf16),
            pltpu.VMEM((WINDOWS * WIN, C), bf16),
            pltpu.VMEM((WINDOWS * WIN, C), bf16),
            pltpu.VMEM((WINDOWS * WIN, C), bf16),
            pltpu.VMEM((WINDOWS, 3 * C, WIN), bf16),
            pltpu.VMEM((WINDOWS, C, WIN), bf16),
            pltpu.VMEM((WINDOWS, WIN, (HEADS + 1) * MAIN), f32),
            pltpu.VMEM((WINDOWS, WIN, (HEADS + 1) * MAIN), f32),
            pltpu.VMEM((WINDOWS, WIN, (HEADS + 1) * MAIN), bf16),
            pltpu.VMEM((WINDOWS, WIN, (HEADS + 1) * MAIN), bf16),
            pltpu.VMEM((TYPES, WIN, MAIN), f32),
            pltpu.VMEM((2, WIN, MAIN), f32),
            pltpu.VMEM((C, 3 * WIDTH), f32),
            pltpu.VMEM((C, C), f32),
            pltpu.VMEM((8, C), f32),
            pltpu.VMEM((WINDOWS * WIN, 3 * WIDTH), bf16),
            pltpu.VMEM((C, 2 * WINDOWS * MAIN), bf16),
            pltpu.VMEM((2 * WINDOWS * MAIN, C), bf16),
            pltpu.VMEM((16, WIDE), f32),
            pltpu.VMEM((3, TYPES * 16, 128), f32),
            pltpu.VMEM((B_TILES * 16, 128), f32),
            pltpu.VMEM((PARTS, 16, 128 * W_SLOTS), bf16),
            pltpu.VMEM((PARTS, 16, 128), bf16),
            pltpu.SemaphoreType.DMA((2,)),
        ],
        compiler_params=pltpu.CompilerParams(vmem_limit_bytes=VMEM_LIMIT),
        cost_estimate=pl.CostEstimate(
            flops=20_000_000_000, bytes_accessed=4_000_000, transcendentals=750_000
        ),
        name="window_grads",
    )(own, lat_in, lon_in, corner_in, gain, w3, w3t, wproj_t, bias, bias_left, match)


def pieces_kernel(rows_ref, own_out, lat_out, lon_out, corner_out):
    order_t = window_order(True)
    for a in range(6):
        line = jnp.concatenate(
            [rows_ref[WIN * w + 24 * a : WIN * w + 24 * a + 24, :] for w in range(WINDOWS)], axis=0
        )
        line = dot(order_t, line)
        body, tail = line[:BODY].astype(bf16), line[BODY:].astype(bf16)
        if a < 3:
            own_out[a], lon_out[a] = body, tail
        else:
            lat_out[a - 3], corner_out[a - 3] = body, tail


def pieces(rows):
    vmem = pl.BlockSpec(memory_space=pltpu.VMEM)
    return pl.pallas_call(
        pieces_kernel,
        out_shape=(
            jax.ShapeDtypeStruct((3, BODY, C), bf16),
            jax.ShapeDtypeStruct((3, BODY, C), bf16),
            jax.ShapeDtypeStruct((3, TAIL, C), bf16),
            jax.ShapeDtypeStruct((3, TAIL, C), bf16),
        ),
        in_specs=[vmem],
        out_specs=(vmem,) * 4,
        compiler_params=pltpu.CompilerParams(vmem_limit_bytes=VMEM_LIMIT),
        cost_estimate=pl.CostEstimate(
            flops=500_000_000, bytes_accessed=700_000, transcendentals=0
        ),
        name="pieces",
    )(rows)


def norm_kernel(x_ref, g_ref, gain_ref, own_ref, lat_ref, lon_ref, corner_ref, out_ref):
    gain = gain_ref[...]
    for a in range(6):
        if a < 3:
            head, body = corner_ref[a], lat_ref[a]
        else:
            head, body = lon_ref[a - 3], own_ref[a - 3]
        grad = jnp.concatenate([head.astype(f32), body.astype(f32)], axis=0)
        standard, inverse = normalised(x_ref[a].reshape(WIN, C).astype(f32))
        scaled = grad * gain
        local = inverse * (
            scaled
            - jnp.mean(scaled, axis=-1, keepdims=True)
            - standard * jnp.mean(scaled * standard, axis=-1, keepdims=True)
        )
        total = (g_ref[a].reshape(WIN, C).astype(f32) + local).astype(bf16)
        out_ref[a] = total.reshape(36, 4, C)


def norm_grads(x, g, gain, own, lat_in, lon_in, corner_in):
    vmem = pl.BlockSpec(memory_space=pltpu.VMEM)
    return pl.pallas_call(
        norm_kernel,
        out_shape=jax.ShapeDtypeStruct(x.shape, bf16),
        in_specs=[vmem] * 7,
        out_specs=vmem,
        compiler_params=pltpu.CompilerParams(vmem_limit_bytes=VMEM_LIMIT),
        cost_estimate=pl.CostEstimate(
            flops=10_000_000, bytes_accessed=1_500_000, transcendentals=1000
        ),
        name="norm_grads",
    )(x, g, gain, own, lat_in, lon_in, corner_in)


def unpack_kernel(parts_ref, gain_out, wqkv_out, wproj_out, bias_out, stack):
    last = slice(128 * W_SLOTS, 128 * SLOTS)
    gains = parts_ref[GAIN_PART, :, last].astype(f32)
    gain_out[:, :128] = gains[0:1]
    gain_out[:, 128:] = gains[8:9, : C - 128]

    def tile(t):
        p, slot = w_place(t)
        return parts_ref[p, :, 128 * slot : 128 * slot + 128].astype(f32)

    for row in range(C // 16):
        lines = slice(16 * row, 16 * row + 16)
        for column in range(4):
            wqkv_out[lines, 128 * column : 128 * column + 128] = tile(6 * row + column)
        mixed = tile(6 * row + 4)
        wqkv_out[lines, 512:] = mixed[:, :64]
        wproj_out[lines, :] = jnp.concatenate([mixed[:, 64:], tile(6 * row + 5)], axis=1)
    for n in range(B_TILES):
        stack[16 * n : 16 * n + 16, :] = parts_ref[B_FIRST + n, :, last].astype(f32)
    for n in range(B_COLUMNS):
        width = min(128, TABLE - 128 * n)
        for h in range(HEADS):
            for lz in range(2):
                t = TYPES * n + lz * HEADS + h
                bias_out[h, lz : lz + 1, 128 * n : 128 * n + width] = stack[t : t + 1, :width]


def unpack(parts):
    vmem = pl.BlockSpec(memory_space=pltpu.VMEM)
    return pl.pallas_call(
        unpack_kernel,
        out_shape=(
            jax.ShapeDtypeStruct((1, C), f32),
            jax.ShapeDtypeStruct((C, 3 * C), f32),
            jax.ShapeDtypeStruct((C, C), f32),
            jax.ShapeDtypeStruct((HEADS, 2, TABLE), f32),
        ),
        in_specs=[vmem],
        out_specs=(vmem,) * 4,
        scratch_shapes=[pltpu.VMEM((B_TILES * 16, 128), f32)],
        compiler_params=pltpu.CompilerParams(vmem_limit_bytes=VMEM_LIMIT),
        name="unpack",
    )(parts)


def fold_kernel(got_ref, out_ref):
    shared = jnp.zeros((16, 128 * W_SLOTS), f32)
    last = [jnp.zeros((16, 128), f32)] * LATS
    for p in range(PARTS):
        shared += got_ref[p, :, : 128 * W_SLOTS].astype(f32)
        last[LATS - 1 - p % LATS] += got_ref[p, :, 128 * W_SLOTS :].astype(f32)
    total = jnp.concatenate([shared] + last, axis=1).astype(bf16)
    for n in range(out_ref.shape[0]):
        out_ref[n] = total


def share_kernel(got_ref, out_ref):
    total = jnp.zeros(got_ref.shape[1:], f32)
    for n in range(got_ref.shape[0]):
        total += got_ref[n].astype(f32)
    shared = total[:, : 128 * W_SLOTS].astype(bf16)
    last = [total[:, 128 * (W_SLOTS + n) : 128 * (W_SLOTS + n + 1)] for n in range(LATS)]
    everywhere = last[0] + last[1] + last[2] + last[3]
    part = PARTS - 1 - lax.axis_index(GROUP)
    per_lat = (part >= B_FIRST) & (part < GAIN_PART)
    last = [jnp.where(per_lat, one, everywhere).astype(bf16) for one in last]
    for p in range(PARTS):
        out_ref[p, :, : 128 * W_SLOTS] = shared
        out_ref[p, :, 128 * W_SLOTS :] = last[LATS - 1 - p % LATS]


def on_chip(kernel, shape, name):
    vmem = pl.BlockSpec(memory_space=pltpu.VMEM)
    return pl.pallas_call(
        kernel,
        out_shape=jax.ShapeDtypeStruct(shape, bf16),
        in_specs=[vmem],
        out_specs=vmem,
        compiler_params=pltpu.CompilerParams(vmem_limit_bytes=VMEM_LIMIT),
        cost_estimate=pl.CostEstimate(flops=1_000_000, bytes_accessed=600_000, transcendentals=0),
        name=name,
    )


def pack_kernel(x_hbm, g_hbm, corner_out, lon_out, lat_out, corner, lon, lat, sems):
    places = (
        (pl.ds(0, 3), pl.ds(6, 30), lat, lat_out),
        (pl.ds(0, 3), pl.ds(0, 6), corner, corner_out),
        (pl.ds(3, 3), pl.ds(0, 6), lon, lon_out),
    )
    copies = []
    for n, (a, b, to, _) in enumerate(places):
        for k, array in enumerate((x_hbm, g_hbm)):
            copies.append(pltpu.make_async_copy(array.at[a, b], to.at[k], sems.at[2 * n + k]))
    for copy in copies:
        copy.start()
    for n, (_, _, held, out) in enumerate(places):
        copies[2 * n].wait()
        copies[2 * n + 1].wait()
        for a in range(3):
            out[a] = side_by_side(held, a)


def side_by_side(held, a):
    rows = held.shape[2] * 4
    return jnp.concatenate([held[k, a].reshape(rows, C) for k in range(2)], axis=1)


def pack(x, g):
    vmem = pl.BlockSpec(memory_space=pltpu.VMEM)
    return pl.pallas_call(
        pack_kernel,
        out_shape=(
            jax.ShapeDtypeStruct((3, TAIL, 2 * C), bf16),
            jax.ShapeDtypeStruct((3, TAIL, 2 * C), bf16),
            jax.ShapeDtypeStruct((3, BODY, 2 * C), bf16),
        ),
        in_specs=[pl.BlockSpec(memory_space=pltpu.HBM)] * 2,
        out_specs=(vmem,) * 3,
        scratch_shapes=[
            pltpu.VMEM((2, 3, 6, 4, C), bf16),
            pltpu.VMEM((2, 3, 6, 4, C), bf16),
            pltpu.VMEM((2, 3, 30, 4, C), bf16),
            pltpu.SemaphoreType.DMA((6,)),
        ],
        compiler_params=pltpu.CompilerParams(vmem_limit_bytes=VMEM_LIMIT),
        name="pack",
    )(in_hbm(x), in_hbm(g))


def exchange(blocks, axes):
    order = [list(reversed(range(blocks.shape[0])))]
    return lax.all_to_all(blocks, axes, 0, 0, tiled=True, axis_index_groups=order)


def on_device(x, g, ln_gain, w_qkv, w_proj, bias_table):
    lon_axes, lat_axes = ("z", "y", "xh"), ("xl", "c")
    both = lon_axes + lat_axes
    lons, lats = lax.axis_size(lon_axes), lax.axis_size(lat_axes)
    lon_swap = [(i, i ^ 1) for i in range(lons)]
    lat_down = [(i, (i - 1) % lats) for i in range(lats)]
    lat_up = [(i, (i + 1) % lats) for i in range(lats)]
    corner_up = [(i * lats + a, (i ^ 1) * lats + b) for i in range(lons) for a, b in lat_up]
    corner_down = [(i * lats + a, (i ^ 1) * lats + b) for i in range(lons) for a, b in lat_down]

    x, g = x.transpose(1, 2, 0, 3), g.transpose(1, 2, 0, 3)
    to_corner, to_lon, to_lat = pack(x, g)
    corner_in = lax.ppermute(to_corner, both, corner_down)
    lon_in = lax.ppermute(to_lon, lon_axes, lon_swap)
    lat_in = lax.ppermute(to_lat, lat_axes, lat_down)
    bias, bias_left, w3, w3t, wproj_t, own, match, gain = prepare(
        bias_table[0].transpose(1, 0, 2), w_qkv, w_proj, ln_gain.reshape(1, C), x, g
    )
    rows, send = main(
        own, lat_in, lon_in, corner_in, gain, w3, w3t, wproj_t, bias, bias_left, match
    )
    own, to_lat, to_lon, to_corner = pieces(rows)
    back = (
        lax.ppermute(to_lat, lat_axes, lat_up),
        lax.ppermute(to_lon, lon_axes, lon_swap),
        lax.ppermute(to_corner, both, corner_up),
    )
    got = exchange(send, GROUP)
    mixed = on_chip(fold_kernel, (lax.axis_size(REST), 16, 128 * (W_SLOTS + LATS)), "fold")(got)
    got = exchange(mixed, REST)
    spread = on_chip(share_kernel, send.shape, "share")(got)
    spread, back = lax.optimization_barrier((spread, back))
    parts = exchange(spread, GROUP)
    grad_gain, grad_wqkv, grad_wproj, grad_bias = unpack(parts)
    grad_x = norm_grads(x, g, gain, own, *back)
    grad_x = grad_x.transpose(2, 0, 1, 3)
    grad_bias = grad_bias.transpose(1, 0, 2)[None]
    return grad_x, grad_gain.reshape(C), grad_wqkv, grad_wproj, grad_bias


def solution(mesh):
    shape = (mesh.shape["lon"] // 8, 4, 2, 2, 2)
    split = Mesh(mesh.devices.reshape(shape), ("z", "y", "xh", "xl", "c"))
    tokens = P(None, ("xl", "c"), ("z", "y", "xh"), None)
    table = P(("xl", "c"), None, None, None)
    return jax.shard_map(
        on_device,
        mesh=split,
        in_specs=(tokens, tokens, P(), P(), P(), table),
        out_specs=(tokens, P(), P(), P(), table),
        check_vma=False,
    )
```

```python
import functools

import jax
import jax.numpy as jnp
from jax import lax
from jax.experimental import pallas as pl
from jax.experimental.pallas import tpu as pltpu
from jax.sharding import Mesh, PartitionSpec as P

C = 192
HEADS = 6
HEAD_DIM = 32
WLON = 12
WIN = 144
TABLE = 3312
PAIRS = 12
OFFSETS = 23
LOG2E = 1.4426950408889634
SCALE = HEAD_DIM**-0.5
BODY = 120
TAIL = 24
MAIN = 128
LEFT = 16
SHARED = HEADS * LEFT
STRIPS = 3
WINDOWS = 6
TYPES = 12
GROUP = ("y", "xh", "xl", "c")
REST = "z"
PARTS = 32
ORDER = [31 - (y * 8 + xh * 4 + xl * 2 + c) for c in range(2) for xl in range(2) for xh in range(2) for y in range(4)]
SLOTS = 3
W_TILES = 72
W_SLOTS = 2
B_COLUMNS = 26
B_TILES = 20
B_FIRST = 8
GAIN_PART = B_FIRST + B_TILES
WIDTH = 256
LATS = 4
WIDE = 3584
f32 = jnp.float32
bf16 = jnp.bfloat16
VMEM_LIMIT = 40 * 1024 * 1024

NN = (((1,), (0,)), ((), ()))
TN = (((0,), (0,)), ((), ()))


def dot(a, b, dims=NN):
    return lax.dot_general(a, b, dims, preferred_element_type=f32)


def table_offset(zl_i, zl_j):
    li, zi = divmod(zl_i, 2)
    lj, zj = divmod(zl_j, 2)
    return (((zi * 2 + zj) * 6 + li) * 6 + lj) * OFFSETS


def iota(shape, dim):
    return lax.broadcasted_iota(jnp.int32, shape, dim)


def ones_where(condition):
    return jnp.where(condition, 1.0, 0.0).astype(bf16)


def query_index(column):
    return jnp.where(column < MAIN, column, MAIN + column % LEFT)


def offset_match(oj, transposed):
    shape = (2 * MAIN, PAIRS * 32) if transposed else (PAIRS * 32, 2 * MAIN)
    row, col = iota(shape, 1 if transposed else 0), iota(shape, 0 if transposed else 1)
    token = query_index(col)
    zl = token // WLON
    target = zl * 32 + (oj + 11) - (token - zl * WLON)
    return ones_where((row == target) & (col < MAIN + SHARED))


def window_order(transposed):
    dest, source = iota((WIN, WIN), 1 if transposed else 0), iota((WIN, WIN), 0 if transposed else 1)
    window = dest // 24
    lz = window // STRIPS
    strip = window - lz * STRIPS
    inside = dest - window * 24
    zi = inside // WLON
    longitude = strip * WLON + inside - zi * WLON
    level = (2 * lz + zi + 1) % 4
    return ones_where(source == 4 * longitude + level)


def prepare_kernel(
    table_hbm, wqkv_hbm, wproj_hbm, gain_hbm, x_hbm, g_hbm,
    main_ref, left_ref, w3_ref, w3t_ref, wprojt_ref, own_ref, match_ref, gain_out,
    wide, pairs, table_ref, wqkv_ref, wproj_ref, mine, sems,
):
    kept = pl.ds(3, 3), pl.ds(6, 30)
    moves = (
        (table_hbm, table_ref),
        (wqkv_hbm, wqkv_ref),
        (wproj_hbm, wproj_ref),
        (gain_hbm, gain_out),
        (x_hbm.at[kept], mine.at[0]),
        (g_hbm.at[kept], mine.at[1]),
    )
    copies = [pltpu.make_async_copy(a, b, sems.at[n]) for n, (a, b) in enumerate(moves)]
    for copy in copies:
        copy.start()
    for oj in range(WLON):
        match_ref[oj] = offset_match(oj, True)
    for copy in copies:
        copy.wait()
    for k in range(3):
        part = wqkv_ref[:, k * C : (k + 1) * C]
        w3_ref[k] = part
        w3t_ref[k * WIDTH : k * WIDTH + C] = part.T
        w3t_ref[k * WIDTH + C : (k + 1) * WIDTH] = jnp.zeros((WIDTH - C, C), bf16)
    wprojt_ref[...] = wproj_ref[...].T
    for a in range(3):
        own_ref[a] = side_by_side(mine, a)
    wide[...] = jnp.zeros_like(wide)
    for h in range(HEADS):
        for lz in range(2):
            wide[lz * HEADS + h : lz * HEADS + h + 1, :TABLE] = table_ref[h, lz : lz + 1] * LOG2E
    pairs[...] = jnp.zeros_like(pairs)
    lane = iota((16, 128), 1)
    for zl_j in range(PAIRS):
        for v in range(3):
            total = jnp.zeros((16, 128), f32)
            for q in range(4):
                off = table_offset(4 * v + q, zl_j)
                base, rest = off // 128 * 128, off % 128
                width = 128 if rest + OFFSETS <= 128 else 256
                piece = wide[:, base : base + width]
                shift = (32 * q - rest) % width
                if shift:
                    piece = pltpu.roll(piece, shift, 1)
                inside = (lane >= 32 * q) & (lane < 32 * q + OFFSETS)
                total = jnp.where(inside, piece[:, :128], total)
            pairs[v, pl.ds(zl_j, TYPES, stride=16), :] = total[:TYPES]
    full = jnp.concatenate([pairs[v] for v in range(3)], axis=1)
    high = full.astype(bf16)
    rest = full - high.astype(f32)
    middle = rest.astype(bf16)
    low = (rest - middle.astype(f32)).astype(bf16)
    lane_head = iota((PAIRS, MAIN), 1) // LEFT
    for oj in range(WLON):
        match = offset_match(oj, False)
        dense = dot(high, match) + (dot(middle, match) + dot(low, match))
        for lz in range(2):
            left = jnp.zeros((PAIRS, MAIN), f32)
            for h in range(HEADS):
                t = lz * HEADS + h
                block = dense[t * 16 : t * 16 + PAIRS]
                main_ref[t, pl.ds(oj, PAIRS, stride=WLON), :] = block[:, :MAIN]
                left = jnp.where(lane_head == h, block[:, MAIN:], left)
            left_ref[lz, pl.ds(oj, PAIRS, stride=WLON), :] = left
    lat = lax.axis_index("xl") * 2 + lax.axis_index("c")
    last_band = (lat == LATS - 1).astype(jnp.int32)

    def region(token, last_level):
        upper = (token // WLON) % 2 * (2 * last_level)
        return upper + jnp.where(token >= 72, last_band, 0)

    j = iota((WIN, MAIN), 0)
    column = iota((WIN, MAIN), 1)
    for lz in range(2):
        allowed = region(column, lz) == region(j, lz)
        for h in range(HEADS):
            t = lz * HEADS + h
            main_ref[t] = jnp.where(allowed, main_ref[t], -1e30)
        allowed = region(query_index(column + MAIN), lz) == region(j, lz)
        left_ref[lz] = jnp.where(allowed, left_ref[lz], -1e30)


def in_hbm(array):
    return pltpu.with_memory_space_constraint(array, pltpu.HBM)


def prepare(table, wqkv, wproj, gain, x, g):
    vmem = pl.BlockSpec(memory_space=pltpu.VMEM)
    return pl.pallas_call(
        prepare_kernel,
        out_shape=(
            jax.ShapeDtypeStruct((TYPES, WIN, MAIN), f32),
            jax.ShapeDtypeStruct((2, WIN, MAIN), f32),
            jax.ShapeDtypeStruct((3, C, C), bf16),
            jax.ShapeDtypeStruct((3 * WIDTH, C), bf16),
            jax.ShapeDtypeStruct((C, C), bf16),
            jax.ShapeDtypeStruct((3, BODY, 2 * C), bf16),
            jax.ShapeDtypeStruct((WLON, 2 * MAIN, PAIRS * 32), bf16),
            jax.ShapeDtypeStruct((1, C), f32),
        ),
        in_specs=[pl.BlockSpec(memory_space=pltpu.HBM)] * 6,
        out_specs=(vmem,) * 8,
        scratch_shapes=[
            pltpu.VMEM((16, WIDE), f32),
            pltpu.VMEM((3, TYPES * 16, 128), f32),
            pltpu.VMEM((HEADS, 2, TABLE), f32),
            pltpu.VMEM((C, 3 * C), bf16),
            pltpu.VMEM((C, C), bf16),
            pltpu.VMEM((2, 3, 30, 4, C), bf16),
            pltpu.SemaphoreType.DMA((6,)),
        ],
        compiler_params=pltpu.CompilerParams(vmem_limit_bytes=VMEM_LIMIT),
        cost_estimate=pl.CostEstimate(
            flops=400_000_000, bytes_accessed=400_000, transcendentals=0
        ),
        name="prepare",
    )(*(in_hbm(a) for a in (table, wqkv, wproj, gain, x, g)))


def normalised(values):
    mean = jnp.mean(values, axis=-1, keepdims=True)
    centred = values - mean
    inverse = lax.rsqrt(jnp.mean(centred * centred, axis=-1, keepdims=True) + 1e-05)
    return centred * inverse, inverse


def w_place(t):
    if t < W_SLOTS * PARTS:
        return t // W_SLOTS, t % W_SLOTS
    return t - W_SLOTS * PARTS, W_SLOTS


def main_kernel(
    own_ref, lat_ref, lon_ref, corner_ref, gain_ref, w3_ref, w3t_ref, wprojt_ref,
    bias_ref, left_ref, match_ref, rows_out, send_hbm,
    xw, gw, standard_ref, cot_ref, query_ref, key_ref, value_ref, mixed_ref, tokens_ref,
    qkv_t_ref, mixed_t_ref, scores_ref, grad_attend_ref, half_ref, grad_half_ref, dense, dense_left,
    wsum, psum, gsum, spread, outputs_ref, cots_ref, wide, grads, stack,
    send_shared, send_last, sems,
):
    order = window_order(False)
    for a in range(6):
        body, tail = (own_ref[a], lon_ref[a]) if a < 3 else (lat_ref[a - 3], corner_ref[a - 3])
        line = dot(order[:, :BODY], body) + dot(order[:, BODY:], tail)
        for w in range(WINDOWS):
            xw[w, 24 * a : 24 * a + 24, :] = line[24 * w : 24 * w + 24, :C]
            gw[w, 24 * a : 24 * a + 24, :] = line[24 * w : 24 * w + 24, C:]
    dense[...] = jnp.zeros_like(dense)
    dense_left[...] = jnp.zeros_like(dense_left)
    gsum[...] = jnp.zeros_like(gsum)
    spread[...] = jnp.zeros_like(spread)
    gain = gain_ref[...]
    lane_head = iota((WIN, C), 1) // HEAD_DIM
    shape = (WIN, MAIN)
    repeat = ones_where((iota(shape, 0) == MAIN + iota(shape, 1) % LEFT) & (iota(shape, 1) < SHARED))
    shape = (LEFT, MAIN)
    gather = ones_where((iota(shape, 0) == iota(shape, 1) % LEFT) & (iota(shape, 1) < SHARED))
    own_head_t = iota((C, MAIN), 0) // HEAD_DIM == iota((C, MAIN), 1) // LEFT
    own_head = iota((MAIN, C), 1) // HEAD_DIM == iota((MAIN, C), 0) // LEFT

    def of_head(value, h):
        return jnp.where(lane_head[: value.shape[0]] == h, value, jnp.zeros_like(value))

    def per_head(columns, left):
        blocks = []
        for h in range(HEADS):
            above = jnp.zeros((h * HEAD_DIM, MAIN), bf16)
            below = jnp.zeros((C - (h + 1) * HEAD_DIM, MAIN), bf16)
            own = columns[h * HEAD_DIM : (h + 1) * HEAD_DIM, :MAIN]
            blocks.append(jnp.concatenate([x for x in (above, own, below) if x.shape[0]], axis=0))
        return jnp.concatenate(blocks + [only_head(own_head_t, left)], axis=1)

    def repeated(rows):
        zeros = jnp.zeros((MAIN - SHARED, C), bf16)
        return jnp.concatenate([rows[MAIN:]] * HEADS + [zeros], axis=0)

    def only_head(mask, value):
        return jnp.where(mask, value, jnp.zeros_like(value)).astype(bf16)

    standard, _ = normalised(xw[...].reshape(WINDOWS * WIN, C))
    standard_ref[...] = standard
    tokens = (standard * gain).astype(bf16)
    tokens_ref[...] = tokens
    cots = gw[...].reshape(WINDOWS * WIN, C).astype(bf16)
    cot_ref[...] = cots
    query_ref[...] = dot(tokens, w3_ref[0]).astype(bf16)
    key_ref[...] = dot(tokens, w3_ref[1]).astype(bf16)
    value_ref[...] = dot(tokens, w3_ref[2]).astype(bf16)
    mixed_ref[...] = dot(cots, wprojt_ref[...]).astype(bf16)
    for w in range(WINDOWS):
        span = slice(w * WIN, (w + 1) * WIN)
        for k, ref in enumerate((query_ref, key_ref, value_ref)):
            qkv_t_ref[w, k * C : (k + 1) * C] = ref[span].T
        mixed_t_ref[w] = mixed_ref[span].T

    for w in range(WINDOWS):
        lz = w // STRIPS
        span = slice(w * WIN, (w + 1) * WIN)
        query_t, mixed_t = qkv_t_ref[w, 0:C], mixed_t_ref[w]
        key, value = key_ref[span], value_ref[span]
        scores_ref[w] = dot(key, per_head(query_t, dot(query_t, repeat)))
        grad_attend_ref[w] = dot(value, per_head(mixed_t, dot(mixed_t, repeat)))
        for t in range(HEADS + 1):
            columns = slice(t * MAIN, (t + 1) * MAIN)
            bias = bias_ref[lz * HEADS + t] if t < HEADS else left_ref[lz]
            scores = scores_ref[w, :, columns] * (SCALE * LOG2E) + bias
            top = jnp.max(scores, axis=0, keepdims=True)
            powers = jnp.exp2(scores - top)
            attend = powers * (1.0 / jnp.sum(powers, axis=0, keepdims=True))
            half_ref[w, :, columns] = attend.astype(bf16)
            grad_attend = grad_attend_ref[w, :, columns]
            total = jnp.sum(attend * grad_attend, axis=0, keepdims=True)
            grad_scores = attend * (grad_attend - total)
            grad_half_ref[w, :, columns] = grad_scores.astype(bf16)
            if t < HEADS:
                dense[lz * HEADS + t] += grad_scores
            else:
                dense_left[lz] += grad_scores

    for w in range(WINDOWS):
        span = slice(w * WIN, (w + 1) * WIN)

        def per_query(left, right_ref):
            parts = []
            for h in range(0, HEADS, 2):
                two = dot(
                    left[h * HEAD_DIM : (h + 2) * HEAD_DIM],
                    right_ref[w, :, h * MAIN : (h + 2) * MAIN],
                )
                parts += [two[:HEAD_DIM, :MAIN], two[HEAD_DIM:, MAIN:]]
            shared = dot(left, right_ref[w, :, HEADS * MAIN :])
            return jnp.concatenate(parts, axis=0), jnp.where(own_head_t, shared, 0.0)

        def per_key(left_ref, right):
            parts = [of_head(right[:MAIN], h) for h in range(HEADS)]
            parts.append(only_head(own_head, repeated(right)))
            return dot(left_ref[w], jnp.concatenate(parts, axis=0))

        cot = cot_ref[span]
        out_t, out_left = per_query(qkv_t_ref[w, 2 * C :], half_ref)
        outputs_ref[:, 2 * w * MAIN : (2 * w + 1) * MAIN] = out_t.astype(bf16)
        outputs_ref[:, (2 * w + 1) * MAIN : 2 * (w + 1) * MAIN] = out_left.astype(bf16)
        cots_ref[2 * w * MAIN : (2 * w + 1) * MAIN] = cot[:MAIN]
        cots_ref[(2 * w + 1) * MAIN : 2 * (w + 1) * MAIN] = repeated(cot)
        query_grad, query_left = per_query(qkv_t_ref[w, C : 2 * C], grad_half_ref)
        first = slice(w * WIN, w * WIN + MAIN)
        last = slice(w * WIN + MAIN, (w + 1) * WIN)
        spread[first, 0:C] = (query_grad * SCALE).astype(bf16).T
        spread[last, 0:C] = dot(gather, (query_left * SCALE).astype(bf16).T).astype(bf16)
        grad_key = per_key(grad_half_ref, query_ref[span]) * SCALE
        spread[span, WIDTH : WIDTH + C] = grad_key.astype(bf16)
        spread[span, 2 * WIDTH : 2 * WIDTH + C] = per_key(half_ref, mixed_ref[span]).astype(bf16)

    grad_projected = spread[...]
    back = dot(grad_projected, w3t_ref[...]).astype(bf16)
    rows_out[...] = back
    gsum[0:1, :] = jnp.sum(back.astype(f32) * standard_ref[...], axis=0, keepdims=True)
    wsum[...] = dot(tokens_ref[...], grad_projected, TN)
    psum[...] = dot(outputs_ref[...], cots_ref[...])

    weights = jnp.concatenate(
        [wsum[:, k * WIDTH : k * WIDTH + C] for k in range(3)] + [psum[...]], axis=1
    )
    for t in range(W_TILES):
        row, column = divmod(t, 6)
        tile = weights[16 * row : 16 * row + 16, 128 * column : 128 * column + 128]
        p, slot = w_place(t)
        if slot < W_SLOTS:
            send_shared[p, :, 128 * slot : 128 * slot + 128] = tile.astype(bf16)
        else:
            send_last[p] = tile.astype(bf16)
    shared_copy = pltpu.make_async_copy(
        send_shared, send_hbm.at[:, :, pl.ds(0, 128 * W_SLOTS)], sems.at[0]
    )
    shared_copy.start()

    total = jnp.zeros((TYPES * 16, PAIRS * 32), f32)
    lane_left = iota((PAIRS, MAIN), 1) // LEFT
    for oj in range(WLON):
        picked = []
        for lz in range(2):
            left = dense_left[lz, pl.ds(oj, PAIRS, stride=WLON), :]
            for h in range(HEADS):
                first = dense[lz * HEADS + h, pl.ds(oj, PAIRS, stride=WLON), :]
                both = jnp.concatenate([first, jnp.where(lane_left == h, left, 0.0)], axis=1)
                picked += [both, jnp.zeros((4, 2 * MAIN), f32)]
        picked = jnp.concatenate(picked, axis=0)
        high = picked.astype(bf16)
        match = match_ref[oj]
        total += dot(high, match)
    for v in range(3):
        grads[v] = total[:, 128 * v : 128 * (v + 1)]
    wide[...] = jnp.zeros_like(wide)
    lane = iota((TYPES, 256), 1)
    for zl_j in range(PAIRS):
        for v in range(3):
            four = grads[v, pl.ds(zl_j, TYPES, stride=16), :]
            for q in range(4):
                off = table_offset(4 * v + q, zl_j)
                base, rest = off // 128 * 128, off % 128
                width = 128 if rest + OFFSETS <= 128 else 256
                piece = four
                if width == 256:
                    piece = jnp.concatenate([four, jnp.zeros_like(four)], axis=1)
                shift = (rest - 32 * q) % width
                if shift:
                    piece = pltpu.roll(piece, shift, 1)
                position = lane[:, :width]
                inside = (position >= rest) & (position < rest + OFFSETS)
                target = (slice(0, TYPES), slice(base, base + width))
                wide[target] = jnp.where(inside, piece, wide[target])

    stack[...] = jnp.zeros_like(stack)
    for n in range(B_COLUMNS):
        stack[TYPES * n : TYPES * (n + 1), :] = wide[:TYPES, 128 * n : 128 * (n + 1)]
    for n in range(B_TILES):
        send_last[B_FIRST + n] = stack[16 * n : 16 * n + 16, :].astype(bf16)
    for p in range(GAIN_PART, PARTS):
        if p == GAIN_PART:
            line = gsum[0:1, :]
            gains = jnp.concatenate([line[:, :128], jnp.zeros((7, 128), f32)], axis=0)
            more = jnp.concatenate([line[:, 128:], jnp.zeros((1, 256 - C), f32)], axis=1)
            more = jnp.concatenate([more, jnp.zeros((7, 128), f32)], axis=0)
            send_last[p] = jnp.concatenate([gains, more], axis=0).astype(bf16)
        else:
            send_last[p] = jnp.zeros((16, 128), bf16)
    second = pltpu.make_async_copy(
        send_last, send_hbm.at[:, :, pl.ds(128 * W_SLOTS, 128)], sems.at[1]
    )
    second.start()
    shared_copy.wait()
    second.wait()


def main(own, lat_in, lon_in, corner_in, gain, w3, w3t, wproj_t, bias, bias_left, match):
    vmem = pl.BlockSpec(memory_space=pltpu.VMEM)
    return pl.pallas_call(
        main_kernel,
        out_shape=(
            jax.ShapeDtypeStruct((WINDOWS * WIN, C), bf16),
            jax.ShapeDtypeStruct((PARTS, 16, SLOTS * 128), bf16),
        ),
        in_specs=[vmem] * 11,
        out_specs=(vmem, pl.BlockSpec(memory_space=pltpu.HBM)),
        scratch_shapes=[
            pltpu.VMEM((WINDOWS, WIN, C), f32),
            pltpu.VMEM((WINDOWS, WIN, C), f32),
            pltpu.VMEM((WINDOWS * WIN, C), f32),
            pltpu.VMEM((WINDOWS * WIN, C), bf16),
            pltpu.VMEM((WINDOWS * WIN, C), bf16),
            pltpu.VMEM((WINDOWS * WIN, C), bf16),
            pltpu.VMEM((WINDOWS * WIN, C), bf16),
            pltpu.VMEM((WINDOWS * WIN, C), bf16),
            pltpu.VMEM((WINDOWS * WIN, C), bf16),
            pltpu.VMEM((WINDOWS, 3 * C, WIN), bf16),
            pltpu.VMEM((WINDOWS, C, WIN), bf16),
            pltpu.VMEM((WINDOWS, WIN, (HEADS + 1) * MAIN), f32),
            pltpu.VMEM((WINDOWS, WIN, (HEADS + 1) * MAIN), f32),
            pltpu.VMEM((WINDOWS, WIN, (HEADS + 1) * MAIN), bf16),
            pltpu.VMEM((WINDOWS, WIN, (HEADS + 1) * MAIN), bf16),
            pltpu.VMEM((TYPES, WIN, MAIN), f32),
            pltpu.VMEM((2, WIN, MAIN), f32),
            pltpu.VMEM((C, 3 * WIDTH), f32),
            pltpu.VMEM((C, C), f32),
            pltpu.VMEM((8, C), f32),
            pltpu.VMEM((WINDOWS * WIN, 3 * WIDTH), bf16),
            pltpu.VMEM((C, 2 * WINDOWS * MAIN), bf16),
            pltpu.VMEM((2 * WINDOWS * MAIN, C), bf16),
            pltpu.VMEM((16, WIDE), f32),
            pltpu.VMEM((3, TYPES * 16, 128), f32),
            pltpu.VMEM((B_TILES * 16, 128), f32),
            pltpu.VMEM((PARTS, 16, 128 * W_SLOTS), bf16),
            pltpu.VMEM((PARTS, 16, 128), bf16),
            pltpu.SemaphoreType.DMA((2,)),
        ],
        compiler_params=pltpu.CompilerParams(vmem_limit_bytes=VMEM_LIMIT),
        cost_estimate=pl.CostEstimate(
            flops=20_000_000_000, bytes_accessed=4_000_000, transcendentals=750_000
        ),
        name="window_grads",
    )(own, lat_in, lon_in, corner_in, gain, w3, w3t, wproj_t, bias, bias_left, match)


def pieces_kernel(rows_ref, own_out, lat_out, lon_out, corner_out):
    order_t = window_order(True)
    for a in range(6):
        line = jnp.concatenate(
            [rows_ref[WIN * w + 24 * a : WIN * w + 24 * a + 24, :] for w in range(WINDOWS)], axis=0
        )
        line = dot(order_t, line)
        body, tail = line[:BODY].astype(bf16), line[BODY:].astype(bf16)
        if a < 3:
            own_out[a], lon_out[a] = body, tail
        else:
            lat_out[a - 3], corner_out[a - 3] = body, tail


def pieces(rows):
    vmem = pl.BlockSpec(memory_space=pltpu.VMEM)
    return pl.pallas_call(
        pieces_kernel,
        out_shape=(
            jax.ShapeDtypeStruct((3, BODY, C), bf16),
            jax.ShapeDtypeStruct((3, BODY, C), bf16),
            jax.ShapeDtypeStruct((3, TAIL, C), bf16),
            jax.ShapeDtypeStruct((3, TAIL, C), bf16),
        ),
        in_specs=[vmem],
        out_specs=(vmem,) * 4,
        compiler_params=pltpu.CompilerParams(vmem_limit_bytes=VMEM_LIMIT),
        cost_estimate=pl.CostEstimate(
            flops=500_000_000, bytes_accessed=700_000, transcendentals=0
        ),
        name="pieces",
    )(rows)


def norm_kernel(x_ref, g_ref, gain_ref, own_ref, lat_ref, lon_ref, corner_ref, out_ref):
    gain = gain_ref[...]
    for a in range(6):
        if a < 3:
            head, body = corner_ref[a], lat_ref[a]
        else:
            head, body = lon_ref[a - 3], own_ref[a - 3]
        grad = jnp.concatenate([head.astype(f32), body.astype(f32)], axis=0)
        standard, inverse = normalised(x_ref[a].reshape(WIN, C).astype(f32))
        scaled = grad * gain
        local = inverse * (
            scaled
            - jnp.mean(scaled, axis=-1, keepdims=True)
            - standard * jnp.mean(scaled * standard, axis=-1, keepdims=True)
        )
        total = (g_ref[a].reshape(WIN, C).astype(f32) + local).astype(bf16)
        out_ref[a] = total.reshape(36, 4, C)


def norm_grads(x, g, gain, own, lat_in, lon_in, corner_in):
    vmem = pl.BlockSpec(memory_space=pltpu.VMEM)
    return pl.pallas_call(
        norm_kernel,
        out_shape=jax.ShapeDtypeStruct(x.shape, bf16),
        in_specs=[vmem] * 7,
        out_specs=vmem,
        compiler_params=pltpu.CompilerParams(vmem_limit_bytes=VMEM_LIMIT),
        cost_estimate=pl.CostEstimate(
            flops=10_000_000, bytes_accessed=1_500_000, transcendentals=1000
        ),
        name="norm_grads",
    )(x, g, gain, own, lat_in, lon_in, corner_in)


def unpack_kernel(parts_ref, gain_out, wqkv_out, wproj_out, bias_out, stack):
    last = slice(128 * W_SLOTS, 128 * SLOTS)
    gains = parts_ref[GAIN_PART, :, last].astype(f32)
    gain_out[:, :128] = gains[0:1]
    gain_out[:, 128:] = gains[8:9, : C - 128]

    def tile(t):
        p, slot = w_place(t)
        return parts_ref[p, :, 128 * slot : 128 * slot + 128].astype(f32)

    for row in range(C // 16):
        lines = slice(16 * row, 16 * row + 16)
        for column in range(4):
            wqkv_out[lines, 128 * column : 128 * column + 128] = tile(6 * row + column)
        mixed = tile(6 * row + 4)
        wqkv_out[lines, 512:] = mixed[:, :64]
        wproj_out[lines, :] = jnp.concatenate([mixed[:, 64:], tile(6 * row + 5)], axis=1)
    for n in range(B_TILES):
        stack[16 * n : 16 * n + 16, :] = parts_ref[B_FIRST + n, :, last].astype(f32)
    for n in range(B_COLUMNS):
        width = min(128, TABLE - 128 * n)
        for h in range(HEADS):
            for lz in range(2):
                t = TYPES * n + lz * HEADS + h
                bias_out[h, lz : lz + 1, 128 * n : 128 * n + width] = stack[t : t + 1, :width]


def unpack(parts):
    vmem = pl.BlockSpec(memory_space=pltpu.VMEM)
    return pl.pallas_call(
        unpack_kernel,
        out_shape=(
            jax.ShapeDtypeStruct((1, C), f32),
            jax.ShapeDtypeStruct((C, 3 * C), f32),
            jax.ShapeDtypeStruct((C, C), f32),
            jax.ShapeDtypeStruct((HEADS, 2, TABLE), f32),
        ),
        in_specs=[vmem],
        out_specs=(vmem,) * 4,
        scratch_shapes=[pltpu.VMEM((B_TILES * 16, 128), f32)],
        compiler_params=pltpu.CompilerParams(vmem_limit_bytes=VMEM_LIMIT),
        name="unpack",
    )(parts)


def fold_kernel(got_ref, out_ref):
    shared = jnp.zeros((16, 128 * W_SLOTS), f32)
    last = [jnp.zeros((16, 128), f32)] * LATS
    for p in range(PARTS):
        shared += got_ref[p, :, : 128 * W_SLOTS].astype(f32)
        last[ORDER[p] % LATS] += got_ref[p, :, 128 * W_SLOTS :].astype(f32)
    total = jnp.concatenate([shared] + last, axis=1).astype(bf16)
    for n in range(out_ref.shape[0]):
        out_ref[n] = total


def share_kernel(got_ref, out_ref):
    total = jnp.zeros(got_ref.shape[1:], f32)
    for n in range(got_ref.shape[0]):
        total += got_ref[n].astype(f32)
    shared = total[:, : 128 * W_SLOTS].astype(bf16)
    last = [total[:, 128 * (W_SLOTS + n) : 128 * (W_SLOTS + n + 1)] for n in range(LATS)]
    everywhere = last[0] + last[1] + last[2] + last[3]
    place = lax.axis_index(GROUP)
    per_lat = place == ORDER[B_FIRST]
    for p in range(B_FIRST + 1, GAIN_PART):
        per_lat |= place == ORDER[p]
    last = [jnp.where(per_lat, one, everywhere).astype(bf16) for one in last]
    for p in range(PARTS):
        out_ref[p, :, : 128 * W_SLOTS] = shared
        out_ref[p, :, 128 * W_SLOTS :] = last[ORDER[p] % LATS]


def on_chip(kernel, shape, name):
    vmem = pl.BlockSpec(memory_space=pltpu.VMEM)
    return pl.pallas_call(
        kernel,
        out_shape=jax.ShapeDtypeStruct(shape, bf16),
        in_specs=[vmem],
        out_specs=vmem,
        compiler_params=pltpu.CompilerParams(vmem_limit_bytes=VMEM_LIMIT),
        cost_estimate=pl.CostEstimate(flops=1_000_000, bytes_accessed=600_000, transcendentals=0),
        name=name,
    )


def pack_kernel(x_hbm, g_hbm, corner_out, lon_out, lat_out, corner, lon, lat, sems):
    places = (
        (pl.ds(0, 3), pl.ds(6, 30), lat, lat_out),
        (pl.ds(0, 3), pl.ds(0, 6), corner, corner_out),
        (pl.ds(3, 3), pl.ds(0, 6), lon, lon_out),
    )
    copies = []
    for n, (a, b, to, _) in enumerate(places):
        for k, array in enumerate((x_hbm, g_hbm)):
            copies.append(pltpu.make_async_copy(array.at[a, b], to.at[k], sems.at[2 * n + k]))
    for copy in copies:
        copy.start()
    for n, (_, _, held, out) in enumerate(places):
        copies[2 * n].wait()
        copies[2 * n + 1].wait()
        for a in range(3):
            out[a] = side_by_side(held, a)


def side_by_side(held, a):
    rows = held.shape[2] * 4
    return jnp.concatenate([held[k, a].reshape(rows, C) for k in range(2)], axis=1)


def pack(x, g):
    vmem = pl.BlockSpec(memory_space=pltpu.VMEM)
    return pl.pallas_call(
        pack_kernel,
        out_shape=(
            jax.ShapeDtypeStruct((3, TAIL, 2 * C), bf16),
            jax.ShapeDtypeStruct((3, TAIL, 2 * C), bf16),
            jax.ShapeDtypeStruct((3, BODY, 2 * C), bf16),
        ),
        in_specs=[pl.BlockSpec(memory_space=pltpu.HBM)] * 2,
        out_specs=(vmem,) * 3,
        scratch_shapes=[
            pltpu.VMEM((2, 3, 6, 4, C), bf16),
            pltpu.VMEM((2, 3, 6, 4, C), bf16),
            pltpu.VMEM((2, 3, 30, 4, C), bf16),
            pltpu.SemaphoreType.DMA((6,)),
        ],
        compiler_params=pltpu.CompilerParams(vmem_limit_bytes=VMEM_LIMIT),
        name="pack",
    )(in_hbm(x), in_hbm(g))


def exchange(blocks, axes, order):
    return lax.all_to_all(blocks, axes, 0, 0, tiled=True, axis_index_groups=[order])


def on_device(x, g, ln_gain, w_qkv, w_proj, bias_table):
    lon_axes, lat_axes = ("z", "y", "xh"), ("xl", "c")
    both = lon_axes + lat_axes
    lons, lats = lax.axis_size(lon_axes), lax.axis_size(lat_axes)
    lon_swap = [(i, i ^ 1) for i in range(lons)]
    lat_down = [(i, (i - 1) % lats) for i in range(lats)]
    lat_up = [(i, (i + 1) % lats) for i in range(lats)]
    corner_up = [(i * lats + a, (i ^ 1) * lats + b) for i in range(lons) for a, b in lat_up]
    corner_down = [(i * lats + a, (i ^ 1) * lats + b) for i in range(lons) for a, b in lat_down]

    x, g = x.transpose(1, 2, 0, 3), g.transpose(1, 2, 0, 3)
    to_corner, to_lon, to_lat = pack(x, g)
    corner_in = lax.ppermute(to_corner, both, corner_down)
    lon_in = lax.ppermute(to_lon, lon_axes, lon_swap)
    lat_in = lax.ppermute(to_lat, lat_axes, lat_down)
    bias, bias_left, w3, w3t, wproj_t, own, match, gain = prepare(
        bias_table[0].transpose(1, 0, 2), w_qkv, w_proj, ln_gain.reshape(1, C), x, g
    )
    rows, send = main(
        own, lat_in, lon_in, corner_in, gain, w3, w3t, wproj_t, bias, bias_left, match
    )
    own, to_lat, to_lon, to_corner = pieces(rows)
    back = (
        lax.ppermute(to_lat, lat_axes, lat_up),
        lax.ppermute(to_lon, lon_axes, lon_swap),
        lax.ppermute(to_corner, both, corner_up),
    )
    got = exchange(send, GROUP, ORDER)
    mixed = on_chip(fold_kernel, (lax.axis_size(REST), 16, 128 * (W_SLOTS + LATS)), "fold")(got)
    got = exchange(mixed, REST, list(reversed(range(mixed.shape[0]))))
    spread = on_chip(share_kernel, send.shape, "share")(got)
    spread, back = lax.optimization_barrier((spread, back))
    parts = exchange(spread, GROUP, ORDER)
    grad_gain, grad_wqkv, grad_wproj, grad_bias = unpack(parts)
    grad_x = norm_grads(x, g, gain, own, *back)
    grad_x = grad_x.transpose(2, 0, 1, 3)
    grad_bias = grad_bias.transpose(1, 0, 2)[None]
    return grad_x, grad_gain.reshape(C), grad_wqkv, grad_wproj, grad_bias


def solution(mesh):
    shape = (mesh.shape["lon"] // 8, 4, 2, 2, 2)
    split = Mesh(mesh.devices.reshape(shape), ("z", "y", "xh", "xl", "c"))
    tokens = P(None, ("xl", "c"), ("z", "y", "xh"), None)
    table = P(("xl", "c"), None, None, None)
    return jax.shard_map(
        on_device,
        mesh=split,
        in_specs=(tokens, tokens, P(), P(), P(), table),
        out_specs=(tokens, P(), P(), P(), table),
        check_vma=False,
    )
```

```python
import functools

import jax
import jax.numpy as jnp
from jax import lax
from jax.experimental import pallas as pl
from jax.experimental.pallas import tpu as pltpu
from jax.sharding import Mesh, PartitionSpec as P

C = 192
HEADS = 6
HEAD_DIM = 32
WLON = 12
WIN = 144
TABLE = 3312
PAIRS = 12
OFFSETS = 23
LOG2E = 1.4426950408889634
SCALE = HEAD_DIM**-0.5
BODY = 120
TAIL = 24
MAIN = 128
LEFT = 16
SHARED = HEADS * LEFT
STRIPS = 3
WINDOWS = 6
TYPES = 12
GROUP = ("y", "xh", "xl", "c")
REST = "z"
PARTS = 32
ORDER = [31 - (y * 8 + xh * 4 + xl * 2 + c) for c in range(2) for xl in range(2) for xh in range(2) for y in range(4)]
SLOTS = 3
W_TILES = 72
W_SLOTS = 2
B_COLUMNS = 26
B_TILES = 20
B_FIRST = 8
GAIN_PART = B_FIRST + B_TILES
WIDTH = 256
LATS = 4
WIDE = 3584
TALL = 160
TALLER = 208
f32 = jnp.float32
bf16 = jnp.bfloat16
VMEM_LIMIT = 40 * 1024 * 1024

NN = (((1,), (0,)), ((), ()))
TN = (((0,), (0,)), ((), ()))


def dot(a, b, dims=NN):
    return lax.dot_general(a, b, dims, preferred_element_type=f32)


def table_offset(zl_i, zl_j):
    li, zi = divmod(zl_i, 2)
    lj, zj = divmod(zl_j, 2)
    return (((zi * 2 + zj) * 6 + li) * 6 + lj) * OFFSETS


def iota(shape, dim):
    return lax.broadcasted_iota(jnp.int32, shape, dim)


def ones_where(condition):
    return jnp.where(condition, 1.0, 0.0).astype(bf16)


def query_index(column):
    return jnp.where(column < MAIN, column, MAIN + column % LEFT)


def offset_match(oj, transposed):
    shape = (2 * MAIN, PAIRS * 32) if transposed else (PAIRS * 32, 2 * MAIN)
    row, col = iota(shape, 1 if transposed else 0), iota(shape, 0 if transposed else 1)
    token = query_index(col)
    zl = token // WLON
    target = zl * 32 + (oj + 11) - (token - zl * WLON)
    return ones_where((row == target) & (col < MAIN + SHARED))


def window_order(transposed):
    dest, source = iota((WIN, WIN), 1 if transposed else 0), iota((WIN, WIN), 0 if transposed else 1)
    window = dest // 24
    lz = window // STRIPS
    strip = window - lz * STRIPS
    inside = dest - window * 24
    zi = inside // WLON
    longitude = strip * WLON + inside - zi * WLON
    level = (2 * lz + zi + 1) % 4
    return ones_where(source == 4 * longitude + level)


def prepare_kernel(
    table_hbm, wqkv_hbm, wproj_hbm, gain_hbm, x_hbm, g_hbm,
    main_ref, left_ref, w3_ref, w3t_ref, wprojt_ref, own_ref, match_ref, gain_out,
    wide, pairs, plain, plain_left, table_ref, wqkv_ref, wproj_ref, mine, sems,
):
    kept = pl.ds(3, 3), pl.ds(6, 30)
    moves = (
        (table_hbm, table_ref),
        (wqkv_hbm, wqkv_ref),
        (wproj_hbm, wproj_ref),
        (gain_hbm, gain_out),
        (x_hbm.at[kept], mine.at[0]),
        (g_hbm.at[kept], mine.at[1]),
    )
    copies = [pltpu.make_async_copy(a, b, sems.at[n]) for n, (a, b) in enumerate(moves)]
    for copy in copies:
        copy.start()
    for oj in range(WLON):
        match_ref[oj] = offset_match(oj, True)
    for copy in copies:
        copy.wait()
    for k in range(3):
        part = wqkv_ref[:, k * C : (k + 1) * C]
        w3_ref[k] = part
        w3t_ref[k * WIDTH : k * WIDTH + C] = part.T
        w3t_ref[k * WIDTH + C : (k + 1) * WIDTH] = jnp.zeros((WIDTH - C, C), bf16)
    wprojt_ref[...] = wproj_ref[...].T
    for a in range(3):
        own_ref[a] = side_by_side(mine, a)
    wide[...] = jnp.zeros_like(wide)
    for h in range(HEADS):
        for lz in range(2):
            wide[lz * HEADS + h : lz * HEADS + h + 1, :TABLE] = table_ref[h, lz : lz + 1] * LOG2E
    pairs[...] = jnp.zeros_like(pairs)
    lane = iota((16, 128), 1)
    for zl_j in range(PAIRS):
        for v in range(3):
            total = jnp.zeros((16, 128), f32)
            for q in range(4):
                off = table_offset(4 * v + q, zl_j)
                base, rest = off // 128 * 128, off % 128
                width = 128 if rest + OFFSETS <= 128 else 256
                piece = wide[:, base : base + width]
                shift = (32 * q - rest) % width
                if shift:
                    piece = pltpu.roll(piece, shift, 1)
                inside = (lane >= 32 * q) & (lane < 32 * q + OFFSETS)
                total = jnp.where(inside, piece[:, :128], total)
            pairs[v, pl.ds(zl_j, TYPES, stride=16), :] = total[:TYPES]
    full = jnp.concatenate([pairs[v, : TYPES * 16] for v in range(3)], axis=1)
    high = full.astype(bf16)
    rest = full - high.astype(f32)
    middle = rest.astype(bf16)
    low = (rest - middle.astype(f32)).astype(bf16)
    lane_head = iota((PAIRS, MAIN), 1) // LEFT
    for oj in range(WLON):
        match = offset_match(oj, False)
        dense = dot(high, match) + (dot(middle, match) + dot(low, match))
        for lz in range(2):
            left = jnp.zeros((PAIRS, MAIN), f32)
            for h in range(HEADS):
                t = lz * HEADS + h
                block = dense[t * 16 : t * 16 + PAIRS]
                plain[t, pl.ds(oj, PAIRS, stride=WLON), :] = block[:, :MAIN]
                left = jnp.where(lane_head == h, block[:, MAIN:], left)
            plain_left[lz, pl.ds(oj, PAIRS, stride=WLON), :] = left
    lat = lax.axis_index("xl") * 2 + lax.axis_index("c")
    last_band = (lat == LATS - 1).astype(jnp.int32)

    def region(token, last_level):
        upper = (token // WLON) % 2 * (2 * last_level)
        return upper + jnp.where(token >= 72, last_band, 0)

    j = iota((WIN, MAIN), 0)
    column = iota((WIN, MAIN), 1)
    for lz in range(2):
        allowed = region(column, lz) == region(j, lz)
        for h in range(HEADS):
            t = lz * HEADS + h
            main_ref[t] = jnp.where(allowed, plain[t, :WIN], -1e30)
        allowed = region(query_index(column + MAIN), lz) == region(j, lz)
        left_ref[lz] = jnp.where(allowed, plain_left[lz, :WIN], -1e30)


def in_hbm(array):
    return pltpu.with_memory_space_constraint(array, pltpu.HBM)


def prepare(table, wqkv, wproj, gain, x, g):
    vmem = pl.BlockSpec(memory_space=pltpu.VMEM)
    return pl.pallas_call(
        prepare_kernel,
        out_shape=(
            jax.ShapeDtypeStruct((TYPES, WIN, MAIN), f32),
            jax.ShapeDtypeStruct((2, WIN, MAIN), f32),
            jax.ShapeDtypeStruct((3, C, C), bf16),
            jax.ShapeDtypeStruct((3 * WIDTH, C), bf16),
            jax.ShapeDtypeStruct((C, C), bf16),
            jax.ShapeDtypeStruct((3, BODY, 2 * C), bf16),
            jax.ShapeDtypeStruct((WLON, 2 * MAIN, PAIRS * 32), bf16),
            jax.ShapeDtypeStruct((1, C), f32),
        ),
        in_specs=[pl.BlockSpec(memory_space=pltpu.HBM)] * 6,
        out_specs=(vmem,) * 8,
        scratch_shapes=[
            pltpu.VMEM((16, WIDE), f32),
            pltpu.VMEM((3, TALLER, 128), f32),
            pltpu.VMEM((TYPES, TALL, MAIN), f32),
            pltpu.VMEM((2, TALL, MAIN), f32),
            pltpu.VMEM((HEADS, 2, TABLE), f32),
            pltpu.VMEM((C, 3 * C), bf16),
            pltpu.VMEM((C, C), bf16),
            pltpu.VMEM((2, 3, 30, 4, C), bf16),
            pltpu.SemaphoreType.DMA((6,)),
        ],
        compiler_params=pltpu.CompilerParams(vmem_limit_bytes=VMEM_LIMIT),
        cost_estimate=pl.CostEstimate(
            flops=400_000_000, bytes_accessed=400_000, transcendentals=0
        ),
        name="prepare",
    )(*(in_hbm(a) for a in (table, wqkv, wproj, gain, x, g)))


def normalised(values):
    mean = jnp.mean(values, axis=-1, keepdims=True)
    centred = values - mean
    inverse = lax.rsqrt(jnp.mean(centred * centred, axis=-1, keepdims=True) + 1e-05)
    return centred * inverse, inverse


def w_place(t):
    if t < W_SLOTS * PARTS:
        return t // W_SLOTS, t % W_SLOTS
    return t - W_SLOTS * PARTS, W_SLOTS


def main_kernel(
    own_ref, lat_ref, lon_ref, corner_ref, gain_ref, w3_ref, w3t_ref, wprojt_ref,
    bias_ref, left_ref, match_ref, rows_out, send_hbm,
    xw, gw, standard_ref, cot_ref, query_ref, key_ref, value_ref, mixed_ref, tokens_ref,
    qkv_t_ref, mixed_t_ref, scores_ref, grad_attend_ref, half_ref, grad_half_ref, dense, dense_left,
    wsum, psum, gsum, spread, outputs_ref, cots_ref, wide, grads, stack,
    send_shared, send_last, sems,
):
    order = window_order(False)
    for a in range(6):
        body, tail = (own_ref[a], lon_ref[a]) if a < 3 else (lat_ref[a - 3], corner_ref[a - 3])
        line = dot(order[:, :BODY], body) + dot(order[:, BODY:], tail)
        for w in range(WINDOWS):
            xw[w, 24 * a : 24 * a + 24, :] = line[24 * w : 24 * w + 24, :C]
            gw[w, 24 * a : 24 * a + 24, :] = line[24 * w : 24 * w + 24, C:]
    dense[...] = jnp.zeros_like(dense)
    dense_left[...] = jnp.zeros_like(dense_left)
    gsum[...] = jnp.zeros_like(gsum)
    spread[...] = jnp.zeros_like(spread)
    gain = gain_ref[...]
    lane_head = iota((WIN, C), 1) // HEAD_DIM
    shape = (WIN, MAIN)
    repeat = ones_where((iota(shape, 0) == MAIN + iota(shape, 1) % LEFT) & (iota(shape, 1) < SHARED))
    shape = (LEFT, MAIN)
    gather = ones_where((iota(shape, 0) == iota(shape, 1) % LEFT) & (iota(shape, 1) < SHARED))
    own_head_t = iota((C, MAIN), 0) // HEAD_DIM == iota((C, MAIN), 1) // LEFT
    own_head = iota((MAIN, C), 1) // HEAD_DIM == iota((MAIN, C), 0) // LEFT

    def of_head(value, h):
        return jnp.where(lane_head[: value.shape[0]] == h, value, jnp.zeros_like(value))

    def per_head(columns, left):
        blocks = []
        for h in range(HEADS):
            above = jnp.zeros((h * HEAD_DIM, MAIN), bf16)
            below = jnp.zeros((C - (h + 1) * HEAD_DIM, MAIN), bf16)
            own = columns[h * HEAD_DIM : (h + 1) * HEAD_DIM, :MAIN]
            blocks.append(jnp.concatenate([x for x in (above, own, below) if x.shape[0]], axis=0))
        return jnp.concatenate(blocks + [only_head(own_head_t, left)], axis=1)

    def repeated(rows):
        zeros = jnp.zeros((MAIN - SHARED, C), bf16)
        return jnp.concatenate([rows[MAIN:]] * HEADS + [zeros], axis=0)

    def only_head(mask, value):
        return jnp.where(mask, value, jnp.zeros_like(value)).astype(bf16)

    standard, _ = normalised(xw[...].reshape(WINDOWS * WIN, C))
    standard_ref[...] = standard
    tokens = (standard * gain).astype(bf16)
    tokens_ref[...] = tokens
    cots = gw[...].reshape(WINDOWS * WIN, C).astype(bf16)
    cot_ref[...] = cots
    query_ref[...] = dot(tokens, w3_ref[0]).astype(bf16)
    key_ref[...] = dot(tokens, w3_ref[1]).astype(bf16)
    value_ref[...] = dot(tokens, w3_ref[2]).astype(bf16)
    mixed_ref[...] = dot(cots, wprojt_ref[...]).astype(bf16)
    for w in range(WINDOWS):
        span = slice(w * WIN, (w + 1) * WIN)
        for k, ref in enumerate((query_ref, key_ref, value_ref)):
            qkv_t_ref[w, k * C : (k + 1) * C] = ref[span].T
        mixed_t_ref[w] = mixed_ref[span].T

    for w in range(WINDOWS):
        lz = w // STRIPS
        span = slice(w * WIN, (w + 1) * WIN)
        query_t, mixed_t = qkv_t_ref[w, 0:C], mixed_t_ref[w]
        key, value = key_ref[span], value_ref[span]
        scores_ref[w] = dot(key, per_head(query_t, dot(query_t, repeat)))
        grad_attend_ref[w] = dot(value, per_head(mixed_t, dot(mixed_t, repeat)))
        for t in range(HEADS + 1):
            columns = slice(t * MAIN, (t + 1) * MAIN)
            bias = bias_ref[lz * HEADS + t] if t < HEADS else left_ref[lz]
            scores = scores_ref[w, :, columns] * (SCALE * LOG2E) + bias
            top = jnp.max(scores, axis=0, keepdims=True)
            powers = jnp.exp2(scores - top)
            attend = powers * (1.0 / jnp.sum(powers, axis=0, keepdims=True))
            half_ref[w, :, columns] = attend.astype(bf16)
            grad_attend = grad_attend_ref[w, :, columns]
            total = jnp.sum(attend * grad_attend, axis=0, keepdims=True)
            grad_scores = attend * (grad_attend - total)
            grad_half_ref[w, :, columns] = grad_scores.astype(bf16)
            if t < HEADS:
                dense[lz * HEADS + t, :WIN] += grad_scores
            else:
                dense_left[lz, :WIN] += grad_scores

    for w in range(WINDOWS):
        span = slice(w * WIN, (w + 1) * WIN)

        def per_query(left, right_ref):
            parts = []
            for h in range(0, HEADS, 2):
                two = dot(
                    left[h * HEAD_DIM : (h + 2) * HEAD_DIM],
                    right_ref[w, :, h * MAIN : (h + 2) * MAIN],
                )
                parts += [two[:HEAD_DIM, :MAIN], two[HEAD_DIM:, MAIN:]]
            shared = dot(left, right_ref[w, :, HEADS * MAIN :])
            return jnp.concatenate(parts, axis=0), jnp.where(own_head_t, shared, 0.0)

        def per_key(left_ref, right):
            parts = [of_head(right[:MAIN], h) for h in range(HEADS)]
            parts.append(only_head(own_head, repeated(right)))
            return dot(left_ref[w], jnp.concatenate(parts, axis=0))

        cot = cot_ref[span]
        out_t, out_left = per_query(qkv_t_ref[w, 2 * C :], half_ref)
        outputs_ref[:, 2 * w * MAIN : (2 * w + 1) * MAIN] = out_t.astype(bf16)
        outputs_ref[:, (2 * w + 1) * MAIN : 2 * (w + 1) * MAIN] = out_left.astype(bf16)
        cots_ref[2 * w * MAIN : (2 * w + 1) * MAIN] = cot[:MAIN]
        cots_ref[(2 * w + 1) * MAIN : 2 * (w + 1) * MAIN] = repeated(cot)
        query_grad, query_left = per_query(qkv_t_ref[w, C : 2 * C], grad_half_ref)
        first = slice(w * WIN, w * WIN + MAIN)
        last = slice(w * WIN + MAIN, (w + 1) * WIN)
        spread[first, 0:C] = (query_grad * SCALE).astype(bf16).T
        spread[last, 0:C] = dot(gather, (query_left * SCALE).astype(bf16).T).astype(bf16)
        grad_key = per_key(grad_half_ref, query_ref[span]) * SCALE
        spread[span, WIDTH : WIDTH + C] = grad_key.astype(bf16)
        spread[span, 2 * WIDTH : 2 * WIDTH + C] = per_key(half_ref, mixed_ref[span]).astype(bf16)

    grad_projected = spread[...]
    back = dot(grad_projected, w3t_ref[...]).astype(bf16)
    rows_out[...] = back
    gsum[0:1, :] = jnp.sum(back.astype(f32) * standard_ref[...], axis=0, keepdims=True)
    wsum[...] = dot(tokens_ref[...], grad_projected, TN)
    psum[...] = dot(outputs_ref[...], cots_ref[...])

    weights = jnp.concatenate(
        [wsum[:, k * WIDTH : k * WIDTH + C] for k in range(3)] + [psum[...]], axis=1
    )
    for t in range(W_TILES):
        row, column = divmod(t, 6)
        tile = weights[16 * row : 16 * row + 16, 128 * column : 128 * column + 128]
        p, slot = w_place(t)
        if slot < W_SLOTS:
            send_shared[p, :, 128 * slot : 128 * slot + 128] = tile.astype(bf16)
        else:
            send_last[p] = tile.astype(bf16)
    shared_copy = pltpu.make_async_copy(
        send_shared, send_hbm.at[:, :, pl.ds(0, 128 * W_SLOTS)], sems.at[0]
    )
    shared_copy.start()

    total = jnp.zeros((TYPES * 16, PAIRS * 32), f32)
    lane_left = iota((PAIRS, MAIN), 1) // LEFT
    for oj in range(WLON):
        picked = []
        for lz in range(2):
            left = dense_left[lz, pl.ds(oj, PAIRS, stride=WLON), :]
            for h in range(HEADS):
                first = dense[lz * HEADS + h, pl.ds(oj, PAIRS, stride=WLON), :]
                both = jnp.concatenate([first, jnp.where(lane_left == h, left, 0.0)], axis=1)
                picked += [both, jnp.zeros((4, 2 * MAIN), f32)]
        picked = jnp.concatenate(picked, axis=0)
        high = picked.astype(bf16)
        match = match_ref[oj]
        total += dot(high, match)
    for v in range(3):
        grads[v, : TYPES * 16] = total[:, 128 * v : 128 * (v + 1)]
    wide[...] = jnp.zeros_like(wide)
    lane = iota((TYPES, 256), 1)
    for zl_j in range(PAIRS):
        for v in range(3):
            four = grads[v, pl.ds(zl_j, TYPES, stride=16), :]
            for q in range(4):
                off = table_offset(4 * v + q, zl_j)
                base, rest = off // 128 * 128, off % 128
                width = 128 if rest + OFFSETS <= 128 else 256
                piece = four
                if width == 256:
                    piece = jnp.concatenate([four, jnp.zeros_like(four)], axis=1)
                shift = (rest - 32 * q) % width
                if shift:
                    piece = pltpu.roll(piece, shift, 1)
                position = lane[:, :width]
                inside = (position >= rest) & (position < rest + OFFSETS)
                target = (slice(0, TYPES), slice(base, base + width))
                wide[target] = jnp.where(inside, piece, wide[target])

    stack[...] = jnp.zeros_like(stack)
    for n in range(B_COLUMNS):
        stack[TYPES * n : TYPES * (n + 1), :] = wide[:TYPES, 128 * n : 128 * (n + 1)]
    for n in range(B_TILES):
        send_last[B_FIRST + n] = stack[16 * n : 16 * n + 16, :].astype(bf16)
    for p in range(GAIN_PART, PARTS):
        if p == GAIN_PART:
            line = gsum[0:1, :]
            gains = jnp.concatenate([line[:, :128], jnp.zeros((7, 128), f32)], axis=0)
            more = jnp.concatenate([line[:, 128:], jnp.zeros((1, 256 - C), f32)], axis=1)
            more = jnp.concatenate([more, jnp.zeros((7, 128), f32)], axis=0)
            send_last[p] = jnp.concatenate([gains, more], axis=0).astype(bf16)
        else:
            send_last[p] = jnp.zeros((16, 128), bf16)
    second = pltpu.make_async_copy(
        send_last, send_hbm.at[:, :, pl.ds(128 * W_SLOTS, 128)], sems.at[1]
    )
    second.start()
    shared_copy.wait()
    second.wait()


def main(own, lat_in, lon_in, corner_in, gain, w3, w3t, wproj_t, bias, bias_left, match):
    vmem = pl.BlockSpec(memory_space=pltpu.VMEM)
    return pl.pallas_call(
        main_kernel,
        out_shape=(
            jax.ShapeDtypeStruct((WINDOWS * WIN, C), bf16),
            jax.ShapeDtypeStruct((PARTS, 16, SLOTS * 128), bf16),
        ),
        in_specs=[vmem] * 11,
        out_specs=(vmem, pl.BlockSpec(memory_space=pltpu.HBM)),
        scratch_shapes=[
            pltpu.VMEM((WINDOWS, WIN, C), f32),
            pltpu.VMEM((WINDOWS, WIN, C), f32),
            pltpu.VMEM((WINDOWS * WIN, C), f32),
            pltpu.VMEM((WINDOWS * WIN, C), bf16),
            pltpu.VMEM((WINDOWS * WIN, C), bf16),
            pltpu.VMEM((WINDOWS * WIN, C), bf16),
            pltpu.VMEM((WINDOWS * WIN, C), bf16),
            pltpu.VMEM((WINDOWS * WIN, C), bf16),
            pltpu.VMEM((WINDOWS * WIN, C), bf16),
            pltpu.VMEM((WINDOWS, 3 * C, WIN), bf16),
            pltpu.VMEM((WINDOWS, C, WIN), bf16),
            pltpu.VMEM((WINDOWS, WIN, (HEADS + 1) * MAIN), f32),
            pltpu.VMEM((WINDOWS, WIN, (HEADS + 1) * MAIN), f32),
            pltpu.VMEM((WINDOWS, WIN, (HEADS + 1) * MAIN), bf16),
            pltpu.VMEM((WINDOWS, WIN, (HEADS + 1) * MAIN), bf16),
            pltpu.VMEM((TYPES, TALL, MAIN), f32),
            pltpu.VMEM((2, TALL, MAIN), f32),
            pltpu.VMEM((C, 3 * WIDTH), f32),
            pltpu.VMEM((C, C), f32),
            pltpu.VMEM((8, C), f32),
            pltpu.VMEM((WINDOWS * WIN, 3 * WIDTH), bf16),
            pltpu.VMEM((C, 2 * WINDOWS * MAIN), bf16),
            pltpu.VMEM((2 * WINDOWS * MAIN, C), bf16),
            pltpu.VMEM((16, WIDE), f32),
            pltpu.VMEM((3, TALLER, 128), f32),
            pltpu.VMEM((B_TILES * 16, 128), f32),
            pltpu.VMEM((PARTS, 16, 128 * W_SLOTS), bf16),
            pltpu.VMEM((PARTS, 16, 128), bf16),
            pltpu.SemaphoreType.DMA((2,)),
        ],
        compiler_params=pltpu.CompilerParams(vmem_limit_bytes=VMEM_LIMIT),
        cost_estimate=pl.CostEstimate(
            flops=20_000_000_000, bytes_accessed=4_000_000, transcendentals=750_000
        ),
        name="window_grads",
    )(own, lat_in, lon_in, corner_in, gain, w3, w3t, wproj_t, bias, bias_left, match)


def pieces_kernel(rows_ref, own_out, lat_out, lon_out, corner_out):
    order_t = window_order(True)
    for a in range(6):
        line = jnp.concatenate(
            [rows_ref[WIN * w + 24 * a : WIN * w + 24 * a + 24, :] for w in range(WINDOWS)], axis=0
        )
        line = dot(order_t, line)
        body, tail = line[:BODY].astype(bf16), line[BODY:].astype(bf16)
        if a < 3:
            own_out[a], lon_out[a] = body, tail
        else:
            lat_out[a - 3], corner_out[a - 3] = body, tail


def pieces(rows):
    vmem = pl.BlockSpec(memory_space=pltpu.VMEM)
    return pl.pallas_call(
        pieces_kernel,
        out_shape=(
            jax.ShapeDtypeStruct((3, BODY, C), bf16),
            jax.ShapeDtypeStruct((3, BODY, C), bf16),
            jax.ShapeDtypeStruct((3, TAIL, C), bf16),
            jax.ShapeDtypeStruct((3, TAIL, C), bf16),
        ),
        in_specs=[vmem],
        out_specs=(vmem,) * 4,
        compiler_params=pltpu.CompilerParams(vmem_limit_bytes=VMEM_LIMIT),
        cost_estimate=pl.CostEstimate(
            flops=500_000_000, bytes_accessed=700_000, transcendentals=0
        ),
        name="pieces",
    )(rows)


def norm_kernel(x_ref, g_ref, gain_ref, own_ref, lat_ref, lon_ref, corner_ref, out_ref):
    gain = gain_ref[...]
    for a in range(6):
        if a < 3:
            head, body = corner_ref[a], lat_ref[a]
        else:
            head, body = lon_ref[a - 3], own_ref[a - 3]
        grad = jnp.concatenate([head.astype(f32), body.astype(f32)], axis=0)
        standard, inverse = normalised(x_ref[a].reshape(WIN, C).astype(f32))
        scaled = grad * gain
        local = inverse * (
            scaled
            - jnp.mean(scaled, axis=-1, keepdims=True)
            - standard * jnp.mean(scaled * standard, axis=-1, keepdims=True)
        )
        total = (g_ref[a].reshape(WIN, C).astype(f32) + local).astype(bf16)
        out_ref[a] = total.reshape(36, 4, C)


def norm_grads(x, g, gain, own, lat_in, lon_in, corner_in):
    vmem = pl.BlockSpec(memory_space=pltpu.VMEM)
    return pl.pallas_call(
        norm_kernel,
        out_shape=jax.ShapeDtypeStruct(x.shape, bf16),
        in_specs=[vmem] * 7,
        out_specs=vmem,
        compiler_params=pltpu.CompilerParams(vmem_limit_bytes=VMEM_LIMIT),
        cost_estimate=pl.CostEstimate(
            flops=10_000_000, bytes_accessed=1_500_000, transcendentals=1000
        ),
        name="norm_grads",
    )(x, g, gain, own, lat_in, lon_in, corner_in)


def unpack_kernel(parts_ref, gain_out, wqkv_out, wproj_out, bias_out, stack):
    last = slice(128 * W_SLOTS, 128 * SLOTS)
    gains = parts_ref[GAIN_PART, :, last].astype(f32)
    gain_out[:, :128] = gains[0:1]
    gain_out[:, 128:] = gains[8:9, : C - 128]

    def tile(t):
        p, slot = w_place(t)
        return parts_ref[p, :, 128 * slot : 128 * slot + 128].astype(f32)

    for row in range(C // 16):
        lines = slice(16 * row, 16 * row + 16)
        for column in range(4):
            wqkv_out[lines, 128 * column : 128 * column + 128] = tile(6 * row + column)
        mixed = tile(6 * row + 4)
        wqkv_out[lines, 512:] = mixed[:, :64]
        wproj_out[lines, :] = jnp.concatenate([mixed[:, 64:], tile(6 * row + 5)], axis=1)
    for n in range(B_TILES):
        stack[16 * n : 16 * n + 16, :] = parts_ref[B_FIRST + n, :, last].astype(f32)
    for n in range(B_COLUMNS):
        width = min(128, TABLE - 128 * n)
        for h in range(HEADS):
            for lz in range(2):
                t = TYPES * n + lz * HEADS + h
                bias_out[h, lz : lz + 1, 128 * n : 128 * n + width] = stack[t : t + 1, :width]


def unpack(parts):
    vmem = pl.BlockSpec(memory_space=pltpu.VMEM)
    return pl.pallas_call(
        unpack_kernel,
        out_shape=(
            jax.ShapeDtypeStruct((1, C), f32),
            jax.ShapeDtypeStruct((C, 3 * C), f32),
            jax.ShapeDtypeStruct((C, C), f32),
            jax.ShapeDtypeStruct((HEADS, 2, TABLE), f32),
        ),
        in_specs=[vmem],
        out_specs=(vmem,) * 4,
        scratch_shapes=[pltpu.VMEM((B_TILES * 16, 128), f32)],
        compiler_params=pltpu.CompilerParams(vmem_limit_bytes=VMEM_LIMIT),
        name="unpack",
    )(parts)


def fold_kernel(got_ref, out_ref):
    shared = jnp.zeros((16, 128 * W_SLOTS), f32)
    last = [jnp.zeros((16, 128), f32)] * LATS
    for p in range(PARTS):
        shared += got_ref[p, :, : 128 * W_SLOTS].astype(f32)
        last[ORDER[p] % LATS] += got_ref[p, :, 128 * W_SLOTS :].astype(f32)
    total = jnp.concatenate([shared] + last, axis=1).astype(bf16)
    for n in range(out_ref.shape[0]):
        out_ref[n] = total


def share_kernel(got_ref, out_ref):
    total = jnp.zeros(got_ref.shape[1:], f32)
    for n in range(got_ref.shape[0]):
        total += got_ref[n].astype(f32)
    shared = total[:, : 128 * W_SLOTS].astype(bf16)
    last = [total[:, 128 * (W_SLOTS + n) : 128 * (W_SLOTS + n + 1)] for n in range(LATS)]
    everywhere = last[0] + last[1] + last[2] + last[3]
    place = lax.axis_index(GROUP)
    per_lat = place == ORDER[B_FIRST]
    for p in range(B_FIRST + 1, GAIN_PART):
        per_lat |= place == ORDER[p]
    last = [jnp.where(per_lat, one, everywhere).astype(bf16) for one in last]
    for p in range(PARTS):
        out_ref[p, :, : 128 * W_SLOTS] = shared
        out_ref[p, :, 128 * W_SLOTS :] = last[ORDER[p] % LATS]


def on_chip(kernel, shape, name):
    vmem = pl.BlockSpec(memory_space=pltpu.VMEM)
    return pl.pallas_call(
        kernel,
        out_shape=jax.ShapeDtypeStruct(shape, bf16),
        in_specs=[vmem],
        out_specs=vmem,
        compiler_params=pltpu.CompilerParams(vmem_limit_bytes=VMEM_LIMIT),
        cost_estimate=pl.CostEstimate(flops=1_000_000, bytes_accessed=600_000, transcendentals=0),
        name=name,
    )


def pack_kernel(x_hbm, g_hbm, corner_out, lon_out, lat_out, corner, lon, lat, sems):
    places = (
        (pl.ds(0, 3), pl.ds(6, 30), lat, lat_out),
        (pl.ds(0, 3), pl.ds(0, 6), corner, corner_out),
        (pl.ds(3, 3), pl.ds(0, 6), lon, lon_out),
    )
    copies = []
    for n, (a, b, to, _) in enumerate(places):
        for k, array in enumerate((x_hbm, g_hbm)):
            copies.append(pltpu.make_async_copy(array.at[a, b], to.at[k], sems.at[2 * n + k]))
    for copy in copies:
        copy.start()
    for n, (_, _, held, out) in enumerate(places):
        copies[2 * n].wait()
        copies[2 * n + 1].wait()
        for a in range(3):
            out[a] = side_by_side(held, a)


def side_by_side(held, a):
    rows = held.shape[2] * 4
    return jnp.concatenate([held[k, a].reshape(rows, C) for k in range(2)], axis=1)


def pack(x, g):
    vmem = pl.BlockSpec(memory_space=pltpu.VMEM)
    return pl.pallas_call(
        pack_kernel,
        out_shape=(
            jax.ShapeDtypeStruct((3, TAIL, 2 * C), bf16),
            jax.ShapeDtypeStruct((3, TAIL, 2 * C), bf16),
            jax.ShapeDtypeStruct((3, BODY, 2 * C), bf16),
        ),
        in_specs=[pl.BlockSpec(memory_space=pltpu.HBM)] * 2,
        out_specs=(vmem,) * 3,
        scratch_shapes=[
            pltpu.VMEM((2, 3, 6, 4, C), bf16),
            pltpu.VMEM((2, 3, 6, 4, C), bf16),
            pltpu.VMEM((2, 3, 30, 4, C), bf16),
            pltpu.SemaphoreType.DMA((6,)),
        ],
        compiler_params=pltpu.CompilerParams(vmem_limit_bytes=VMEM_LIMIT),
        name="pack",
    )(in_hbm(x), in_hbm(g))


def exchange(blocks, axes, order):
    return lax.all_to_all(blocks, axes, 0, 0, tiled=True, axis_index_groups=[order])


def on_device(x, g, ln_gain, w_qkv, w_proj, bias_table):
    lon_axes, lat_axes = ("z", "y", "xh"), ("xl", "c")
    both = lon_axes + lat_axes
    lons, lats = lax.axis_size(lon_axes), lax.axis_size(lat_axes)
    lon_swap = [(i, i ^ 1) for i in range(lons)]
    lat_down = [(i, (i - 1) % lats) for i in range(lats)]
    lat_up = [(i, (i + 1) % lats) for i in range(lats)]
    corner_up = [(i * lats + a, (i ^ 1) * lats + b) for i in range(lons) for a, b in lat_up]
    corner_down = [(i * lats + a, (i ^ 1) * lats + b) for i in range(lons) for a, b in lat_down]

    x, g = x.transpose(1, 2, 0, 3), g.transpose(1, 2, 0, 3)
    to_corner, to_lon, to_lat = pack(x, g)
    corner_in = lax.ppermute(to_corner, both, corner_down)
    lon_in = lax.ppermute(to_lon, lon_axes, lon_swap)
    lat_in = lax.ppermute(to_lat, lat_axes, lat_down)
    bias, bias_left, w3, w3t, wproj_t, own, match, gain = prepare(
        bias_table[0].transpose(1, 0, 2), w_qkv, w_proj, ln_gain.reshape(1, C), x, g
    )
    rows, send = main(
        own, lat_in, lon_in, corner_in, gain, w3, w3t, wproj_t, bias, bias_left, match
    )
    own, to_lat, to_lon, to_corner = pieces(rows)
    back = (
        lax.ppermute(to_lat, lat_axes, lat_up),
        lax.ppermute(to_lon, lon_axes, lon_swap),
        lax.ppermute(to_corner, both, corner_up),
    )
    got = exchange(send, GROUP, ORDER)
    mixed = on_chip(fold_kernel, (lax.axis_size(REST), 16, 128 * (W_SLOTS + LATS)), "fold")(got)
    got = exchange(mixed, REST, list(reversed(range(mixed.shape[0]))))
    spread = on_chip(share_kernel, send.shape, "share")(got)
    spread, back = lax.optimization_barrier((spread, back))
    parts = exchange(spread, GROUP, ORDER)
    grad_gain, grad_wqkv, grad_wproj, grad_bias = unpack(parts)
    grad_x = norm_grads(x, g, gain, own, *back)
    grad_x = grad_x.transpose(2, 0, 1, 3)
    grad_bias = grad_bias.transpose(1, 0, 2)[None]
    return grad_x, grad_gain.reshape(C), grad_wqkv, grad_wproj, grad_bias


def solution(mesh):
    shape = (mesh.shape["lon"] // 8, 4, 2, 2, 2)
    split = Mesh(mesh.devices.reshape(shape), ("z", "y", "xh", "xl", "c"))
    tokens = P(None, ("xl", "c"), ("z", "y", "xh"), None)
    table = P(("xl", "c"), None, None, None)
    return jax.shard_map(
        on_device,
        mesh=split,
        in_specs=(tokens, tokens, P(), P(), P(), table),
        out_specs=(tokens, P(), P(), P(), table),
        check_vma=False,
    )
```

```python
import functools

import jax
import jax.numpy as jnp
from jax import lax
from jax.experimental import pallas as pl
from jax.experimental.pallas import tpu as pltpu
from jax.sharding import Mesh, PartitionSpec as P

C = 192
HEADS = 6
HEAD_DIM = 32
WLON = 12
WIN = 144
TABLE = 3312
PAIRS = 12
OFFSETS = 23
LOG2E = 1.4426950408889634
SCALE = HEAD_DIM**-0.5
BODY = 120
TAIL = 24
MAIN = 128
LEFT = 16
SHARED = HEADS * LEFT
STRIPS = 3
WINDOWS = 6
TYPES = 12
GROUP = ("y", "xh", "xl", "c")
REST = "z"
PARTS = 32
ORDER = [31 - (y * 8 + xh * 4 + xl * 2 + c) for c in range(2) for xh in range(2) for xl in range(2) for y in range(4)]
SLOTS = 3
W_TILES = 72
W_SLOTS = 2
B_COLUMNS = 26
B_TILES = 20
B_FIRST = 8
GAIN_PART = B_FIRST + B_TILES
WIDTH = 256
LATS = 4
WIDE = 3584
TALL = 160
TALLER = 208
f32 = jnp.float32
bf16 = jnp.bfloat16
VMEM_LIMIT = 40 * 1024 * 1024

NN = (((1,), (0,)), ((), ()))
TN = (((0,), (0,)), ((), ()))


def dot(a, b, dims=NN):
    return lax.dot_general(a, b, dims, preferred_element_type=f32)


def table_offset(zl_i, zl_j):
    li, zi = divmod(zl_i, 2)
    lj, zj = divmod(zl_j, 2)
    return (((zi * 2 + zj) * 6 + li) * 6 + lj) * OFFSETS


def iota(shape, dim):
    return lax.broadcasted_iota(jnp.int32, shape, dim)


def ones_where(condition):
    return jnp.where(condition, 1.0, 0.0).astype(bf16)


def query_index(column):
    return jnp.where(column < MAIN, column, MAIN + column % LEFT)


def offset_match(oj, transposed):
    shape = (2 * MAIN, PAIRS * 32) if transposed else (PAIRS * 32, 2 * MAIN)
    row, col = iota(shape, 1 if transposed else 0), iota(shape, 0 if transposed else 1)
    token = query_index(col)
    zl = token // WLON
    target = zl * 32 + (oj + 11) - (token - zl * WLON)
    return ones_where((row == target) & (col < MAIN + SHARED))


def window_order(transposed):
    dest, source = iota((WIN, WIN), 1 if transposed else 0), iota((WIN, WIN), 0 if transposed else 1)
    window = dest // 24
    lz = window // STRIPS
    strip = window - lz * STRIPS
    inside = dest - window * 24
    zi = inside // WLON
    longitude = strip * WLON + inside - zi * WLON
    level = (2 * lz + zi + 1) % 4
    return ones_where(source == 4 * longitude + level)


def prepare_kernel(
    table_hbm, wqkv_hbm, wproj_hbm, gain_hbm, x_hbm, g_hbm,
    main_ref, left_ref, w3_ref, w3t_ref, wprojt_ref, own_ref, match_ref, gain_out,
    wide, pairs, plain, plain_left, table_ref, wqkv_ref, wproj_ref, mine, sems,
):
    kept = pl.ds(3, 3), pl.ds(6, 30)
    moves = (
        (table_hbm, table_ref),
        (wqkv_hbm, wqkv_ref),
        (wproj_hbm, wproj_ref),
        (gain_hbm, gain_out),
        (x_hbm.at[kept], mine.at[0]),
        (g_hbm.at[kept], mine.at[1]),
    )
    copies = [pltpu.make_async_copy(a, b, sems.at[n]) for n, (a, b) in enumerate(moves)]
    for copy in copies:
        copy.start()
    for oj in range(WLON):
        match_ref[oj] = offset_match(oj, True)
    for copy in copies:
        copy.wait()
    for k in range(3):
        part = wqkv_ref[:, k * C : (k + 1) * C]
        w3_ref[k] = part
        w3t_ref[k * WIDTH : k * WIDTH + C] = part.T
        w3t_ref[k * WIDTH + C : (k + 1) * WIDTH] = jnp.zeros((WIDTH - C, C), bf16)
    wprojt_ref[...] = wproj_ref[...].T
    for a in range(3):
        own_ref[a] = side_by_side(mine, a)
    wide[...] = jnp.zeros_like(wide)
    for h in range(HEADS):
        for lz in range(2):
            wide[lz * HEADS + h : lz * HEADS + h + 1, :TABLE] = table_ref[h, lz : lz + 1] * LOG2E
    pairs[...] = jnp.zeros_like(pairs)
    lane = iota((16, 128), 1)
    for zl_j in range(PAIRS):
        for v in range(3):
            total = jnp.zeros((16, 128), f32)
            for q in range(4):
                off = table_offset(4 * v + q, zl_j)
                base, rest = off // 128 * 128, off % 128
                width = 128 if rest + OFFSETS <= 128 else 256
                piece = wide[:, base : base + width]
                shift = (32 * q - rest) % width
                if shift:
                    piece = pltpu.roll(piece, shift, 1)
                inside = (lane >= 32 * q) & (lane < 32 * q + OFFSETS)
                total = jnp.where(inside, piece[:, :128], total)
            pairs[v, pl.ds(zl_j, TYPES, stride=16), :] = total[:TYPES]
    full = jnp.concatenate([pairs[v, : TYPES * 16] for v in range(3)], axis=1)
    high = full.astype(bf16)
    rest = full - high.astype(f32)
    middle = rest.astype(bf16)
    low = (rest - middle.astype(f32)).astype(bf16)
    lane_head = iota((PAIRS, MAIN), 1) // LEFT
    for oj in range(WLON):
        match = offset_match(oj, False)
        dense = dot(high, match) + (dot(middle, match) + dot(low, match))
        for lz in range(2):
            left = jnp.zeros((PAIRS, MAIN), f32)
            for h in range(HEADS):
                t = lz * HEADS + h
                block = dense[t * 16 : t * 16 + PAIRS]
                plain[t, pl.ds(oj, PAIRS, stride=WLON), :] = block[:, :MAIN]
                left = jnp.where(lane_head == h, block[:, MAIN:], left)
            plain_left[lz, pl.ds(oj, PAIRS, stride=WLON), :] = left
    lat = lax.axis_index("xl") * 2 + lax.axis_index("c")
    last_band = (lat == LATS - 1).astype(jnp.int32)

    def region(token, last_level):
        upper = (token // WLON) % 2 * (2 * last_level)
        return upper + jnp.where(token >= 72, last_band, 0)

    j = iota((WIN, MAIN), 0)
    column = iota((WIN, MAIN), 1)
    for lz in range(2):
        allowed = region(column, lz) == region(j, lz)
        for h in range(HEADS):
            t = lz * HEADS + h
            main_ref[t] = jnp.where(allowed, plain[t, :WIN], -1e30)
        allowed = region(query_index(column + MAIN), lz) == region(j, lz)
        left_ref[lz] = jnp.where(allowed, plain_left[lz, :WIN], -1e30)


def in_hbm(array):
    return pltpu.with_memory_space_constraint(array, pltpu.HBM)


def prepare(table, wqkv, wproj, gain, x, g):
    vmem = pl.BlockSpec(memory_space=pltpu.VMEM)
    return pl.pallas_call(
        prepare_kernel,
        out_shape=(
            jax.ShapeDtypeStruct((TYPES, WIN, MAIN), f32),
            jax.ShapeDtypeStruct((2, WIN, MAIN), f32),
            jax.ShapeDtypeStruct((3, C, C), bf16),
            jax.ShapeDtypeStruct((3 * WIDTH, C), bf16),
            jax.ShapeDtypeStruct((C, C), bf16),
            jax.ShapeDtypeStruct((3, BODY, 2 * C), bf16),
            jax.ShapeDtypeStruct((WLON, 2 * MAIN, PAIRS * 32), bf16),
            jax.ShapeDtypeStruct((1, C), f32),
        ),
        in_specs=[pl.BlockSpec(memory_space=pltpu.HBM)] * 6,
        out_specs=(vmem,) * 8,
        scratch_shapes=[
            pltpu.VMEM((16, WIDE), f32),
            pltpu.VMEM((3, TALLER, 128), f32),
            pltpu.VMEM((TYPES, TALL, MAIN), f32),
            pltpu.VMEM((2, TALL, MAIN), f32),
            pltpu.VMEM((HEADS, 2, TABLE), f32),
            pltpu.VMEM((C, 3 * C), bf16),
            pltpu.VMEM((C, C), bf16),
            pltpu.VMEM((2, 3, 30, 4, C), bf16),
            pltpu.SemaphoreType.DMA((6,)),
        ],
        compiler_params=pltpu.CompilerParams(vmem_limit_bytes=VMEM_LIMIT),
        cost_estimate=pl.CostEstimate(
            flops=400_000_000, bytes_accessed=400_000, transcendentals=0
        ),
        name="prepare",
    )(*(in_hbm(a) for a in (table, wqkv, wproj, gain, x, g)))


def normalised(values):
    mean = jnp.mean(values, axis=-1, keepdims=True)
    centred = values - mean
    inverse = lax.rsqrt(jnp.mean(centred * centred, axis=-1, keepdims=True) + 1e-05)
    return centred * inverse, inverse


def w_place(t):
    if t < W_SLOTS * PARTS:
        return t // W_SLOTS, t % W_SLOTS
    return t - W_SLOTS * PARTS, W_SLOTS


def main_kernel(
    own_ref, lat_ref, lon_ref, corner_ref, gain_ref, w3_ref, w3t_ref, wprojt_ref,
    bias_ref, left_ref, match_ref, rows_out, send_hbm,
    xw, gw, standard_ref, cot_ref, query_ref, key_ref, value_ref, mixed_ref, tokens_ref,
    qkv_t_ref, mixed_t_ref, scores_ref, grad_attend_ref, half_ref, grad_half_ref, dense, dense_left,
    wsum, psum, gsum, spread, outputs_ref, cots_ref, wide, grads, stack,
    send_shared, send_last, sems,
):
    order = window_order(False)
    for a in range(6):
        body, tail = (own_ref[a], lon_ref[a]) if a < 3 else (lat_ref[a - 3], corner_ref[a - 3])
        line = dot(order[:, :BODY], body) + dot(order[:, BODY:], tail)
        for w in range(WINDOWS):
            xw[w, 24 * a : 24 * a + 24, :] = line[24 * w : 24 * w + 24, :C]
            gw[w, 24 * a : 24 * a + 24, :] = line[24 * w : 24 * w + 24, C:]
    dense[...] = jnp.zeros_like(dense)
    dense_left[...] = jnp.zeros_like(dense_left)
    gsum[...] = jnp.zeros_like(gsum)
    spread[...] = jnp.zeros_like(spread)
    gain = gain_ref[...]
    lane_head = iota((WIN, C), 1) // HEAD_DIM
    shape = (WIN, MAIN)
    repeat = ones_where((iota(shape, 0) == MAIN + iota(shape, 1) % LEFT) & (iota(shape, 1) < SHARED))
    shape = (LEFT, MAIN)
    gather = ones_where((iota(shape, 0) == iota(shape, 1) % LEFT) & (iota(shape, 1) < SHARED))
    own_head_t = iota((C, MAIN), 0) // HEAD_DIM == iota((C, MAIN), 1) // LEFT
    own_head = iota((MAIN, C), 1) // HEAD_DIM == iota((MAIN, C), 0) // LEFT

    def of_head(value, h):
        return jnp.where(lane_head[: value.shape[0]] == h, value, jnp.zeros_like(value))

    def per_head(columns, left):
        blocks = []
        for h in range(HEADS):
            above = jnp.zeros((h * HEAD_DIM, MAIN), bf16)
            below = jnp.zeros((C - (h + 1) * HEAD_DIM, MAIN), bf16)
            own = columns[h * HEAD_DIM : (h + 1) * HEAD_DIM, :MAIN]
            blocks.append(jnp.concatenate([x for x in (above, own, below) if x.shape[0]], axis=0))
        return jnp.concatenate(blocks + [only_head(own_head_t, left)], axis=1)

    def repeated(rows):
        zeros = jnp.zeros((MAIN - SHARED, C), bf16)
        return jnp.concatenate([rows[MAIN:]] * HEADS + [zeros], axis=0)

    def only_head(mask, value):
        return jnp.where(mask, value, jnp.zeros_like(value)).astype(bf16)

    standard, _ = normalised(xw[...].reshape(WINDOWS * WIN, C))
    standard_ref[...] = standard
    tokens = (standard * gain).astype(bf16)
    tokens_ref[...] = tokens
    cots = gw[...].reshape(WINDOWS * WIN, C).astype(bf16)
    cot_ref[...] = cots
    query_ref[...] = dot(tokens, w3_ref[0]).astype(bf16)
    key_ref[...] = dot(tokens, w3_ref[1]).astype(bf16)
    value_ref[...] = dot(tokens, w3_ref[2]).astype(bf16)
    mixed_ref[...] = dot(cots, wprojt_ref[...]).astype(bf16)
    for w in range(WINDOWS):
        span = slice(w * WIN, (w + 1) * WIN)
        for k, ref in enumerate((query_ref, key_ref, value_ref)):
            qkv_t_ref[w, k * C : (k + 1) * C] = ref[span].T
        mixed_t_ref[w] = mixed_ref[span].T

    for w in range(WINDOWS):
        lz = w // STRIPS
        span = slice(w * WIN, (w + 1) * WIN)
        query_t, mixed_t = qkv_t_ref[w, 0:C], mixed_t_ref[w]
        key, value = key_ref[span], value_ref[span]
        scores_ref[w] = dot(key, per_head(query_t, dot(query_t, repeat)))
        grad_attend_ref[w] = dot(value, per_head(mixed_t, dot(mixed_t, repeat)))
        for t in range(HEADS + 1):
            columns = slice(t * MAIN, (t + 1) * MAIN)
            bias = bias_ref[lz * HEADS + t] if t < HEADS else left_ref[lz]
            scores = scores_ref[w, :, columns] * (SCALE * LOG2E) + bias
            top = jnp.max(scores, axis=0, keepdims=True)
            powers = jnp.exp2(scores - top)
            attend = powers * (1.0 / jnp.sum(powers, axis=0, keepdims=True))
            half_ref[w, :, columns] = attend.astype(bf16)
            grad_attend = grad_attend_ref[w, :, columns]
            total = jnp.sum(attend * grad_attend, axis=0, keepdims=True)
            grad_scores = attend * (grad_attend - total)
            grad_half_ref[w, :, columns] = grad_scores.astype(bf16)
            if t < HEADS:
                dense[lz * HEADS + t, :WIN] += grad_scores
            else:
                dense_left[lz, :WIN] += grad_scores

    for w in range(WINDOWS):
        span = slice(w * WIN, (w + 1) * WIN)

        def per_query(left, right_ref):
            parts = []
            for h in range(0, HEADS, 2):
                two = dot(
                    left[h * HEAD_DIM : (h + 2) * HEAD_DIM],
                    right_ref[w, :, h * MAIN : (h + 2) * MAIN],
                )
                parts += [two[:HEAD_DIM, :MAIN], two[HEAD_DIM:, MAIN:]]
            shared = dot(left, right_ref[w, :, HEADS * MAIN :])
            return jnp.concatenate(parts, axis=0), jnp.where(own_head_t, shared, 0.0)

        def per_key(left_ref, right):
            parts = [of_head(right[:MAIN], h) for h in range(HEADS)]
            parts.append(only_head(own_head, repeated(right)))
            return dot(left_ref[w], jnp.concatenate(parts, axis=0))

        cot = cot_ref[span]
        out_t, out_left = per_query(qkv_t_ref[w, 2 * C :], half_ref)
        outputs_ref[:, 2 * w * MAIN : (2 * w + 1) * MAIN] = out_t.astype(bf16)
        outputs_ref[:, (2 * w + 1) * MAIN : 2 * (w + 1) * MAIN] = out_left.astype(bf16)
        cots_ref[2 * w * MAIN : (2 * w + 1) * MAIN] = cot[:MAIN]
        cots_ref[(2 * w + 1) * MAIN : 2 * (w + 1) * MAIN] = repeated(cot)
        query_grad, query_left = per_query(qkv_t_ref[w, C : 2 * C], grad_half_ref)
        first = slice(w * WIN, w * WIN + MAIN)
        last = slice(w * WIN + MAIN, (w + 1) * WIN)
        spread[first, 0:C] = (query_grad * SCALE).astype(bf16).T
        spread[last, 0:C] = dot(gather, (query_left * SCALE).astype(bf16).T).astype(bf16)
        grad_key = per_key(grad_half_ref, query_ref[span]) * SCALE
        spread[span, WIDTH : WIDTH + C] = grad_key.astype(bf16)
        spread[span, 2 * WIDTH : 2 * WIDTH + C] = per_key(half_ref, mixed_ref[span]).astype(bf16)

    grad_projected = spread[...]
    back = dot(grad_projected, w3t_ref[...]).astype(bf16)
    rows_out[...] = back
    gsum[0:1, :] = jnp.sum(back.astype(f32) * standard_ref[...], axis=0, keepdims=True)
    wsum[...] = dot(tokens_ref[...], grad_projected, TN)
    psum[...] = dot(outputs_ref[...], cots_ref[...])

    weights = jnp.concatenate(
        [wsum[:, k * WIDTH : k * WIDTH + C] for k in range(3)] + [psum[...]], axis=1
    )
    for t in range(W_TILES):
        row, column = divmod(t, 6)
        tile = weights[16 * row : 16 * row + 16, 128 * column : 128 * column + 128]
        p, slot = w_place(t)
        if slot < W_SLOTS:
            send_shared[p, :, 128 * slot : 128 * slot + 128] = tile.astype(bf16)
        else:
            send_last[p] = tile.astype(bf16)
    shared_copy = pltpu.make_async_copy(
        send_shared, send_hbm.at[:, :, pl.ds(0, 128 * W_SLOTS)], sems.at[0]
    )
    shared_copy.start()

    total = jnp.zeros((TYPES * 16, PAIRS * 32), f32)
    lane_left = iota((PAIRS, MAIN), 1) // LEFT
    for oj in range(WLON):
        picked = []
        for lz in range(2):
            left = dense_left[lz, pl.ds(oj, PAIRS, stride=WLON), :]
            for h in range(HEADS):
                first = dense[lz * HEADS + h, pl.ds(oj, PAIRS, stride=WLON), :]
                both = jnp.concatenate([first, jnp.where(lane_left == h, left, 0.0)], axis=1)
                picked += [both, jnp.zeros((4, 2 * MAIN), f32)]
        picked = jnp.concatenate(picked, axis=0)
        high = picked.astype(bf16)
        match = match_ref[oj]
        total += dot(high, match)
    for v in range(3):
        grads[v, : TYPES * 16] = total[:, 128 * v : 128 * (v + 1)]
    wide[...] = jnp.zeros_like(wide)
    lane = iota((TYPES, 256), 1)
    for zl_j in range(PAIRS):
        for v in range(3):
            four = grads[v, pl.ds(zl_j, TYPES, stride=16), :]
            for q in range(4):
                off = table_offset(4 * v + q, zl_j)
                base, rest = off // 128 * 128, off % 128
                width = 128 if rest + OFFSETS <= 128 else 256
                piece = four
                if width == 256:
                    piece = jnp.concatenate([four, jnp.zeros_like(four)], axis=1)
                shift = (rest - 32 * q) % width
                if shift:
                    piece = pltpu.roll(piece, shift, 1)
                position = lane[:, :width]
                inside = (position >= rest) & (position < rest + OFFSETS)
                target = (slice(0, TYPES), slice(base, base + width))
                wide[target] = jnp.where(inside, piece, wide[target])

    stack[...] = jnp.zeros_like(stack)
    for n in range(B_COLUMNS):
        stack[TYPES * n : TYPES * (n + 1), :] = wide[:TYPES, 128 * n : 128 * (n + 1)]
    for n in range(B_TILES):
        send_last[B_FIRST + n] = stack[16 * n : 16 * n + 16, :].astype(bf16)
    for p in range(GAIN_PART, PARTS):
        if p == GAIN_PART:
            line = gsum[0:1, :]
            gains = jnp.concatenate([line[:, :128], jnp.zeros((7, 128), f32)], axis=0)
            more = jnp.concatenate([line[:, 128:], jnp.zeros((1, 256 - C), f32)], axis=1)
            more = jnp.concatenate([more, jnp.zeros((7, 128), f32)], axis=0)
            send_last[p] = jnp.concatenate([gains, more], axis=0).astype(bf16)
        else:
            send_last[p] = jnp.zeros((16, 128), bf16)
    second = pltpu.make_async_copy(
        send_last, send_hbm.at[:, :, pl.ds(128 * W_SLOTS, 128)], sems.at[1]
    )
    second.start()
    shared_copy.wait()
    second.wait()


def main(own, lat_in, lon_in, corner_in, gain, w3, w3t, wproj_t, bias, bias_left, match):
    vmem = pl.BlockSpec(memory_space=pltpu.VMEM)
    return pl.pallas_call(
        main_kernel,
        out_shape=(
            jax.ShapeDtypeStruct((WINDOWS * WIN, C), bf16),
            jax.ShapeDtypeStruct((PARTS, 16, SLOTS * 128), bf16),
        ),
        in_specs=[vmem] * 11,
        out_specs=(vmem, pl.BlockSpec(memory_space=pltpu.HBM)),
        scratch_shapes=[
            pltpu.VMEM((WINDOWS, WIN, C), f32),
            pltpu.VMEM((WINDOWS, WIN, C), f32),
            pltpu.VMEM((WINDOWS * WIN, C), f32),
            pltpu.VMEM((WINDOWS * WIN, C), bf16),
            pltpu.VMEM((WINDOWS * WIN, C), bf16),
            pltpu.VMEM((WINDOWS * WIN, C), bf16),
            pltpu.VMEM((WINDOWS * WIN, C), bf16),
            pltpu.VMEM((WINDOWS * WIN, C), bf16),
            pltpu.VMEM((WINDOWS * WIN, C), bf16),
            pltpu.VMEM((WINDOWS, 3 * C, WIN), bf16),
            pltpu.VMEM((WINDOWS, C, WIN), bf16),
            pltpu.VMEM((WINDOWS, WIN, (HEADS + 1) * MAIN), f32),
            pltpu.VMEM((WINDOWS, WIN, (HEADS + 1) * MAIN), f32),
            pltpu.VMEM((WINDOWS, WIN, (HEADS + 1) * MAIN), bf16),
            pltpu.VMEM((WINDOWS, WIN, (HEADS + 1) * MAIN), bf16),
            pltpu.VMEM((TYPES, TALL, MAIN), f32),
            pltpu.VMEM((2, TALL, MAIN), f32),
            pltpu.VMEM((C, 3 * WIDTH), f32),
            pltpu.VMEM((C, C), f32),
            pltpu.VMEM((8, C), f32),
            pltpu.VMEM((WINDOWS * WIN, 3 * WIDTH), bf16),
            pltpu.VMEM((C, 2 * WINDOWS * MAIN), bf16),
            pltpu.VMEM((2 * WINDOWS * MAIN, C), bf16),
            pltpu.VMEM((16, WIDE), f32),
            pltpu.VMEM((3, TALLER, 128), f32),
            pltpu.VMEM((B_TILES * 16, 128), f32),
            pltpu.VMEM((PARTS, 16, 128 * W_SLOTS), bf16),
            pltpu.VMEM((PARTS, 16, 128), bf16),
            pltpu.SemaphoreType.DMA((2,)),
        ],
        compiler_params=pltpu.CompilerParams(vmem_limit_bytes=VMEM_LIMIT),
        cost_estimate=pl.CostEstimate(
            flops=20_000_000_000, bytes_accessed=4_000_000, transcendentals=750_000
        ),
        name="window_grads",
    )(own, lat_in, lon_in, corner_in, gain, w3, w3t, wproj_t, bias, bias_left, match)


def pieces_kernel(rows_ref, own_out, lat_out, lon_out, corner_out):
    order_t = window_order(True)
    for a in range(6):
        line = jnp.concatenate(
            [rows_ref[WIN * w + 24 * a : WIN * w + 24 * a + 24, :] for w in range(WINDOWS)], axis=0
        )
        line = dot(order_t, line)
        body, tail = line[:BODY].astype(bf16), line[BODY:].astype(bf16)
        if a < 3:
            own_out[a], lon_out[a] = body, tail
        else:
            lat_out[a - 3], corner_out[a - 3] = body, tail


def pieces(rows):
    vmem = pl.BlockSpec(memory_space=pltpu.VMEM)
    return pl.pallas_call(
        pieces_kernel,
        out_shape=(
            jax.ShapeDtypeStruct((3, BODY, C), bf16),
            jax.ShapeDtypeStruct((3, BODY, C), bf16),
            jax.ShapeDtypeStruct((3, TAIL, C), bf16),
            jax.ShapeDtypeStruct((3, TAIL, C), bf16),
        ),
        in_specs=[vmem],
        out_specs=(vmem,) * 4,
        compiler_params=pltpu.CompilerParams(vmem_limit_bytes=VMEM_LIMIT),
        cost_estimate=pl.CostEstimate(
            flops=500_000_000, bytes_accessed=700_000, transcendentals=0
        ),
        name="pieces",
    )(rows)


def norm_kernel(x_ref, g_ref, gain_ref, own_ref, lat_ref, lon_ref, corner_ref, out_ref):
    gain = gain_ref[...]
    for a in range(6):
        if a < 3:
            head, body = corner_ref[a], lat_ref[a]
        else:
            head, body = lon_ref[a - 3], own_ref[a - 3]
        grad = jnp.concatenate([head.astype(f32), body.astype(f32)], axis=0)
        standard, inverse = normalised(x_ref[a].reshape(WIN, C).astype(f32))
        scaled = grad * gain
        local = inverse * (
            scaled
            - jnp.mean(scaled, axis=-1, keepdims=True)
            - standard * jnp.mean(scaled * standard, axis=-1, keepdims=True)
        )
        total = (g_ref[a].reshape(WIN, C).astype(f32) + local).astype(bf16)
        out_ref[a] = total.reshape(36, 4, C)


def norm_grads(x, g, gain, own, lat_in, lon_in, corner_in):
    vmem = pl.BlockSpec(memory_space=pltpu.VMEM)
    return pl.pallas_call(
        norm_kernel,
        out_shape=jax.ShapeDtypeStruct(x.shape, bf16),
        in_specs=[vmem] * 7,
        out_specs=vmem,
        compiler_params=pltpu.CompilerParams(vmem_limit_bytes=VMEM_LIMIT),
        cost_estimate=pl.CostEstimate(
            flops=10_000_000, bytes_accessed=1_500_000, transcendentals=1000
        ),
        name="norm_grads",
    )(x, g, gain, own, lat_in, lon_in, corner_in)


def unpack_kernel(parts_ref, gain_out, wqkv_out, wproj_out, bias_out, stack):
    last = slice(128 * W_SLOTS, 128 * SLOTS)
    gains = parts_ref[GAIN_PART, :, last].astype(f32)
    gain_out[:, :128] = gains[0:1]
    gain_out[:, 128:] = gains[8:9, : C - 128]

    def tile(t):
        p, slot = w_place(t)
        return parts_ref[p, :, 128 * slot : 128 * slot + 128].astype(f32)

    for row in range(C // 16):
        lines = slice(16 * row, 16 * row + 16)
        for column in range(4):
            wqkv_out[lines, 128 * column : 128 * column + 128] = tile(6 * row + column)
        mixed = tile(6 * row + 4)
        wqkv_out[lines, 512:] = mixed[:, :64]
        wproj_out[lines, :] = jnp.concatenate([mixed[:, 64:], tile(6 * row + 5)], axis=1)
    for n in range(B_TILES):
        stack[16 * n : 16 * n + 16, :] = parts_ref[B_FIRST + n, :, last].astype(f32)
    for n in range(B_COLUMNS):
        width = min(128, TABLE - 128 * n)
        for h in range(HEADS):
            for lz in range(2):
                t = TYPES * n + lz * HEADS + h
                bias_out[h, lz : lz + 1, 128 * n : 128 * n + width] = stack[t : t + 1, :width]


def unpack(parts):
    vmem = pl.BlockSpec(memory_space=pltpu.VMEM)
    return pl.pallas_call(
        unpack_kernel,
        out_shape=(
            jax.ShapeDtypeStruct((1, C), f32),
            jax.ShapeDtypeStruct((C, 3 * C), f32),
            jax.ShapeDtypeStruct((C, C), f32),
            jax.ShapeDtypeStruct((HEADS, 2, TABLE), f32),
        ),
        in_specs=[vmem],
        out_specs=(vmem,) * 4,
        scratch_shapes=[pltpu.VMEM((B_TILES * 16, 128), f32)],
        compiler_params=pltpu.CompilerParams(vmem_limit_bytes=VMEM_LIMIT),
        name="unpack",
    )(parts)


def fold_kernel(got_ref, out_ref):
    shared = jnp.zeros((16, 128 * W_SLOTS), f32)
    last = [jnp.zeros((16, 128), f32)] * LATS
    for p in range(PARTS):
        shared += got_ref[p, :, : 128 * W_SLOTS].astype(f32)
        last[ORDER[p] % LATS] += got_ref[p, :, 128 * W_SLOTS :].astype(f32)
    total = jnp.concatenate([shared] + last, axis=1).astype(bf16)
    for n in range(out_ref.shape[0]):
        out_ref[n] = total


def share_kernel(got_ref, out_ref):
    total = jnp.zeros(got_ref.shape[1:], f32)
    for n in range(got_ref.shape[0]):
        total += got_ref[n].astype(f32)
    shared = total[:, : 128 * W_SLOTS].astype(bf16)
    last = [total[:, 128 * (W_SLOTS + n) : 128 * (W_SLOTS + n + 1)] for n in range(LATS)]
    everywhere = last[0] + last[1] + last[2] + last[3]
    place = lax.axis_index(GROUP)
    per_lat = place == ORDER[B_FIRST]
    for p in range(B_FIRST + 1, GAIN_PART):
        per_lat |= place == ORDER[p]
    last = [jnp.where(per_lat, one, everywhere).astype(bf16) for one in last]
    for p in range(PARTS):
        out_ref[p, :, : 128 * W_SLOTS] = shared
        out_ref[p, :, 128 * W_SLOTS :] = last[ORDER[p] % LATS]


def on_chip(kernel, shape, name):
    vmem = pl.BlockSpec(memory_space=pltpu.VMEM)
    return pl.pallas_call(
        kernel,
        out_shape=jax.ShapeDtypeStruct(shape, bf16),
        in_specs=[vmem],
        out_specs=vmem,
        compiler_params=pltpu.CompilerParams(vmem_limit_bytes=VMEM_LIMIT),
        cost_estimate=pl.CostEstimate(flops=1_000_000, bytes_accessed=600_000, transcendentals=0),
        name=name,
    )


def pack_kernel(x_hbm, g_hbm, corner_out, lon_out, lat_out, corner, lon, lat, sems):
    places = (
        (pl.ds(0, 3), pl.ds(6, 30), lat, lat_out),
        (pl.ds(0, 3), pl.ds(0, 6), corner, corner_out),
        (pl.ds(3, 3), pl.ds(0, 6), lon, lon_out),
    )
    copies = []
    for n, (a, b, to, _) in enumerate(places):
        for k, array in enumerate((x_hbm, g_hbm)):
            copies.append(pltpu.make_async_copy(array.at[a, b], to.at[k], sems.at[2 * n + k]))
    for copy in copies:
        copy.start()
    for n, (_, _, held, out) in enumerate(places):
        copies[2 * n].wait()
        copies[2 * n + 1].wait()
        for a in range(3):
            out[a] = side_by_side(held, a)


def side_by_side(held, a):
    rows = held.shape[2] * 4
    return jnp.concatenate([held[k, a].reshape(rows, C) for k in range(2)], axis=1)


def pack(x, g):
    vmem = pl.BlockSpec(memory_space=pltpu.VMEM)
    return pl.pallas_call(
        pack_kernel,
        out_shape=(
            jax.ShapeDtypeStruct((3, TAIL, 2 * C), bf16),
            jax.ShapeDtypeStruct((3, TAIL, 2 * C), bf16),
            jax.ShapeDtypeStruct((3, BODY, 2 * C), bf16),
        ),
        in_specs=[pl.BlockSpec(memory_space=pltpu.HBM)] * 2,
        out_specs=(vmem,) * 3,
        scratch_shapes=[
            pltpu.VMEM((2, 3, 6, 4, C), bf16),
            pltpu.VMEM((2, 3, 6, 4, C), bf16),
            pltpu.VMEM((2, 3, 30, 4, C), bf16),
            pltpu.SemaphoreType.DMA((6,)),
        ],
        compiler_params=pltpu.CompilerParams(vmem_limit_bytes=VMEM_LIMIT),
        name="pack",
    )(in_hbm(x), in_hbm(g))


def exchange(blocks, axes, order):
    return lax.all_to_all(blocks, axes, 0, 0, tiled=True, axis_index_groups=[order])


def on_device(x, g, ln_gain, w_qkv, w_proj, bias_table):
    lon_axes, lat_axes = ("z", "y", "xh"), ("xl", "c")
    both = lon_axes + lat_axes
    lons, lats = lax.axis_size(lon_axes), lax.axis_size(lat_axes)
    lon_swap = [(i, i ^ 1) for i in range(lons)]
    lat_down = [(i, (i - 1) % lats) for i in range(lats)]
    lat_up = [(i, (i + 1) % lats) for i in range(lats)]
    corner_up = [(i * lats + a, (i ^ 1) * lats + b) for i in range(lons) for a, b in lat_up]
    corner_down = [(i * lats + a, (i ^ 1) * lats + b) for i in range(lons) for a, b in lat_down]

    x, g = x.transpose(1, 2, 0, 3), g.transpose(1, 2, 0, 3)
    to_corner, to_lon, to_lat = pack(x, g)
    corner_in = lax.ppermute(to_corner, both, corner_down)
    lon_in = lax.ppermute(to_lon, lon_axes, lon_swap)
    lat_in = lax.ppermute(to_lat, lat_axes, lat_down)
    bias, bias_left, w3, w3t, wproj_t, own, match, gain = prepare(
        bias_table[0].transpose(1, 0, 2), w_qkv, w_proj, ln_gain.reshape(1, C), x, g
    )
    rows, send = main(
        own, lat_in, lon_in, corner_in, gain, w3, w3t, wproj_t, bias, bias_left, match
    )
    own, to_lat, to_lon, to_corner = pieces(rows)
    back = (
        lax.ppermute(to_lat, lat_axes, lat_up),
        lax.ppermute(to_lon, lon_axes, lon_swap),
        lax.ppermute(to_corner, both, corner_up),
    )
    got = exchange(send, GROUP, ORDER)
    mixed = on_chip(fold_kernel, (lax.axis_size(REST), 16, 128 * (W_SLOTS + LATS)), "fold")(got)
    got = exchange(mixed, REST, list(reversed(range(mixed.shape[0]))))
    spread = on_chip(share_kernel, send.shape, "share")(got)
    spread, back = lax.optimization_barrier((spread, back))
    parts = exchange(spread, GROUP, ORDER)
    grad_gain, grad_wqkv, grad_wproj, grad_bias = unpack(parts)
    grad_x = norm_grads(x, g, gain, own, *back)
    grad_x = grad_x.transpose(2, 0, 1, 3)
    grad_bias = grad_bias.transpose(1, 0, 2)[None]
    return grad_x, grad_gain.reshape(C), grad_wqkv, grad_wproj, grad_bias


def solution(mesh):
    shape = (mesh.shape["lon"] // 8, 4, 2, 2, 2)
    split = Mesh(mesh.devices.reshape(shape), ("z", "y", "xh", "xl", "c"))
    tokens = P(None, ("xl", "c"), ("z", "y", "xh"), None)
    table = P(("xl", "c"), None, None, None)
    return jax.shard_map(
        on_device,
        mesh=split,
        in_specs=(tokens, tokens, P(), P(), P(), table),
        out_specs=(tokens, P(), P(), P(), table),
        check_vma=False,
    )
```
